32 devices in a mesh: gx: 8 (over y, x, core), gy: 4 (over z).
Axes of the slice: x: 2, y: 2, z: 4, core: 2. Of those that a mesh axis runs over, the one named last changes fastest.
Arguments:
- right_side: float32 [4, 3, 8, 64, 512], P(None, None, None, 'gx', 'gy'), may hold values from -6 to 6
- material: int32 [8, 64, 512], P(None, 'gx', 'gy'), may hold values 0 or 1
Outputs:
- solution: float32 [4, 3, 8, 64, 512], P(None, None, None, 'gx', 'gy')
The draws below stay inside these ranges and needn't reach their ends.
All inputs are finite; a program needn't handle non-finite values. No bound on the sum of `material` on one device may be relied on, other than what follows from the above.
Results may differ from the reference program's by a relative error of at most 0.00002.
Values sent between devices are 32-bit elements; how exact they have to be, the bound alone decides.
No kernel may reach another device: no remote copies, remote signals or barrier semaphores. Data moves between devices by JAX's collectives and lax.ppermute only.
A program may use at most 64 MiB of HBM per device.

```python
import jax
import jax.numpy as jnp

NZ = 8
VEC = 4
LEVELS = 4
COARSE = 6
NX = 64
NY = 512


def with_ends(entries, key, low, top_value):
    place = [jax.random.randint(jax.random.fold_in(key, axis), (), 0, length) for axis, length in enumerate(entries.shape)]
    widest = entries.shape.index(max(entries.shape))
    neighbour = place[:widest] + [(place[widest] + 1) % entries.shape[widest]] + place[widest + 1:]
    return entries.at[tuple(place)].set(low).at[tuple(neighbour)].set(top_value)


def steps_of(rng, dims, cuts, low, top_value):
    def one(position, blocks):
        draws = jax.random.uniform(jax.random.fold_in(jax.random.fold_in(rng, 6), position), (blocks,), jnp.float32, low / len(cuts), top_value / len(cuts))
        return jnp.repeat(jnp.exp(draws), dims[position] // blocks).reshape((-1,) + (1,) * (len(dims) - position - 1))

    gain = one(*cuts[0])
    for cut in cuts[1:]:
        gain = gain * one(*cut)
    return gain


def centred(own_key, dims, scale, reach, cuts=(), dtype=jnp.bfloat16):
    values = jax.random.normal(own_key, dims, jnp.float32) * scale
    if len(cuts) > 0:
        values = steps_of(own_key, dims, cuts, -0.22, 0.18) * values
    return jnp.clip(values, min=-reach, max=reach).astype(dtype)


def setup_inputs(seed: int = 0) -> dict:
    streams_of = jax.random.split(jax.random.key(seed), 3)
    right_side = centred(streams_of[0], (VEC, 3, NZ, NX, NY), 1.0, 6.0, ((3, 8), (4, 4)), jnp.float32)
    material = with_ends((jax.random.randint(streams_of[1], (NZ, NX, NY), 0, 4) < 3).astype(jnp.int32), jax.random.fold_in(streams_of[1], 1), 0, 1)
    return dict(right_side=right_side, material=material)


relax_weight = 0.6
mass_shift = 0.01
grad_div = 2.5
unit_moves = ((0, 1, 0), (0, 0, 1), (1, 0, 0))


def offset_view(padded, move):
    depth_z = padded.shape[-3]
    width_x = padded.shape[-2]
    width_y = padded.shape[-1]
    return padded[..., 1 + move[0]:depth_z - 1 + move[0], 1 + move[1]:width_x - 1 + move[1], 1 + move[2]:width_y - 1 + move[2]]


def signed_move(first, first_sign, second, second_sign):
    return tuple(first_sign * first[index] + second_sign * second[index] for index in range(3))


def diagonal_of(coeff_pad, scale):
    coeff = offset_view(coeff_pad, (0, 0, 0))
    faces = jnp.zeros_like(coeff)
    for direction in range(3):
        for sign in (1, -1):
            move = tuple(sign * entry for entry in unit_moves[direction])
            faces = faces + 0.5 * (coeff + offset_view(coeff_pad, move))
    return mass_shift + scale * (faces + 2.0 * grad_div * coeff)


def stencil(padded, coeff_pad, scale):
    center = offset_view(padded, (0, 0, 0))
    coeff = offset_view(coeff_pad, (0, 0, 0))
    laplace = jnp.zeros_like(center)
    for direction in range(3):
        for sign in (1, -1):
            move = tuple(sign * entry for entry in unit_moves[direction])
            face = 0.5 * (coeff + offset_view(coeff_pad, move))
            laplace = laplace + face * (center - offset_view(padded, move))
    pieces = []
    for comp in range(3):
        total = jnp.zeros_like(center[:, 0])
        for other in range(3):
            field = padded[:, other]
            if comp == other:
                step_move = unit_moves[comp]
                back_move = tuple(-entry for entry in step_move)
                total = total + (offset_view(field, step_move) - 2.0 * offset_view(field, (0, 0, 0)) + offset_view(field, back_move))
            else:
                first = unit_moves[comp]
                second = unit_moves[other]
                mixed = offset_view(field, signed_move(first, 1, second, 1)) - offset_view(field, signed_move(first, 1, second, -1))
                mixed = mixed - offset_view(field, signed_move(first, -1, second, 1)) + offset_view(field, signed_move(first, -1, second, -1))
                total = total + 0.25 * mixed
        pieces.append(total)
    graddiv = jnp.stack(pieces, axis=1)
    return mass_shift * center + scale * (laplace - grad_div * coeff * graddiv)


def coarsen(array):
    lead = array.shape[:-3]
    depth_z, width_x, width_y = array.shape[-3:]
    grouped = array.reshape(lead + (depth_z // 2, 2, width_x // 2, 2, width_y // 2, 2))
    return jnp.mean(grouped, axis=(-5, -3, -1))


def refine(array):
    return jnp.repeat(jnp.repeat(jnp.repeat(array, 2, axis=-3), 2, axis=-2), 2, axis=-1)


def operate(field, coeff, scale):
    padded = jnp.pad(field, ((0, 0), (0, 0), (1, 1), (1, 1), (1, 1)))
    return stencil(padded, jnp.pad(coeff, 1), scale)


def cycle(source, coeff, level):
    scale = 0.25 ** level
    diagonal = diagonal_of(jnp.pad(coeff, 1), scale)
    current = relax_weight * source / diagonal
    if level == LEVELS - 1:
        for sweep in range(COARSE - 1):
            current = current + relax_weight * (source - operate(current, coeff, scale)) / diagonal
        return current
    current = current + relax_weight * (source - operate(current, coeff, scale)) / diagonal
    remainder = source - operate(current, coeff, scale)
    correction = cycle(coarsen(remainder), coarsen(coeff), level + 1)
    current = current + refine(correction)
    for sweep in range(2):
        current = current + relax_weight * (source - operate(current, coeff, scale)) / diagonal
    return current


def reference(right_side, material):
    coeff = jnp.where(material == 1, 1.0, 0.05).astype(jnp.float32)
    return cycle(right_side, coeff, 0)
```

```python
import functools

import jax
import jax.numpy as jnp
from jax import lax
from jax.experimental import pallas as pl
from jax.experimental.pallas import tpu as pltpu
from jax.sharding import PartitionSpec as P

RELAX = 0.6
MASS = 0.01
GRAD_DIV = 2.5
VEC, COMP, NZ, BX, BY = 4, 3, 8, 8, 128
COARSE = 6
RIM = 16
SEG = BY + 2 * RIM
L0 = VEC * SEG
L1 = 256
FX = 6
CX = 7
F32 = jnp.float32


def iota(shape, dim):
    return lax.broadcasted_iota(jnp.int32, shape, dim)


def exact_dot(value, selector):
    high = value.astype(jnp.bfloat16)
    rest = value - high.astype(F32)
    mid = rest.astype(jnp.bfloat16)
    low = (rest - mid.astype(F32)).astype(jnp.bfloat16)
    dot = functools.partial(jnp.dot, preferred_element_type=F32)
    return dot(high, selector) + dot(mid, selector) + dot(low, selector)


class Level:
    def __init__(self, index, rows, lanes, length=None):
        self.scale = 0.25**index
        self.rows = rows
        self.lanes = lanes
        row = iota((8, lanes), 0)
        self.has_zp, self.has_zm = row < 8 - rows, row >= rows
        self.has_yp = self.has_ym = None
        if length is not None:
            lane = iota((8, lanes), 1)
            self.has_yp, self.has_ym = lane < length - 1, lane > 0

    def yp(self, a):
        return pltpu.roll(a, self.lanes - 1, 1)

    def ym(self, a):
        return pltpu.roll(a, 1, 1)

    def zp(self, a):
        return pltpu.roll(a, 8 - self.rows, 0)

    def zm(self, a):
        return pltpu.roll(a, self.rows, 0)

    @staticmethod
    def keep(mask, a):
        return a if mask is None else jnp.where(mask, a, 0.0)

    def dy_of(self, up, down):
        return self.keep(self.has_yp, up) - self.keep(self.has_ym, down)

    def dz_of(self, up, down):
        return self.keep(self.has_zp, up) - self.keep(self.has_zm, down)

    @property
    def layered(self):
        return self.rows < 8

    def weights(self, coeff, at, k_ref, kat):
        c = coeff[at]
        near = [coeff[at + 1], coeff[at - 1], self.keep(self.has_yp, self.yp(c)), self.keep(self.has_ym, self.ym(c))]
        if self.layered:
            near += [self.keep(self.has_zp, self.zp(c)), self.keep(self.has_zm, self.zm(c))]
        total = near[0]
        for n in near[1:]:
            total = total + n
        diag = MASS + self.scale * (8.0 * c + 0.5 * total)
        gain = jnp.where(c > 0.0, RELAX / diag, 0.0)
        half = (0.5 * self.scale) * gain
        own = (GRAD_DIV * self.scale) * gain * c
        masks = [None, None, self.has_yp, self.has_ym, self.has_zp, self.has_zm]
        for i, n in enumerate(near):
            face = half * (c + n)
            k_ref[i, kat] = self.keep(masks[i], face)
            k_ref[6 + i, kat] = self.keep(masks[i], face + own)
        k_ref[12, kat] = 0.25 * own
        return gain, diag * (1.0 / RELAX)

    def cross(self, u, at, t_ref, tat):
        uy = u[1, at]
        t = self.dy_of(self.yp(uy), self.ym(uy))
        if self.layered:
            uz = u[2, at]
            t = t + self.dz_of(self.zp(uz), self.zm(uz))
        t_ref[tat] = t

    def change(self, u, at, t_ref, tat, k_ref, kat, x1, xat):
        k = lambda i: k_ref[i, kat]
        ux, uy, uz = (u[c, at] for c in range(3))
        fore = [u[c, at + 1] for c in range(3)]
        back = [u[c, at - 1] for c in range(3)]
        y_up = [self.yp(a) for a in (ux, uy, uz)]
        y_dn = [self.ym(a) for a in (ux, uy, uz)]
        dxx = fore[0] - back[0]
        dyy = self.dy_of(y_up[1], y_dn[1])
        side = dxx
        if self.layered:
            z_up = [self.zp(a) for a in (ux, uy, uz)]
            z_dn = [self.zm(a) for a in (ux, uy, uz)]
            side = dxx + self.dz_of(z_up[2], z_dn[2])
        mixed = [t_ref[tat + 1] - t_ref[tat - 1], self.dy_of(self.yp(side), self.ym(side)), None]
        if self.layered:
            below = dxx + dyy
            mixed[2] = self.dz_of(self.zp(below), self.zm(below))
        out = []
        for c, own in enumerate((ux, uy, uz)):
            total = x1[c, xat] - RELAX * own
            total = total + k(6 if c == 0 else 0) * fore[c] + k(7 if c == 0 else 1) * back[c]
            total = total + k(8 if c == 1 else 2) * y_up[c] + k(9 if c == 1 else 3) * y_dn[c]
            if self.layered:
                total = total + k(10 if c == 2 else 4) * z_up[c] + k(11 if c == 2 else 5) * z_dn[c]
            if mixed[c] is not None:
                total = total + k(12) * mixed[c]
            out.append(total)
        return out

    def apply(self, u, uo, t_ref, k_ref, ko, x1, xo, low, high, unroll, write):
        def ahead(p):
            self.cross(u, p + uo, t_ref, p - low + 1)

        def one(p):
            d = self.change(u, p + uo, t_ref, p - low + 1, k_ref, p + ko, x1, p + xo)
            write(p, d)

        each(low - 1, high + 1, unroll, ahead)
        each(low, high, unroll, one)


def each(low, high, unroll, body):
    count = high - low
    while count % unroll:
        unroll -= 1
    if count == unroll:
        for p in range(low, high):
            body(p)
        return

    def step(i, carry):
        for b in range(unroll):
            body(low + i * unroll + b)
        return carry

    lax.fori_loop(0, count // unroll, step, 0)


def segment_lane(shape, dim):
    lane = iota(shape, dim)
    vec = (lane >= SEG).astype(jnp.int32) + (lane >= 2 * SEG).astype(jnp.int32) + (lane >= 3 * SEG).astype(jnp.int32)
    return vec * 128 + (32 - RIM // 2) + ((lane - vec * SEG) >> 1)


def bf16(mask, value):
    return jnp.where(mask, value, 0.0).astype(jnp.bfloat16)


def rows_of(ref, group, x):
    return ref[pl.ds(group * 64 + x, 8, stride=8), :]


def coeff_rows(m_ref, x):
    return jnp.where(rows_of(m_ref, 0, x) == 1, 1.0, 0.05).astype(F32)


def edge_kernel(f_ref, m_ref, left_ref, right_ref):
    for x in range(BX):
        for v in range(VEC):
            for c in range(COMP):
                val = rows_of(f_ref, v * COMP + c, x)
                lanes = pl.ds((x // 4) * 64 + 16 * v, 16)
                left_ref[c * 4 + x % 4, :, lanes] = val[:, :RIM]
                right_ref[c * 4 + x % 4, :, lanes] = val[:, BY - RIM :]
        val = coeff_rows(m_ref, x)
        left_ref[12, :, pl.ds(16 * x, 16)] = val[:, :RIM]
        right_ref[12, :, pl.ds(16 * x, 16)] = val[:, BY - RIM :]


def join_kernel(gy, f_ref, m_ref, l_ref, r_ref, own_ref, coeff_ref, left_ref, right_ref):
    place = lax.axis_index("gy")
    from_left = (place > 0).astype(F32)
    from_right = (place < gy - 1).astype(F32)
    for x in range(BX):
        for c in range(COMP):
            left = l_ref[c * 4 + x % 4] * from_left
            right = r_ref[c * 4 + x % 4] * from_right
            for v in range(VEC):
                start = SEG * v
                at = (x // 4) * 64 + 16 * v
                own_ref[c, x, :, pl.ds(start, RIM)] = left[:, at : at + RIM]
                own_ref[c, x, :, pl.ds(start + RIM, BY)] = rows_of(f_ref, v * COMP + c, x)
                own_ref[c, x, :, pl.ds(start + RIM + BY, RIM)] = right[:, at : at + RIM]
        start = SEG * (x % 4)
        coeff_ref[x // 4, :, pl.ds(start, RIM)] = l_ref[12, :, pl.ds(16 * x, 16)] * from_left
        coeff_ref[x // 4, :, pl.ds(start + RIM, BY)] = coeff_rows(m_ref, x)
        coeff_ref[x // 4, :, pl.ds(start + RIM + BY, RIM)] = r_ref[12, :, pl.ds(16 * x, 16)] * from_right
    for c in range(COMP):
        for x in range(FX):
            left_ref[c * FX + x] = own_ref[c, x]
            right_ref[c * FX + x] = own_ref[c, x + BX - FX]
    for i in range(2):
        left_ref[COMP * FX + i] = coeff_ref[i]
        right_ref[COMP * FX + i] = coeff_ref[i]


def down_kernel(
    gx, own_ref, coeff_ref, l_ref, r_ref,
    pay_ref, send_l, send_r, x2b_ref, x1b_ref, c1_ref, x2a_ref, x1a_ref, c0_ref,
    cx, k0, dr0, x1, x2, t0, rest, stack, k1, dr1, f1, y1, y2, t1, r1, stack1, pay,
):
    place = lax.axis_index("gx")
    from_left = (place > 0).astype(F32)
    from_right = (place < gx - 1).astype(F32)
    a = Level(0, 1, L0)

    def spread(plane, packed, sub, factor):
        val = packed[:, SEG * sub : SEG * sub + SEG]
        if factor is not None:
            val = val * factor
        for v in range(VEC):
            cx[plane + CX, :, pl.ds(SEG * v, SEG)] = val

    for x in range(BX):
        spread(x, coeff_ref[x // 4], x % 4, None)
    for x in range(CX):
        spread(x - CX, l_ref[COMP * FX + (x + BX - CX) // 4], (x + BX - CX) % 4, from_left)
        spread(x + BX, r_ref[COMP * FX + x // 4], x % 4, from_right)

    def start(low, high, load):
        def body(p):
            gain, back = a.weights(cx, p + CX, k0, p + FX)
            dr0[p + FX] = back
            for c in range(COMP):
                x1[c, p + FX] = gain * load(c, p)

        each(low, high, 1, body)

    start(-FX, 0, lambda c, p: l_ref[c * FX + p + FX])
    start(0, BX, lambda c, p: own_ref[c, p])
    start(BX, BX + FX, lambda c, p: r_ref[c * FX + p - BX])

    def to_x2(p, change):
        for c in range(COMP):
            x2[c, p + FX] = x1[c, p + FX] + change[c]

    a.apply(x1, FX, t0, k0, FX, x1, FX, 1 - FX, BX + FX - 1, 2, to_x2)

    def to_rest(p, change):
        for c in range(COMP):
            rest[c, p + 4] = change[c] * dr0[p + FX]

    a.apply(x2, FX, t0, k0, FX, x1, FX, -4, BX + 4, 2, to_rest)

    def gather_rows(i, plane):
        stack[pl.ds(8 * i, 8), :] = plane + a.zp(plane)

    for c in range(COMP):
        for i in range(8):
            gather_rows(8 * c + i, rest[c, 2 * i] + rest[c, 2 * i + 1])
    for i in range(10):
        gather_rows(24 + i, cx[2 * i + 1] + cx[2 * i + 2])
    selector = bf16(segment_lane((L0, 2 * L1), 0) == iota((L0, 2 * L1), 1), 0.125)
    coarse = exact_dot(stack[...], selector)
    even = (iota((8, L1), 0) & 1) == 0

    def merged(i):
        block = coarse[8 * i : 8 * i + 8]
        return jnp.where(even, block[:, :L1], pltpu.roll(block[:, L1:], 1, 0))

    for c in range(COMP):
        for i in range(8):
            f1[c, i] = merged(8 * c + i)
    for i in range(10):
        c1_ref[i] = merged(24 + i)

    b = Level(1, 2, L1)
    for p in range(-2, 6):
        gain, back = b.weights(c1_ref, p + 3, k1, p + 2)
        dr1[p + 2] = back
        for c in range(COMP):
            y1[c, p + 2] = gain * f1[c, p + 2]

    def to_y2(p, change):
        for c in range(COMP):
            y2[c, p + 1] = y1[c, p + 2] + change[c]

    b.apply(y1, 2, t1, k1, 2, y1, 2, -1, 5, 2, to_y2)

    def to_r1(p, change):
        for c in range(COMP):
            r1[c, p] = change[c] * dr1[p + 2]

    b.apply(y2, 1, t1, k1, 2, y1, 2, 0, 4, 2, to_r1)

    def gather_rows1(i, plane):
        plane = plane + b.zp(plane)
        stack1[pl.ds(8 * i, 8), :] = plane[:, :128]
        stack1[pl.ds(64 + 8 * i, 8), :] = plane[:, 128:]

    for c in range(COMP):
        for i in range(2):
            gather_rows1(2 * c + i, r1[c, 2 * i] + r1[c, 2 * i + 1])
    for i in range(2):
        gather_rows1(6 + i, c1_ref[2 * i + 3] + c1_ref[2 * i + 4])
    lane = iota((128, 128), 0) - 32
    selector1 = bf16((lane >> 1 == iota((128, 128), 1)) & (lane >= 0) & (lane < 64), 0.125)
    coarse1 = exact_dot(stack1[...], selector1)
    first = (iota((8, 32), 0) & 2) == 0
    for g in range(8):
        low = coarse1[8 * g : 8 * g + 8]
        high = pltpu.roll(coarse1[64 + 8 * g : 72 + 8 * g], 2, 0)
        pay[pl.ds(8 * (g // 4), 8), pl.ds(32 * (g % 4), 32)] = jnp.where(first, low[:, :32], high[:, :32])
    packed = pay[...]

    def copy(i, carry):
        pay_ref[i] = packed
        return carry

    lax.fori_loop(0, pay_ref.shape[0], copy, 0)

    for c in range(COMP):
        for i in range(3):
            send_l[3 * c + i] = y2[c, 1 + i]
            send_r[3 * c + i] = y2[c, 2 + i]
        for i in range(4):
            x2b_ref[c, i] = y2[c, 1 + i]
        for i in range(8):
            x1b_ref[c, i] = y1[c, i]
        for i in range(12):
            x2a_ref[c, i] = x2[c, i + 4]
        for i in range(10):
            x1a_ref[c, i] = x1[c, i + 5]
    for i in range(12):
        c0_ref[i] = cx[i + 5]


def up_kernel(
    gx, gy, got_ref, l_ref, r_ref, x2b_ref, x1b_ref, c1_ref, x2a_ref, x1a_ref, c0_ref, out_ref,
    c2, f2, k2, dr2, x1c, ua, ub, rc, t2, s2, c3, k3, x1d, va, vb, t3, s3, sw, w0, w1, k1, t1, sp, k0, u0, u1, t0,
):
    nx2, nx3 = 2 * gx, gx
    y2, l3 = 32 * gy, c3.shape[-1]
    place_x = lax.axis_index("gx")
    place_y = lax.axis_index("gy")
    from_left = (place_x > 0).astype(F32)
    from_right = (place_x < gx - 1).astype(F32)

    zero2 = jnp.zeros((8, y2), F32)
    for ref in (ua, ub):
        for c in range(COMP):
            for i in (0, 1, nx2 + 2, nx2 + 3):
                ref[c, i] = zero2
    c2[0] = zero2
    c2[nx2 + 1] = zero2

    def unpack(i):
        for j in range(gy):
            for g in range(8):
                block = got_ref[i * gy + j, pl.ds(8 * (g // 4), 8), pl.ds(32 * (g % 4), 32)]
                if g < 6:
                    f2[g // 2, 2 * i + g % 2, :, pl.ds(32 * j, 32)] = block
                else:
                    c2[2 * i + g - 5, :, pl.ds(32 * j, 32)] = block

    each(0, gx, 8, unpack)
    m = Level(2, 4, y2, y2)

    def start2(p):
        gain, back = m.weights(c2, p + 1, k2, p)
        dr2[p] = back
        for c in range(COMP):
            val = gain * f2[c, p]
            x1c[c, p] = val
            ua[c, p + 2] = val

    each(0, nx2, 4, start2)

    def sweep2(src, dst):
        def write(p, change):
            for c in range(COMP):
                dst[c, p + 2] = src[c, p + 2] + change[c]

        m.apply(src, 2, t2, k2, 0, x1c, 0, 0, nx2, 4, write)

    sweep2(ua, ub)

    def to_rc(p, change):
        for c in range(COMP):
            rc[c, p] = change[c] * dr2[p]

    m.apply(ub, 2, t2, k2, 0, x1c, 0, 0, nx2, 4, to_rc)

    def gather2(i):
        for c in range(COMP):
            plane = rc[c, 2 * i] + rc[c, 2 * i + 1]
            s2[pl.ds(8 * (c * nx3 + i), 8), :] = plane + pltpu.roll(plane, 4, 0)
        plane = c2[2 * i + 1] + c2[2 * i + 2]
        s2[pl.ds(8 * (COMP * nx3 + i), 8), :] = plane + pltpu.roll(plane, 4, 0)

    for i in range(nx3):
        gather2(i)
    selector = bf16((iota((y2, l3), 0) >> 1) == iota((y2, l3), 1), 0.125)
    coarse = exact_dot(s2[...], selector)
    zero3 = jnp.zeros((8, l3), F32)
    for ref in (va, vb):
        for c in range(COMP):
            ref[c, 0] = zero3
            ref[c, nx3 + 1] = zero3
    c3[0] = zero3
    c3[nx3 + 1] = zero3
    for i in range(nx3):
        c3[i + 1] = coarse[8 * (COMP * nx3 + i) : 8 * (COMP * nx3 + i) + 8]
    n = Level(3, 8, l3, 16 * gy)
    for p in range(nx3):
        gain, _ = n.weights(c3, p + 1, k3, p)
        for c in range(COMP):
            val = gain * coarse[8 * (c * nx3 + p) : 8 * (c * nx3 + p) + 8]
            x1d[c, p] = val
            va[c, p + 1] = val
    src, dst = va, vb
    for _ in range(COARSE - 1):

        def write3(p, change, src=src, dst=dst):
            for c in range(COMP):
                dst[c, p + 1] = src[c, p + 1] + change[c]

        n.apply(src, 1, t3, k3, 0, x1d, 0, 0, nx3, 8, write3)
        src, dst = dst, src
    for c in range(COMP):
        for i in range(nx3):
            s3[pl.ds(8 * (c * nx3 + i), 8), :] = src[c, i + 1]
    selector = bf16((iota((l3, y2), 1) >> 1) == iota((l3, y2), 0), 1.0)
    fine = exact_dot(s3[...], selector)
    for c in range(COMP):
        for i in range(nx3):
            block = fine[8 * (c * nx3 + i) : 8 * (c * nx3 + i) + 8]
            for j in range(2):
                ub[c, 2 * i + j + 2] = ub[c, 2 * i + j + 2] + block
    sweep2(ub, ua)
    sweep2(ua, ub)

    row = iota((8, y2), 0)
    for c in range(COMP):
        for i in range(6):
            e = ub[c, 2 * place_x + i]
            at = 16 * (6 * c + i)
            sw[pl.ds(at, 8), :] = jnp.where((row & 2) == 0, e, pltpu.roll(e, 2, 0))
            sw[pl.ds(at + 8, 8), :] = jnp.where((row & 2) != 0, e, pltpu.roll(e, 6, 0))
    y1g = place_y * 64 + iota((y2, 128), 1) - 32
    fine = exact_dot(sw[...], bf16((y1g >> 1) == iota((y2, 128), 0), 1.0))
    for c in range(COMP):
        for p in range(-3, 7):
            if p < 0:
                val = l_ref[3 * c + p + 3] * from_left
            elif p < 4:
                val = x2b_ref[c, p]
            else:
                val = r_ref[3 * c + p - 4] * from_right
            at = 16 * (6 * c + (p + 4) // 2)
            w0[c, p + 3] = val + jnp.concatenate([fine[at : at + 8], fine[at + 8 : at + 16]], axis=1)
    b = Level(1, 2, L1)
    for p in range(-2, 6):
        b.weights(c1_ref, p + 3, k1, p + 2)

    def write1(p, change):
        for c in range(COMP):
            w1[c, p + 3] = w0[c, p + 3] + change[c]

    b.apply(w0, 3, t1, k1, 2, x1b_ref, 2, -2, 6, 2, write1)

    odd = (iota((8, L1), 0) & 1) != 0

    def write1b(p, change):
        for c in range(COMP):
            e = w1[c, p + 3] + change[c]
            at = 8 * (6 * c + p + 1)
            sp[pl.ds(at, 8), pl.ds(0, L1)] = jnp.where(odd, pltpu.roll(e, 1, 0), e)
            sp[pl.ds(at, 8), pl.ds(L1, L1)] = jnp.where(odd, e, pltpu.roll(e, 7, 0))

    for p in range(-2, 6):
        b.cross(w1, p + 3, t1, p + 2)
    for p in range(-1, 5):
        write1b(p, b.change(w1, p + 3, t1, p + 2, k1, p + 2, x1b_ref, p + 2))

    selector = bf16(segment_lane((2 * L1, L0), 1) == iota((2 * L1, L0), 0), 1.0)
    fine = exact_dot(sp[...], selector)
    for c in range(COMP):
        for i in range(6):
            block = fine[8 * (6 * c + i) : 8 * (6 * c + i) + 8]
            for j in range(2):
                u0[c, 2 * i + j] = x2a_ref[c, 2 * i + j] + block
    a = Level(0, 1, L0)

    def start0(p):
        a.weights(c0_ref, p + 2, k0, p + 1)

    each(-1, 9, 1, start0)

    def write0(p, change):
        for c in range(COMP):
            u1[c, p + 2] = u0[c, p + 2] + change[c]

    a.apply(u0, 2, t0, k0, 1, x1a_ref, 1, -1, 9, 2, write0)

    def write_out(p, change):
        for c in range(COMP):
            val = u1[c, p + 2] + change[c]
            for v in range(VEC):
                at = SEG * v + RIM
                out_ref[pl.ds((v * COMP + c) * 64 + p, 8, stride=8), :] = val[:, at : at + BY]

    a.apply(u1, 2, t0, k0, 1, x1a_ref, 1, 0, BX, 2, write_out)


def call(kernel, outs, scratch, *args):
    vmem = pl.BlockSpec(memory_space=pltpu.VMEM)
    shapes = [jax.ShapeDtypeStruct(s, F32) for s in outs]
    return pl.pallas_call(
        kernel,
        out_shape=shapes,
        in_specs=[vmem] * len(args),
        out_specs=[vmem] * len(outs),
        scratch_shapes=[pltpu.VMEM(s, F32) for s in scratch],
        compiler_params=pltpu.CompilerParams(vmem_limit_bytes=48 * 1024 * 1024),
    )(*args)


def per_device(gx, gy, right_side, material):
    def ring(value, axis, size, step):
        return lax.ppermute(value, axis, [(i, (i + step) % size) for i in range(size)])

    f = right_side.reshape(VEC * COMP * NZ * BX, BY)
    m = material.reshape(NZ * BX, BY)
    edge = (13, 8, 128)
    to_left, to_right = call(edge_kernel, [edge, edge], [], f, m)
    right = ring(to_left, "gy", gy, -1)
    left = ring(to_right, "gy", gy, 1)
    side = (COMP * FX + 2, 8, L0)
    own, coeff, to_left, to_right = call(
        functools.partial(join_kernel, gy), [(COMP, BX, 8, L0), (2, 8, L0), side, side], [], f, m, left, right
    )
    right = ring(to_left, "gx", gx, -1)
    left = ring(to_right, "gx", gx, 1)
    n = gx * gy
    plane = lambda *lead: (*lead, 8, L0)
    plane1 = lambda *lead: (*lead, 8, L1)
    pay, to_left, to_right, *kept = call(
        functools.partial(down_kernel, gx),
        [(n, 16, 128), plane1(9), plane1(9), plane1(3, 4), plane1(3, 8), plane1(10), plane(3, 12), plane(3, 10), plane(12)],
        [
            plane(22), plane(13, 20), plane(20), plane(3, 20), plane(3, 20), plane(20), plane(3, 16), (272, L0),
            plane1(13, 8), plane1(8), plane1(3, 8), plane1(3, 8), plane1(3, 6), plane1(8), plane1(3, 4), (128, 128), (16, 128),
        ],
        own, coeff, left, right,
    )
    right = ring(to_left, "gx", gx, -1)
    left = ring(to_right, "gx", gx, 1)
    got = lax.all_to_all(pay, ("gx", "gy"), 0, 0)
    nx2, nx3, y2, l3 = 2 * gx, gx, 32 * gy, max(128, 16 * gy)
    plane2 = lambda *lead: (*lead, 8, y2)
    plane3 = lambda *lead: (*lead, 8, l3)
    (out,) = call(
        functools.partial(up_kernel, gx, gy),
        [(VEC * COMP * NZ * BX, BY)],
        [
            plane2(nx2 + 2), plane2(3, nx2), plane2(13, nx2), plane2(nx2), plane2(3, nx2), plane2(3, nx2 + 4), plane2(3, nx2 + 4),
            plane2(3, nx2), plane2(nx2 + 2), (32 * nx3, y2),
            plane3(nx3 + 2), plane3(13, nx3), plane3(3, nx3), plane3(3, nx3 + 2), plane3(3, nx3 + 2), plane3(nx3 + 2), (24 * nx3, l3),
            (288, y2), plane1(3, 10), plane1(3, 10), plane1(13, 8), plane1(10), (144, 2 * L1),
            plane(13, 10), plane(3, 12), plane(3, 12), plane(12),
        ],
        got, left, right, *kept,
    )
    return out.reshape(right_side.shape)


def solution(mesh):
    gx, gy = mesh.shape["gx"], mesh.shape["gy"]
    spec = P(None, None, None, "gx", "gy")
    return jax.shard_map(
        functools.partial(per_device, gx, gy), mesh=mesh, in_specs=(spec, P(None, "gx", "gy")), out_specs=spec, check_vma=False
    )
```

```python
import functools

import jax
import jax.numpy as jnp
from jax import lax
from jax.experimental import pallas as pl
from jax.experimental.pallas import tpu as pltpu
from jax.sharding import PartitionSpec as P

RELAX = 0.6
MASS = 0.01
GRAD_DIV = 2.5
VEC, COMP, NZ, BX, BY = 4, 3, 8, 8, 128
COARSE = 6
UNROLL0, UNROLL1, UNROLL2 = 1, 2, 8
RIM = 16
LEFT = 11
PIECE = 108
SPLIT = 112
L0 = 5 * 128
K0 = 2 * 128
L1 = 2 * 128
FX = 6
CX = 7
F32 = jnp.float32


def iota(shape, dim):
    return lax.broadcasted_iota(jnp.int32, shape, dim)


def parts_of(value):
    high = value.astype(jnp.bfloat16)
    rest = value - high.astype(F32)
    mid = rest.astype(jnp.bfloat16)
    return high, mid, (rest - mid.astype(F32)).astype(jnp.bfloat16)


def exact_dot(parts, selector):
    out = [jnp.dot(p, selector, preferred_element_type=F32) for p in parts]
    return out[0] + out[1] + out[2]


class Level:
    def __init__(self, index, rows, width, kinds, length=None):
        self.scale = 0.25**index
        self.rows = rows
        self.width = width
        self.kinds = kinds
        row = iota((8, width), 0)
        self.has_zp, self.has_zm = row < 8 - rows, row >= rows
        self.has_yp = self.has_ym = None
        if length is not None:
            lane = iota((8, width), 1)
            self.has_yp, self.has_ym = lane < length - 1, lane > 0

    def lanes(self, tile):
        return pl.ds(tile * self.width, self.width)

    def yp(self, a):
        return pltpu.roll(a, self.width - 1, 1)

    def ym(self, a):
        return pltpu.roll(a, 1, 1)

    def zp(self, a):
        return pltpu.roll(a, 8 - self.rows, 0)

    def zm(self, a):
        return pltpu.roll(a, self.rows, 0)

    @staticmethod
    def keep(mask, a):
        return a if mask is None else jnp.where(mask, a, 0.0)

    def dy_of(self, up, down):
        return self.keep(self.has_yp, up) - self.keep(self.has_ym, down)

    def dz_of(self, up, down):
        return self.keep(self.has_zp, up) - self.keep(self.has_zm, down)

    @property
    def layered(self):
        return self.rows < 8

    def weights(self, coeff, at, k_ref, kat):
        gains, backs = [], []
        for kind in range(max(self.kinds) + 1):
            lanes = self.lanes(kind)
            c = coeff[at, :, lanes]
            near = [coeff[at + 1, :, lanes], coeff[at - 1, :, lanes]]
            near += [self.keep(self.has_yp, self.yp(c)), self.keep(self.has_ym, self.ym(c))]
            if self.layered:
                near += [self.keep(self.has_zp, self.zp(c)), self.keep(self.has_zm, self.zm(c))]
            total = near[0]
            for n in near[1:]:
                total = total + n
            diag = MASS + self.scale * (8.0 * c + 0.5 * total)
            gain = jnp.where(c > 0.0, RELAX / diag, 0.0)
            half = (0.5 * self.scale) * gain
            own = (GRAD_DIV * self.scale) * gain * c
            masks = [None, None, self.has_yp, self.has_ym, self.has_zp, self.has_zm]
            for i, n in enumerate(near):
                face = half * (c + n)
                k_ref[i, kat, :, lanes] = self.keep(masks[i], face)
                k_ref[6 + i, kat, :, lanes] = self.keep(masks[i], face + own)
            k_ref[12, kat, :, lanes] = 0.25 * own
            gains.append(gain)
            backs.append(diag * (1.0 / RELAX))
        return gains, backs

    def cross(self, u, at, t_ref, tat):
        for tile in range(len(self.kinds)):
            lanes = self.lanes(tile)
            uy = u[1, at, :, lanes]
            t = self.dy_of(self.yp(uy), self.ym(uy))
            if self.layered:
                uz = u[2, at, :, lanes]
                t = t + self.dz_of(self.zp(uz), self.zm(uz))
            t_ref[tat, :, lanes] = t

    def change(self, u, at, t_ref, px_ref, tat, k_ref, kat, x1, xat, write):
        for tile, kind in enumerate(self.kinds):
            lanes = self.lanes(tile)
            k = lambda i: k_ref[i, kat, :, self.lanes(kind)]
            mine = [u[c, at, :, lanes] for c in range(3)]
            fore = [u[c, at + 1, :, lanes] for c in range(3)]
            back = [u[c, at - 1, :, lanes] for c in range(3)]
            y_up = [self.yp(a) for a in mine]
            y_dn = [self.ym(a) for a in mine]
            dxx = fore[0] - back[0]
            dyy = self.dy_of(y_up[1], y_dn[1])
            side = dxx
            cross = dyy
            if self.layered:
                z_up = [self.zp(a) for a in mine]
                z_dn = [self.zm(a) for a in mine]
                dzz = self.dz_of(z_up[2], z_dn[2])
                side = dxx + dzz
                cross = dyy + dzz
            t_ref[tat, :, lanes] = cross
            mixed = [None, self.dy_of(self.yp(side), self.ym(side)), None]
            if self.layered:
                below = dxx + dyy
                mixed[2] = self.dz_of(self.zp(below), self.zm(below))
            for c in range(3):
                total = x1[c, xat, :, lanes] - RELAX * mine[c]
                total = total + (k(6 if c == 0 else 0) * fore[c] + k(7 if c == 0 else 1) * back[c])
                sides = k(8 if c == 1 else 2) * y_up[c] + k(9 if c == 1 else 3) * y_dn[c]
                if self.layered:
                    sides = sides + (k(10 if c == 2 else 4) * z_up[c] + k(11 if c == 2 else 5) * z_dn[c])
                if mixed[c] is not None:
                    sides = sides + k(12) * mixed[c]
                if c == 0:
                    px_ref[tat, :, lanes] = total + sides
                else:
                    write(c, tile, lanes, total + sides)

    def apply(self, u, uo, t_ref, px_ref, k_ref, ko, x1, xo, low, high, unroll, write):
        self.cross(u, low - 1 + uo, t_ref, 0)
        self.cross(u, high + uo, t_ref, high - low + 1)

        def one(p):
            def put(c, tile, lanes, d):
                write(c, p, tile, lanes, d)

            self.change(u, p + uo, t_ref, px_ref, p - low + 1, k_ref, p + ko, x1, p + xo, put)

        def mixed(p):
            at = p - low + 1
            for tile, kind in enumerate(self.kinds):
                lanes = self.lanes(tile)
                t = t_ref[at + 1, :, lanes] - t_ref[at - 1, :, lanes]
                write(0, p, tile, lanes, px_ref[at, :, lanes] + k_ref[12, p + ko, :, self.lanes(kind)] * t)

        each(low, high, unroll, one)
        each(low, high, 2 * unroll, mixed)


def each(low, high, unroll, body):
    count = high - low
    while count % unroll:
        unroll -= 1
    if count == unroll:
        for p in range(low, high):
            body(p)
        return

    def step(i, carry):
        for b in range(unroll):
            body(low + i * unroll + b)
        return carry

    lax.fori_loop(0, count // unroll, step, 0)


def tile_y(lane):
    return (lane & 127) - LEFT, PIECE + (lane & 31), (lane & 127) >> 5


def bf16(mask, value):
    return jnp.where(mask, value, 0.0).astype(jnp.bfloat16)


def rows_of(ref, group, x):
    return ref[pl.ds(group * 64 + x, 8, stride=8), :]


def coeff_rows(m_ref, x):
    return jnp.where(rows_of(m_ref, 0, x) == 1, 1.0, 0.05).astype(F32)


def edge_kernel(f_ref, m_ref, left_ref, right_ref):
    for x in range(BX):
        for v in range(VEC):
            for c in range(COMP):
                val = rows_of(f_ref, v * COMP + c, x)
                lanes = pl.ds((x // 4) * 64 + 16 * v, 16)
                left_ref[c * 4 + x % 4, :, lanes] = val[:, :RIM]
                right_ref[c * 4 + x % 4, :, lanes] = val[:, BY - RIM :]
        val = coeff_rows(m_ref, x)
        left_ref[12, :, pl.ds(16 * x, 16)] = val[:, :RIM]
        right_ref[12, :, pl.ds(16 * x, 16)] = val[:, BY - RIM :]


def join_kernel(gy, f_ref, m_ref, l_ref, r_ref, own_ref, left_ref, right_ref):
    place = lax.axis_index("gy")
    from_left = (place > 0).astype(F32)
    from_right = (place < gy - 1).astype(F32)
    kept = BY - PIECE

    def put(ref, at, start, piece_at, piece_start, val, left, right):
        ref[*at, :, pl.ds(start, LEFT)] = left[:, RIM - LEFT :]
        ref[*at, :, pl.ds(start + LEFT, 128 - LEFT)] = val[:, : 128 - LEFT]
        ref[*piece_at, :, pl.ds(piece_start, kept)] = val[:, PIECE:]
        ref[*piece_at, :, pl.ds(piece_start + kept, 32 - kept)] = right[:, : 32 - kept]

    for x in range(BX):
        for c in range(COMP):
            left = l_ref[c * 4 + x % 4] * from_left
            right = r_ref[c * 4 + x % 4] * from_right
            for v in range(VEC):
                at = (x // 4) * 64 + 16 * v
                val = rows_of(f_ref, v * COMP + c, x)
                place = (BX * c + x,)
                put(own_ref, place, 128 * v, place, 512 + 32 * v, val, left[:, at : at + RIM], right[:, at : at + RIM])
        left = l_ref[12, :, pl.ds(16 * x, 16)] * from_left
        right = r_ref[12, :, pl.ds(16 * x, 16)] * from_right
        base = COMP * BX
        at, piece = x, 8 + x // 4
        put(
            own_ref, (base + at // 5,), 128 * (at % 5), (base + piece // 5,), 128 * (piece % 5) + 32 * (x % 4),
            coeff_rows(m_ref, x), left, right,
        )
    for c in range(COMP):
        for x in range(FX):
            left_ref[c * FX + x] = own_ref[BX * c + x]
            right_ref[c * FX + x] = own_ref[BX * c + x + BX - FX]
    for i in range(2):
        left_ref[COMP * FX + i] = own_ref[COMP * BX + i]
        right_ref[COMP * FX + i] = own_ref[COMP * BX + i]


def down_kernel(
    gx, own_ref, l_ref, r_ref,
    pay_ref, send_l, send_r, x1, x2, k0, y1, y2, k1,
    cx, dr0, t0, p0, rest, stack, cstack, c1, dr1, f1, t1, p1, r1, stack1, pay,
):
    place = lax.axis_index("gx")
    from_left = (place > 0).astype(F32)
    from_right = (place < gx - 1).astype(F32)
    a = Level(0, 1, 128, (0, 0, 0, 0, 1))

    def spread(plane, ref, base, x, factor):
        at, piece = x, 8 + x // 4
        val = ref[base + at // 5, :, pl.ds(128 * (at % 5), 128)]
        end = ref[base + piece // 5, :, pl.ds(128 * (piece % 5) + 32 * (x % 4), 32)]
        if factor is not None:
            val, end = val * factor, end * factor
        cx[plane + CX, :, pl.ds(0, 128)] = val
        for v in range(VEC):
            cx[plane + CX, :, pl.ds(128 + 32 * v, 32)] = end

    for x in range(BX):
        spread(x, own_ref, COMP * BX, x, None)
    for x in range(CX):
        spread(x - CX, l_ref, COMP * FX, x + BX - CX, from_left)
        spread(x + BX, r_ref, COMP * FX, x, from_right)

    def start(low, high, load):
        def body(p):
            gain, back = a.weights(cx, p + CX, k0, p + FX)
            for kind in range(2):
                dr0[p + FX, :, a.lanes(kind)] = back[kind]
            for c in range(COMP):
                plane = load(c, p)
                for tile, kind in enumerate(a.kinds):
                    x1[c, p + FX, :, a.lanes(tile)] = gain[kind] * plane[:, 128 * tile : 128 * tile + 128]

        each(low, high, 2, body)

    start(-FX, 0, lambda c, p: l_ref[c * FX + p + FX])
    start(0, BX, lambda c, p: own_ref[BX * c + p])
    start(BX, BX + FX, lambda c, p: r_ref[c * FX + p - BX])

    def to_x2(c, p, tile, lanes, d):
        x2[c, p + FX, :, lanes] = x1[c, p + FX, :, lanes] + d

    a.apply(x1, FX, t0, p0, k0, FX, x1, FX, 1 - FX, BX + FX - 1, UNROLL0, to_x2)

    def to_rest(c, p, tile, lanes, d):
        rest[c, p + 4, :, lanes] = d * dr0[p + FX, :, a.lanes(a.kinds[tile])]

    a.apply(x2, FX, t0, p0, k0, FX, x1, FX, -4, BX + 4, UNROLL0, to_rest)

    for c in range(COMP):
        for i in range(8):
            plane = rest[c, 2 * i] + rest[c, 2 * i + 1]
            stack[pl.ds(64 * c + 8 * i, 8), :] = plane + a.zp(plane)
    for i in range(10):
        plane = cx[2 * i + 1] + cx[2 * i + 2]
        cstack[pl.ds(8 * i, 8), :] = plane + a.zp(plane)
    selectors = []
    row, col = iota((K0, 128), 0), iota((K0, 128), 1)
    y, y_piece, vec = tile_y(row)
    for v in range(VEC):
        own_tile = (row < 128) & (y >= -8) & (y < SPLIT) & ((y >> 1) + 32 == col)
        piece = (row >= 128) & (vec == v) & (y_piece >= SPLIT) & (y_piece < BY + 8) & ((y_piece >> 1) + 32 == col)
        selectors.append(bf16(own_tile | piece, 0.125))
    parts = parts_of(stack[...])
    coarse = [
        exact_dot([jnp.concatenate([p[:, 128 * v : 128 * v + 128], p[:, 512:]], axis=1) for p in parts], selectors[v])
        for v in range(VEC)
    ]
    coarse_c = exact_dot(parts_of(cstack[...]), selectors[0])
    even = (iota((8, 128), 0) & 1) == 0
    for c in range(COMP):
        for i in range(8):
            at = 64 * c + 8 * i
            for low in range(2):
                odd = pltpu.roll(coarse[2 + low][at : at + 8], 1, 0)
                f1[c, i, :, pl.ds(128 * low, 128)] = jnp.where(even, coarse[low][at : at + 8], odd)
    for i in range(10):
        block = coarse_c[8 * i : 8 * i + 8]
        c1[i] = jnp.where(even, block, pltpu.roll(block, 1, 0))

    b = Level(1, 2, 128, (0, 0))
    for p in range(-2, 6):
        gain, back = b.weights(c1, p + 3, k1, p + 2)
        dr1[p + 2] = back[0]
        for c in range(COMP):
            for tile in range(2):
                y1[c, p + 2, :, b.lanes(tile)] = gain[0] * f1[c, p + 2, :, b.lanes(tile)]

    def to_y2(c, p, tile, lanes, d):
        y2[c, p + 1, :, lanes] = y1[c, p + 2, :, lanes] + d

    b.apply(y1, 2, t1, p1, k1, 2, y1, 2, -1, 5, UNROLL1, to_y2)
    for c in range(COMP):
        for i in range(3):
            send_l[3 * c + i] = y2[c, 1 + i]
            send_r[3 * c + i] = y2[c, 2 + i]

    def to_r1(c, p, tile, lanes, d):
        r1[c, p, :, lanes] = d * dr1[p + 2]

    b.apply(y2, 1, t1, p1, k1, 2, y1, 2, 0, 4, UNROLL1, to_r1)

    for c in range(COMP):
        for i in range(2):
            plane = r1[c, 2 * i] + r1[c, 2 * i + 1]
            plane = plane + pltpu.roll(plane, 6, 0)
            stack1[pl.ds(8 * (2 * c + i), 8), :] = plane[:, :128]
            stack1[pl.ds(64 + 8 * (2 * c + i), 8), :] = plane[:, 128:]
    for i in range(2):
        plane = c1[2 * i + 3] + c1[2 * i + 4]
        plane = plane + b.zp(plane)
        stack1[pl.ds(8 * (6 + i), 8), :] = plane
        stack1[pl.ds(64 + 8 * (6 + i), 8), :] = plane
    lane = iota((128, 128), 0) - 32
    selector1 = bf16((lane >> 1 == iota((128, 128), 1)) & (lane >= 0) & (lane < 64), 0.125)
    coarse1 = exact_dot(parts_of(stack1[...]), selector1)
    first = (iota((8, 32), 0) & 2) == 0
    for g in range(8):
        low = coarse1[8 * g : 8 * g + 8]
        high = pltpu.roll(coarse1[64 + 8 * g : 72 + 8 * g], 2, 0)
        pay[pl.ds(8 * (g // 4), 8), pl.ds(32 * (g % 4), 32)] = jnp.where(first, low[:, :32], high[:, :32])
    packed = pay[...]

    def copy(i):
        pay_ref[i] = packed

    each(0, pay_ref.shape[0], 8, copy)


def up_kernel(
    gx, gy, got_ref, l_ref, r_ref, x1, x2, k0, y1, y2, k1, out_ref,
    c2, f2, k2, dr2, x1c, ua, ub, rc, t2, p2, s2, c3, k3, x1d, va, vb, t3, p3, s3, sw, w0, w1, t1, p1, sp, u0, u1, t0, p0,
):
    nx2, nx3 = 2 * gx, gx
    yy2, l3 = 32 * gy, c3.shape[-1]
    place_x = lax.axis_index("gx")
    place_y = lax.axis_index("gy")
    from_left = (place_x > 0).astype(F32)
    from_right = (place_x < gx - 1).astype(F32)

    zero2 = jnp.zeros((8, yy2), F32)
    for ref in (ua, ub):
        for c in range(COMP):
            for i in (0, 1, nx2 + 2, nx2 + 3):
                ref[c, i] = zero2
    c2[0] = zero2
    c2[nx2 + 1] = zero2

    def unpack(i):
        for j in range(gy):
            for g in range(8):
                block = got_ref[i * gy + j, pl.ds(8 * (g // 4), 8), pl.ds(32 * (g % 4), 32)]
                if g < 6:
                    f2[g // 2, 2 * i + g % 2, :, pl.ds(32 * j, 32)] = block
                else:
                    c2[2 * i + g - 5, :, pl.ds(32 * j, 32)] = block

    each(0, gx, 8, unpack)
    m = Level(2, 4, yy2, (0,), yy2)

    def start2(p):
        gain, back = m.weights(c2, p + 1, k2, p)
        dr2[p] = back[0]
        for c in range(COMP):
            val = gain[0] * f2[c, p]
            x1c[c, p] = val
            ua[c, p + 2] = val

    each(0, nx2, 8, start2)

    def sweep2(src, dst):
        def write(c, p, tile, lanes, d):
            dst[c, p + 2] = src[c, p + 2] + d

        m.apply(src, 2, t2, p2, k2, 0, x1c, 0, 0, nx2, UNROLL2, write)

    sweep2(ua, ub)

    def to_rc(c, p, tile, lanes, d):
        rc[c, p] = d * dr2[p]

    m.apply(ub, 2, t2, p2, k2, 0, x1c, 0, 0, nx2, UNROLL2, to_rc)

    for i in range(nx3):
        for c in range(COMP):
            plane = rc[c, 2 * i] + rc[c, 2 * i + 1]
            s2[pl.ds(8 * (c * nx3 + i), 8), :] = plane + pltpu.roll(plane, 4, 0)
        plane = c2[2 * i + 1] + c2[2 * i + 2]
        s2[pl.ds(8 * (COMP * nx3 + i), 8), :] = plane + pltpu.roll(plane, 4, 0)
    selector = bf16((iota((yy2, l3), 0) >> 1) == iota((yy2, l3), 1), 0.125)
    coarse = exact_dot(parts_of(s2[...]), selector)
    zero3 = jnp.zeros((8, l3), F32)
    for ref in (va, vb):
        for c in range(COMP):
            ref[c, 0] = zero3
            ref[c, nx3 + 1] = zero3
    c3[0] = zero3
    c3[nx3 + 1] = zero3
    for i in range(nx3):
        c3[i + 1] = coarse[8 * (COMP * nx3 + i) : 8 * (COMP * nx3 + i) + 8]
    n = Level(3, 8, l3, (0,), 16 * gy)
    for p in range(nx3):
        gain, _ = n.weights(c3, p + 1, k3, p)
        for c in range(COMP):
            val = gain[0] * coarse[8 * (c * nx3 + p) : 8 * (c * nx3 + p) + 8]
            x1d[c, p] = val
            va[c, p + 1] = val
    src, dst = va, vb
    for _ in range(COARSE - 1):

        def write3(c, p, tile, lanes, d, src=src, dst=dst):
            dst[c, p + 1] = src[c, p + 1] + d

        n.apply(src, 1, t3, p3, k3, 0, x1d, 0, 0, nx3, UNROLL2, write3)
        src, dst = dst, src
    for c in range(COMP):
        for i in range(nx3):
            s3[pl.ds(8 * (c * nx3 + i), 8), :] = src[c, i + 1]
    selector = bf16((iota((l3, yy2), 1) >> 1) == iota((l3, yy2), 0), 1.0)
    fine = exact_dot(parts_of(s3[...]), selector)
    for c in range(COMP):
        for i in range(nx3):
            block = fine[8 * (c * nx3 + i) : 8 * (c * nx3 + i) + 8]
            for j in range(2):
                ub[c, 2 * i + j + 2] = ub[c, 2 * i + j + 2] + block
    sweep2(ub, ua)
    sweep2(ua, ub)

    row = iota((8, yy2), 0)
    for c in range(COMP):
        for i in range(6):
            e = ub[c, 2 * place_x + i]
            at = 16 * (6 * c + i)
            sw[pl.ds(at, 8), :] = jnp.where((row & 2) == 0, e, pltpu.roll(e, 2, 0))
            sw[pl.ds(at + 8, 8), :] = jnp.where((row & 2) != 0, e, pltpu.roll(e, 6, 0))
    y1g = place_y * 64 + iota((yy2, 128), 1) - 32
    fine = exact_dot(parts_of(sw[...]), bf16((y1g >> 1) == iota((yy2, 128), 0), 1.0))
    for c in range(COMP):
        for p in range(-3, 7):
            if p < 0:
                val = l_ref[3 * c + p + 3] * from_left
            elif p < 4:
                val = y2[c, p + 1]
            else:
                val = r_ref[3 * c + p - 4] * from_right
            at = 16 * (6 * c + (p + 4) // 2)
            w0[c, p + 3] = val + jnp.concatenate([fine[at : at + 8], fine[at + 8 : at + 16]], axis=1)
    b = Level(1, 2, 128, (0, 0))

    def write1(c, p, tile, lanes, d):
        w1[c, p + 3, :, lanes] = w0[c, p + 3, :, lanes] + d

    b.apply(w0, 3, t1, p1, k1, 2, y1, 2, -2, 6, UNROLL1, write1)
    odd = (iota((8, 128), 0) & 1) != 0

    def write1b(c, p, tile, lanes, d):
        e = w1[c, p + 3, :, lanes] + d
        rows = pl.ds(8 * (6 * c + p + 1), 8)
        sp[tile, rows, :] = jnp.where(odd, pltpu.roll(e, 1, 0), e)
        sp[2 + tile, rows, :] = jnp.where(odd, e, pltpu.roll(e, 7, 0))

    b.apply(w1, 3, t1, p1, k1, 2, y1, 2, -1, 5, 6, write1b)

    col = iota((128, K0), 1)
    y, y_piece, vec = tile_y(col)
    piece = None
    for v in range(VEC):
        parent = jnp.where(col < 128, y >> 1, y_piece >> 1) + 32
        selector = bf16((parent == iota((128, K0), 0)) & ((col < 128) | (vec == v)), 1.0)
        fine = exact_dot(parts_of(sp[v]), selector)
        piece = fine[:, 128:] if v == 0 else piece + fine[:, 128:]
        for c in range(COMP):
            for i in range(6):
                at = 8 * (6 * c + i)
                for j in range(2):
                    u0[c, 2 * i + j, :, pl.ds(128 * v, 128)] = x2[c, 2 * i + j + 4, :, pl.ds(128 * v, 128)] + fine[at : at + 8, :128]
    for c in range(COMP):
        for i in range(6):
            at = 8 * (6 * c + i)
            for j in range(2):
                u0[c, 2 * i + j, :, pl.ds(512, 128)] = x2[c, 2 * i + j + 4, :, pl.ds(512, 128)] + piece[at : at + 8]
    a = Level(0, 1, 128, (0, 0, 0, 0, 1))

    def write0(c, p, tile, lanes, d):
        u1[c, p + 2, :, lanes] = u0[c, p + 2, :, lanes] + d

    a.apply(u0, 2, t0, p0, k0, FX, x1, FX, -1, 9, UNROLL0, write0)

    def write_last(c, p, tile, lanes, d):
        u0[c, p + 2, :, lanes] = u1[c, p + 2, :, lanes] + d

    a.apply(u1, 2, t0, p0, k0, FX, x1, FX, 0, BX, UNROLL0, write_last)
    near = iota((8, 128), 1) < SPLIT
    for x in range(BX):
        for c in range(COMP):
            last = u0[c, x + 2, :, pl.ds(512, 128)]
            for v in range(VEC):
                main = pltpu.roll(u0[c, x + 2, :, pl.ds(128 * v, 128)], 128 - LEFT, 1)
                ends = pltpu.roll(last, (PIECE - 32 * v) % 128, 1)
                out_ref[pl.ds((v * COMP + c) * 64 + x, 8, stride=8), :] = jnp.where(near, main, ends)


def call(kernel, outs, scratch, *args):
    vmem = pl.BlockSpec(memory_space=pltpu.VMEM)
    shapes = [jax.ShapeDtypeStruct(s, F32) for s in outs]
    return pl.pallas_call(
        kernel,
        out_shape=shapes,
        in_specs=[vmem] * len(args),
        out_specs=[vmem] * len(outs),
        scratch_shapes=[pltpu.VMEM(s, F32) for s in scratch],
        compiler_params=pltpu.CompilerParams(vmem_limit_bytes=32 * 1024 * 1024),
    )(*args)


def per_device(gx, gy, right_side, material):
    def ring(value, axis, size, step):
        return lax.ppermute(value, axis, [(i, (i + step) % size) for i in range(size)])

    f = right_side.reshape(VEC * COMP * NZ * BX, BY)
    m = material.reshape(NZ * BX, BY)
    edge = (13, 8, 128)
    to_left, to_right = call(edge_kernel, [edge, edge], [], f, m)
    right = ring(to_left, "gy", gy, -1)
    left = ring(to_right, "gy", gy, 1)
    side = (COMP * FX + 2, 8, L0)
    own, to_left, to_right = call(
        functools.partial(join_kernel, gy), [(COMP * BX + 2, 8, L0), side, side], [], f, m, left, right
    )
    right = ring(to_left, "gx", gx, -1)
    left = ring(to_right, "gx", gx, 1)
    n = gx * gy
    plane = lambda *lead: (*lead, 8, L0)
    plane1 = lambda *lead: (*lead, 8, L1)
    nf, nc = BX + 2 * FX, BX + 2 * CX
    pay, to_left, to_right, *kept = call(
        functools.partial(down_kernel, gx),
        [
            (n, 16, 128), plane1(9), plane1(9), plane(3, nf), plane(3, nf), (13, nf, 8, K0), plane1(3, 8), plane1(3, 6), (13, 8, 8, 128),
        ],
        [
            (nc, 8, K0), (nf, 8, K0), plane(nf), plane(nf), plane(3, 16), (192, L0), (80, K0), (10, 8, 128),
            (8, 8, 128), plane1(3, 8), plane1(10), plane1(10), plane1(3, 4), (128, 128), (16, 128),
        ],
        own, left, right,
    )
    right = ring(to_left, "gx", gx, -1)
    left = ring(to_right, "gx", gx, 1)
    got = lax.all_to_all(pay, ("gx", "gy"), 0, 0)
    nx2, nx3, y2, l3 = 2 * gx, gx, 32 * gy, max(128, 16 * gy)
    plane2 = lambda *lead: (*lead, 8, y2)
    plane3 = lambda *lead: (*lead, 8, l3)
    (out,) = call(
        functools.partial(up_kernel, gx, gy),
        [(VEC * COMP * NZ * BX, BY)],
        [
            plane2(nx2 + 2), plane2(3, nx2), plane2(13, nx2), plane2(nx2), plane2(3, nx2), plane2(3, nx2 + 4), plane2(3, nx2 + 4),
            plane2(3, nx2), plane2(nx2 + 2), plane2(nx2 + 2), (32 * nx3, y2),
            plane3(nx3 + 2), plane3(13, nx3), plane3(3, nx3), plane3(3, nx3 + 2), plane3(3, nx3 + 2), plane3(nx3 + 2), plane3(nx3 + 2),
            (24 * nx3, l3), (288, y2), plane1(3, 10), plane1(3, 10), plane1(10), plane1(10), (4, 144, 128),
            plane(3, 12), plane(3, 12), plane(12), plane(12),
        ],
        got, left, right, *kept,
    )
    return out.reshape(right_side.shape)


def solution(mesh):
    gx, gy = mesh.shape["gx"], mesh.shape["gy"]
    spec = P(None, None, None, "gx", "gy")
    return jax.shard_map(
        functools.partial(per_device, gx, gy), mesh=mesh, in_specs=(spec, P(None, "gx", "gy")), out_specs=spec, check_vma=False
    )
```

```python
import functools

import jax
import jax.numpy as jnp
from jax import lax
from jax.experimental import pallas as pl
from jax.experimental.pallas import tpu as pltpu
from jax.sharding import PartitionSpec as P

RELAX = 0.6
MASS = 0.01
GRAD_DIV = 2.5
VEC, COMP, NZ, BX, BY = 4, 3, 8, 8, 128
COARSE = 6
UNROLL0, UNROLL1, UNROLL2 = 4, 4, 16
RIM = 16
LEFT = 11
PIECE = 108
SPLIT = 112
L0 = 5 * 128
K0 = 2 * 128
L1 = 2 * 128
FX = 6
CX = 7
F32 = jnp.float32


def iota(shape, dim):
    return lax.broadcasted_iota(jnp.int32, shape, dim)


def parts_of(value):
    high = value.astype(jnp.bfloat16)
    rest = value - high.astype(F32)
    mid = rest.astype(jnp.bfloat16)
    return high, mid, (rest - mid.astype(F32)).astype(jnp.bfloat16)


def exact_dot(parts, selector):
    out = [jnp.dot(p, selector, preferred_element_type=F32) for p in parts]
    return out[0] + out[1] + out[2]


class Level:
    def __init__(self, index, rows, width, kinds, length=None):
        self.scale = 0.25**index
        self.rows = rows
        self.width = width
        self.kinds = kinds
        row = iota((8, width), 0)
        self.has_zp, self.has_zm = row < 8 - rows, row >= rows
        self.has_yp = self.has_ym = None
        if length is not None:
            lane = iota((8, width), 1)
            self.has_yp, self.has_ym = lane < length - 1, lane > 0

    def lanes(self, tile):
        return pl.ds(tile * self.width, self.width)

    def yp(self, a):
        return pltpu.roll(a, self.width - 1, 1)

    def ym(self, a):
        return pltpu.roll(a, 1, 1)

    def zp(self, a):
        return pltpu.roll(a, 8 - self.rows, 0)

    def zm(self, a):
        return pltpu.roll(a, self.rows, 0)

    @staticmethod
    def keep(mask, a):
        return a if mask is None else jnp.where(mask, a, 0.0)

    def dy_of(self, up, down):
        return self.keep(self.has_yp, up) - self.keep(self.has_ym, down)

    def dz_of(self, up, down):
        return self.keep(self.has_zp, up) - self.keep(self.has_zm, down)

    @property
    def layered(self):
        return self.rows < 8

    def weights(self, coeff, at, k_ref, kat):
        gains, backs = [], []
        for kind in range(max(self.kinds) + 1):
            lanes = self.lanes(kind)
            c = coeff[at, :, lanes]
            near = [coeff[at + 1, :, lanes], coeff[at - 1, :, lanes]]
            near += [self.keep(self.has_yp, self.yp(c)), self.keep(self.has_ym, self.ym(c))]
            if self.layered:
                near += [self.keep(self.has_zp, self.zp(c)), self.keep(self.has_zm, self.zm(c))]
            total = near[0]
            for n in near[1:]:
                total = total + n
            diag = MASS + self.scale * (8.0 * c + 0.5 * total)
            gain = jnp.where(c > 0.0, RELAX / diag, 0.0)
            half = (0.5 * self.scale) * gain
            own = (GRAD_DIV * self.scale) * gain * c
            masks = [None, None, self.has_yp, self.has_ym, self.has_zp, self.has_zm]
            for i, n in enumerate(near):
                face = half * (c + n)
                k_ref[i, kat, :, lanes] = self.keep(masks[i], face)
                k_ref[6 + i, kat, :, lanes] = self.keep(masks[i], face + own)
            k_ref[12, kat, :, lanes] = 0.25 * own
            gains.append(gain)
            backs.append(diag * (1.0 / RELAX))
        return gains, backs

    def cross(self, u, at, t_ref, tat):
        for tile in range(len(self.kinds)):
            lanes = self.lanes(tile)
            uy = u[1, at, :, lanes]
            t = self.dy_of(self.yp(uy), self.ym(uy))
            if self.layered:
                uz = u[2, at, :, lanes]
                t = t + self.dz_of(self.zp(uz), self.zm(uz))
            t_ref[tat, :, lanes] = t

    def change(self, u, at, t_ref, px_ref, tat, k_ref, kat, x1, xat, write):
        for tile, kind in enumerate(self.kinds):
            lanes = self.lanes(tile)
            k = lambda i: k_ref[i, kat, :, self.lanes(kind)]
            mine = [u[c, at, :, lanes] for c in range(3)]
            fore = [u[c, at + 1, :, lanes] for c in range(3)]
            back = [u[c, at - 1, :, lanes] for c in range(3)]
            y_up = [self.yp(a) for a in mine]
            y_dn = [self.ym(a) for a in mine]
            dxx = fore[0] - back[0]
            dyy = self.dy_of(y_up[1], y_dn[1])
            side = dxx
            cross = dyy
            if self.layered:
                z_up = [self.zp(a) for a in mine]
                z_dn = [self.zm(a) for a in mine]
                dzz = self.dz_of(z_up[2], z_dn[2])
                side = dxx + dzz
                cross = dyy + dzz
            t_ref[tat, :, lanes] = cross
            mixed = [None, self.dy_of(self.yp(side), self.ym(side)), None]
            if self.layered:
                below = dxx + dyy
                mixed[2] = self.dz_of(self.zp(below), self.zm(below))
            for c in range(3):
                total = x1[c, xat, :, lanes] - RELAX * mine[c]
                total = total + (k(6 if c == 0 else 0) * fore[c] + k(7 if c == 0 else 1) * back[c])
                sides = k(8 if c == 1 else 2) * y_up[c] + k(9 if c == 1 else 3) * y_dn[c]
                if self.layered:
                    sides = sides + (k(10 if c == 2 else 4) * z_up[c] + k(11 if c == 2 else 5) * z_dn[c])
                if mixed[c] is not None:
                    sides = sides + k(12) * mixed[c]
                if c == 0:
                    px_ref[tat, :, lanes] = total + sides
                else:
                    write(c, tile, lanes, total + sides)

    def apply(self, u, uo, t_ref, px_ref, k_ref, ko, x1, xo, low, high, unroll, write):
        self.cross(u, low - 1 + uo, t_ref, 0)
        self.cross(u, high + uo, t_ref, high - low + 1)

        def one(p):
            def put(c, tile, lanes, d):
                write(c, p, tile, lanes, d)

            self.change(u, p + uo, t_ref, px_ref, p - low + 1, k_ref, p + ko, x1, p + xo, put)

        def mixed(p):
            at = p - low + 1
            for tile, kind in enumerate(self.kinds):
                lanes = self.lanes(tile)
                t = t_ref[at + 1, :, lanes] - t_ref[at - 1, :, lanes]
                write(0, p, tile, lanes, px_ref[at, :, lanes] + k_ref[12, p + ko, :, self.lanes(kind)] * t)

        each(low, high, unroll, one)
        each(low, high, 2 * unroll, mixed)


def each(low, high, unroll, body):
    count = high - low
    while count % unroll:
        unroll -= 1
    if count == unroll:
        for p in range(low, high):
            body(p)
        return

    def step(i, carry):
        for b in range(unroll):
            body(low + i * unroll + b)
        return carry

    lax.fori_loop(0, count // unroll, step, 0)


def tile_y(lane):
    return (lane & 127) - LEFT, PIECE + (lane & 31), (lane & 127) >> 5


def bf16(mask, value):
    return jnp.where(mask, value, 0.0).astype(jnp.bfloat16)


def rows_of(ref, group, x):
    return ref[pl.ds(group * 64 + x, 8, stride=8), :]


def coeff_rows(m_ref, x):
    return jnp.where(rows_of(m_ref, 0, x) == 1, 1.0, 0.05).astype(F32)


def edge_kernel(f_hbm, m_hbm, left_ref, right_ref, f_ref, m_ref, sems):
    copies = [pltpu.make_async_copy(m_hbm, m_ref, sems.at[0]), pltpu.make_async_copy(f_hbm, f_ref, sems.at[1])]
    for copy in copies:
        copy.start()
    for copy in copies:
        copy.wait()
    for x in range(BX):
        for v in range(VEC):
            for c in range(COMP):
                val = rows_of(f_ref, v * COMP + c, x)
                lanes = pl.ds((x // 4) * 64 + 16 * v, 16)
                left_ref[c * 4 + x % 4, :, lanes] = val[:, :RIM]
                right_ref[c * 4 + x % 4, :, lanes] = val[:, BY - RIM :]
        val = coeff_rows(m_ref, x)
        left_ref[12, :, pl.ds(16 * x, 16)] = val[:, :RIM]
        right_ref[12, :, pl.ds(16 * x, 16)] = val[:, BY - RIM :]


def join_kernel(gy, f_ref, m_ref, l_ref, r_ref, own_ref, left_ref, right_ref):
    place = lax.axis_index("gy")
    from_left = (place > 0).astype(F32)
    from_right = (place < gy - 1).astype(F32)
    kept = BY - PIECE

    def put(ref, at, start, piece_at, piece_start, val, left, right):
        ref[*at, :, pl.ds(start, LEFT)] = left[:, RIM - LEFT :]
        ref[*at, :, pl.ds(start + LEFT, 128 - LEFT)] = val[:, : 128 - LEFT]
        ref[*piece_at, :, pl.ds(piece_start, kept)] = val[:, PIECE:]
        ref[*piece_at, :, pl.ds(piece_start + kept, 32 - kept)] = right[:, : 32 - kept]

    for x in range(BX):
        for c in range(COMP):
            left = l_ref[c * 4 + x % 4] * from_left
            right = r_ref[c * 4 + x % 4] * from_right
            for v in range(VEC):
                at = (x // 4) * 64 + 16 * v
                val = rows_of(f_ref, v * COMP + c, x)
                place = (BX * c + x,)
                put(own_ref, place, 128 * v, place, 512 + 32 * v, val, left[:, at : at + RIM], right[:, at : at + RIM])
        left = l_ref[12, :, pl.ds(16 * x, 16)] * from_left
        right = r_ref[12, :, pl.ds(16 * x, 16)] * from_right
        base = COMP * BX
        at, piece = x, 8 + x // 4
        put(
            own_ref, (base + at // 5,), 128 * (at % 5), (base + piece // 5,), 128 * (piece % 5) + 32 * (x % 4),
            coeff_rows(m_ref, x), left, right,
        )
    for c in range(COMP):
        for x in range(FX):
            left_ref[c * FX + x] = own_ref[BX * c + x]
            right_ref[c * FX + x] = own_ref[BX * c + x + BX - FX]
    for i in range(2):
        left_ref[COMP * FX + i] = own_ref[COMP * BX + i]
        right_ref[COMP * FX + i] = own_ref[COMP * BX + i]


def down_kernel(
    gx, own_ref, l_ref, r_ref,
    pay_ref, send_l, send_r, x1_ref, x2_ref, c0_ref, y1, y2_ref, k1,
    x1, x2, k0, y2, cx, dr0, t0, p0, rest, stack, cstack, c1, dr1, f1, t1, p1, r1, stack1, pay,
):
    place = lax.axis_index("gx")
    from_left = (place > 0).astype(F32)
    from_right = (place < gx - 1).astype(F32)
    a = Level(0, 1, 128, (0, 0, 0, 0, 1))

    def spread(plane, ref, base, x, factor):
        at, piece = x, 8 + x // 4
        val = ref[base + at // 5, :, pl.ds(128 * (at % 5), 128)]
        end = ref[base + piece // 5, :, pl.ds(128 * (piece % 5) + 32 * (x % 4), 32)]
        if factor is not None:
            val, end = val * factor, end * factor
        cx[plane + CX, :, pl.ds(0, 128)] = val
        for v in range(VEC):
            cx[plane + CX, :, pl.ds(128 + 32 * v, 32)] = end

    for x in range(BX):
        spread(x, own_ref, COMP * BX, x, None)
    for x in range(CX):
        spread(x - CX, l_ref, COMP * FX, x + BX - CX, from_left)
        spread(x + BX, r_ref, COMP * FX, x, from_right)

    def start(low, high, load):
        def body(p):
            gain, back = a.weights(cx, p + CX, k0, p + FX)
            for kind in range(2):
                dr0[p + FX, :, a.lanes(kind)] = back[kind]
            for c in range(COMP):
                plane = load(c, p)
                for tile, kind in enumerate(a.kinds):
                    x1[c, p + FX, :, a.lanes(tile)] = gain[kind] * plane[:, 128 * tile : 128 * tile + 128]

        each(low, high, 2, body)

    start(-FX, 0, lambda c, p: l_ref[c * FX + p + FX])
    start(0, BX, lambda c, p: own_ref[BX * c + p])
    start(BX, BX + FX, lambda c, p: r_ref[c * FX + p - BX])

    def to_x2(c, p, tile, lanes, d):
        x2[c, p + FX, :, lanes] = x1[c, p + FX, :, lanes] + d

    a.apply(x1, FX, t0, p0, k0, FX, x1, FX, 1 - FX, BX + FX - 1, UNROLL0, to_x2)

    def to_rest(c, p, tile, lanes, d):
        rest[c, p + 4, :, lanes] = d * dr0[p + FX, :, a.lanes(a.kinds[tile])]

    a.apply(x2, FX, t0, p0, k0, FX, x1, FX, -4, BX + 4, UNROLL0, to_rest)

    for c in range(COMP):
        for i in range(8):
            plane = rest[c, 2 * i] + rest[c, 2 * i + 1]
            stack[pl.ds(64 * c + 8 * i, 8), :] = plane + a.zp(plane)
    for i in range(10):
        plane = cx[2 * i + 1] + cx[2 * i + 2]
        cstack[pl.ds(8 * i, 8), :] = plane + a.zp(plane)
    selectors = []
    row, col = iota((K0, 128), 0), iota((K0, 128), 1)
    y, y_piece, vec = tile_y(row)
    for v in range(VEC):
        own_tile = (row < 128) & (y >= -10) & (y < SPLIT) & ((y >> 1) + 32 == col)
        piece = (row >= 128) & (vec == v) & (y_piece >= SPLIT) & (y_piece < BY + 10) & ((y_piece >> 1) + 32 == col)
        selectors.append(bf16(own_tile | piece, 0.125))
    parts = parts_of(stack[...])
    coarse = [
        exact_dot([jnp.concatenate([p[:, 128 * v : 128 * v + 128], p[:, 512:]], axis=1) for p in parts], selectors[v])
        for v in range(VEC)
    ]
    coarse_c = exact_dot(parts_of(cstack[...]), selectors[0])
    even = (iota((8, 128), 0) & 1) == 0
    for c in range(COMP):
        for i in range(8):
            at = 64 * c + 8 * i
            for low in range(2):
                odd = pltpu.roll(coarse[2 + low][at : at + 8], 1, 0)
                f1[c, i, :, pl.ds(128 * low, 128)] = jnp.where(even, coarse[low][at : at + 8], odd)
    for i in range(10):
        block = coarse_c[8 * i : 8 * i + 8]
        c1[i] = jnp.where(even, block, pltpu.roll(block, 1, 0))

    b = Level(1, 2, 128, (0, 0))
    for p in range(-2, 6):
        gain, back = b.weights(c1, p + 3, k1, p + 2)
        dr1[p + 2] = back[0]
        for c in range(COMP):
            for tile in range(2):
                y1[c, p + 2, :, b.lanes(tile)] = gain[0] * f1[c, p + 2, :, b.lanes(tile)]

    def to_y2(c, p, tile, lanes, d):
        y2[c, p + 1, :, lanes] = y1[c, p + 2, :, lanes] + d

    b.apply(y1, 2, t1, p1, k1, 2, y1, 2, -1, 5, UNROLL1, to_y2)
    for c in range(COMP):
        for i in range(3):
            send_l[3 * c + i] = y2[c, 1 + i]
            send_r[3 * c + i] = y2[c, 2 + i]

    def to_r1(c, p, tile, lanes, d):
        r1[c, p, :, lanes] = d * dr1[p + 2]

    b.apply(y2, 1, t1, p1, k1, 2, y1, 2, 0, 4, UNROLL1, to_r1)

    for c in range(COMP):
        for i in range(2):
            plane = r1[c, 2 * i] + r1[c, 2 * i + 1]
            plane = plane + pltpu.roll(plane, 6, 0)
            stack1[pl.ds(8 * (2 * c + i), 8), :] = plane[:, :128]
            stack1[pl.ds(64 + 8 * (2 * c + i), 8), :] = plane[:, 128:]
    for i in range(2):
        plane = c1[2 * i + 3] + c1[2 * i + 4]
        plane = plane + b.zp(plane)
        stack1[pl.ds(8 * (6 + i), 8), :] = plane
        stack1[pl.ds(64 + 8 * (6 + i), 8), :] = plane
    lane = iota((128, 128), 0) - 32
    selector1 = bf16((lane >> 1 == iota((128, 128), 1)) & (lane >= 0) & (lane < 64), 0.125)
    coarse1 = exact_dot(parts_of(stack1[...]), selector1)
    first = (iota((8, 32), 0) & 2) == 0
    for g in range(8):
        low = coarse1[8 * g : 8 * g + 8]
        high = pltpu.roll(coarse1[64 + 8 * g : 72 + 8 * g], 2, 0)
        pay[pl.ds(8 * (g // 4), 8), pl.ds(32 * (g % 4), 32)] = jnp.where(first, low[:, :32], high[:, :32])
    packed = pay[...]

    def copy(i):
        pay_ref[i] = packed

    each(0, pay_ref.shape[0], 8, copy)
    for c in range(COMP):
        for i in range(10):
            x1_ref[c, i] = x1[c, i + 5]
        for i in range(12):
            x2_ref[c, i] = x2[c, i + 4]
        for i in range(4):
            y2_ref[c, i] = y2[c, i + 1]
    for i in range(12):
        c0_ref[i] = cx[i + 5]


def up_kernel(
    gx, gy, got_ref, l_ref, r_ref, x1, x2, c0_ref, y1, y2, k1, out_ref,
    c2, f2, k2, dr2, x1c, ua, ub, rc, t2, p2, s2, c3, k3, x1d, va, vb, t3, p3, s3, sw, w0, w1, t1, p1, sp, k0, u0, u1, t0, p0,
):
    nx2, nx3 = 2 * gx, gx
    yy2, l3 = 32 * gy, c3.shape[-1]
    place_x = lax.axis_index("gx")
    place_y = lax.axis_index("gy")
    from_left = (place_x > 0).astype(F32)
    from_right = (place_x < gx - 1).astype(F32)

    zero2 = jnp.zeros((8, yy2), F32)
    for ref in (ua, ub):
        for c in range(COMP):
            for i in (0, 1, nx2 + 2, nx2 + 3):
                ref[c, i] = zero2
    c2[0] = zero2
    c2[nx2 + 1] = zero2

    def unpack(i):
        for j in range(gy):
            for g in range(8):
                block = got_ref[i * gy + j, pl.ds(8 * (g // 4), 8), pl.ds(32 * (g % 4), 32)]
                if g < 6:
                    f2[g // 2, 2 * i + g % 2, :, pl.ds(32 * j, 32)] = block
                else:
                    c2[2 * i + g - 5, :, pl.ds(32 * j, 32)] = block

    each(0, gx, 8, unpack)
    m = Level(2, 4, yy2, (0,), yy2)

    def start2(p):
        gain, back = m.weights(c2, p + 1, k2, p)
        dr2[p] = back[0]
        for c in range(COMP):
            val = gain[0] * f2[c, p]
            x1c[c, p] = val
            ua[c, p + 2] = val

    each(0, nx2, 8, start2)

    def sweep2(src, dst):
        def write(c, p, tile, lanes, d):
            dst[c, p + 2] = src[c, p + 2] + d

        m.apply(src, 2, t2, p2, k2, 0, x1c, 0, 0, nx2, UNROLL2, write)

    sweep2(ua, ub)

    def to_rc(c, p, tile, lanes, d):
        rc[c, p] = d * dr2[p]

    m.apply(ub, 2, t2, p2, k2, 0, x1c, 0, 0, nx2, UNROLL2, to_rc)

    for i in range(nx3):
        for c in range(COMP):
            plane = rc[c, 2 * i] + rc[c, 2 * i + 1]
            s2[pl.ds(8 * (c * nx3 + i), 8), :] = plane + pltpu.roll(plane, 4, 0)
        plane = c2[2 * i + 1] + c2[2 * i + 2]
        s2[pl.ds(8 * (COMP * nx3 + i), 8), :] = plane + pltpu.roll(plane, 4, 0)
    selector = bf16((iota((yy2, l3), 0) >> 1) == iota((yy2, l3), 1), 0.125)
    coarse = exact_dot(parts_of(s2[...]), selector)
    zero3 = jnp.zeros((8, l3), F32)
    for ref in (va, vb):
        for c in range(COMP):
            ref[c, 0] = zero3
            ref[c, nx3 + 1] = zero3
    c3[0] = zero3
    c3[nx3 + 1] = zero3
    for i in range(nx3):
        c3[i + 1] = coarse[8 * (COMP * nx3 + i) : 8 * (COMP * nx3 + i) + 8]
    n = Level(3, 8, l3, (0,), 16 * gy)
    for p in range(nx3):
        gain, _ = n.weights(c3, p + 1, k3, p)
        for c in range(COMP):
            val = gain[0] * coarse[8 * (c * nx3 + p) : 8 * (c * nx3 + p) + 8]
            x1d[c, p] = val
            va[c, p + 1] = val
    src, dst = va, vb
    for _ in range(COARSE - 1):

        def write3(c, p, tile, lanes, d, src=src, dst=dst):
            dst[c, p + 1] = src[c, p + 1] + d

        n.apply(src, 1, t3, p3, k3, 0, x1d, 0, 0, nx3, UNROLL2, write3)
        src, dst = dst, src
    for c in range(COMP):
        for i in range(nx3):
            s3[pl.ds(8 * (c * nx3 + i), 8), :] = src[c, i + 1]
    selector = bf16((iota((l3, yy2), 1) >> 1) == iota((l3, yy2), 0), 1.0)
    fine = exact_dot(parts_of(s3[...]), selector)
    for c in range(COMP):
        for i in range(nx3):
            block = fine[8 * (c * nx3 + i) : 8 * (c * nx3 + i) + 8]
            for j in range(2):
                ub[c, 2 * i + j + 2] = ub[c, 2 * i + j + 2] + block
    sweep2(ub, ua)
    sweep2(ua, ub)

    row = iota((8, yy2), 0)
    for c in range(COMP):
        for i in range(6):
            e = ub[c, 2 * place_x + i]
            at = 16 * (6 * c + i)
            sw[pl.ds(at, 8), :] = jnp.where((row & 2) == 0, e, pltpu.roll(e, 2, 0))
            sw[pl.ds(at + 8, 8), :] = jnp.where((row & 2) != 0, e, pltpu.roll(e, 6, 0))
    y1g = place_y * 64 + iota((yy2, 128), 1) - 32
    fine = exact_dot(parts_of(sw[...]), bf16((y1g >> 1) == iota((yy2, 128), 0), 1.0))
    for c in range(COMP):
        for p in range(-3, 7):
            if p < 0:
                val = l_ref[3 * c + p + 3] * from_left
            elif p < 4:
                val = y2[c, p]
            else:
                val = r_ref[3 * c + p - 4] * from_right
            at = 16 * (6 * c + (p + 4) // 2)
            w0[c, p + 3] = val + jnp.concatenate([fine[at : at + 8], fine[at + 8 : at + 16]], axis=1)
    b = Level(1, 2, 128, (0, 0))

    def write1(c, p, tile, lanes, d):
        w1[c, p + 3, :, lanes] = w0[c, p + 3, :, lanes] + d

    b.apply(w0, 3, t1, p1, k1, 2, y1, 2, -2, 6, UNROLL1, write1)
    odd = (iota((8, 128), 0) & 1) != 0

    def write1b(c, p, tile, lanes, d):
        e = w1[c, p + 3, :, lanes] + d
        rows = pl.ds(8 * (6 * c + p + 1), 8)
        sp[tile, rows, :] = jnp.where(odd, pltpu.roll(e, 1, 0), e)
        sp[2 + tile, rows, :] = jnp.where(odd, e, pltpu.roll(e, 7, 0))

    b.apply(w1, 3, t1, p1, k1, 2, y1, 2, -1, 5, 6, write1b)

    col = iota((128, K0), 1)
    y, y_piece, vec = tile_y(col)
    piece = None
    for v in range(VEC):
        parent = jnp.where(col < 128, y >> 1, y_piece >> 1) + 32
        selector = bf16((parent == iota((128, K0), 0)) & ((col < 128) | (vec == v)), 1.0)
        fine = exact_dot(parts_of(sp[v]), selector)
        piece = fine[:, 128:] if v == 0 else piece + fine[:, 128:]
        for c in range(COMP):
            for i in range(6):
                at = 8 * (6 * c + i)
                for j in range(2):
                    u0[c, 2 * i + j, :, pl.ds(128 * v, 128)] = x2[c, 2 * i + j, :, pl.ds(128 * v, 128)] + fine[at : at + 8, :128]
    for c in range(COMP):
        for i in range(6):
            at = 8 * (6 * c + i)
            for j in range(2):
                u0[c, 2 * i + j, :, pl.ds(512, 128)] = x2[c, 2 * i + j, :, pl.ds(512, 128)] + piece[at : at + 8]
    a = Level(0, 1, 128, (0, 0, 0, 0, 1))

    def write0(c, p, tile, lanes, d):
        u1[c, p + 2, :, lanes] = u0[c, p + 2, :, lanes] + d

    each(-1, 9, 2, lambda p: a.weights(c0_ref, p + 2, k0, p + 1))
    a.apply(u0, 2, t0, p0, k0, 1, x1, 1, -1, 9, UNROLL0, write0)

    def write_last(c, p, tile, lanes, d):
        u0[c, p + 2, :, lanes] = u1[c, p + 2, :, lanes] + d

    a.apply(u1, 2, t0, p0, k0, 1, x1, 1, 0, BX, UNROLL0, write_last)
    near = iota((8, 128), 1) < SPLIT
    for x in range(BX):
        for c in range(COMP):
            last = u0[c, x + 2, :, pl.ds(512, 128)]
            for v in range(VEC):
                main = pltpu.roll(u0[c, x + 2, :, pl.ds(128 * v, 128)], 128 - LEFT, 1)
                ends = pltpu.roll(last, (PIECE - 32 * v) % 128, 1)
                out_ref[pl.ds((v * COMP + c) * 64 + x, 8, stride=8), :] = jnp.where(near, main, ends)


def call(kernel, outs, scratch, *args):
    vmem = pl.BlockSpec(memory_space=pltpu.VMEM)
    shapes = [jax.ShapeDtypeStruct(s, F32) for s in outs]
    return pl.pallas_call(
        kernel,
        out_shape=shapes,
        in_specs=[vmem] * len(args),
        out_specs=[vmem] * len(outs),
        scratch_shapes=[pltpu.VMEM(s, F32) for s in scratch],
        compiler_params=pltpu.CompilerParams(vmem_limit_bytes=48 * 1024 * 1024),
    )(*args)


def per_device(gx, gy, right_side, material):
    def ring(value, axis, size, step):
        return lax.ppermute(value, axis, [(i, (i + step) % size) for i in range(size)])

    f = right_side.reshape(VEC * COMP * NZ * BX, BY)
    m = material.reshape(NZ * BX, BY)
    edge = (13, 8, 128)
    hbm, vmem = pl.BlockSpec(memory_space=pltpu.HBM), pl.BlockSpec(memory_space=pltpu.VMEM)
    to_left, to_right = pl.pallas_call(
        edge_kernel,
        out_shape=[jax.ShapeDtypeStruct(s, F32) for s in (edge, edge)],
        in_specs=[hbm] * 2,
        out_specs=[vmem] * 2,
        scratch_shapes=[pltpu.VMEM(f.shape, F32), pltpu.VMEM(m.shape, jnp.int32), pltpu.SemaphoreType.DMA((2,))],
        compiler_params=pltpu.CompilerParams(vmem_limit_bytes=8 * 1024 * 1024),
    )(f, m)
    right = ring(to_left, "gy", gy, -1)
    left = ring(to_right, "gy", gy, 1)
    side = (COMP * FX + 2, 8, L0)
    own, to_left, to_right = call(
        functools.partial(join_kernel, gy), [(COMP * BX + 2, 8, L0), side, side], [], f, m, left, right
    )
    right = ring(to_left, "gx", gx, -1)
    left = ring(to_right, "gx", gx, 1)
    n = gx * gy
    plane = lambda *lead: (*lead, 8, L0)
    plane1 = lambda *lead: (*lead, 8, L1)
    nf, nc = BX + 2 * FX, BX + 2 * CX
    pay, to_left, to_right, *kept = call(
        functools.partial(down_kernel, gx),
        [
            (n, 16, 128), plane1(9), plane1(9), plane(3, 10), plane(3, 12), (12, 8, K0), plane1(3, 8), plane1(3, 4), (13, 8, 8, 128),
        ],
        [
            plane(3, nf), plane(3, nf), (13, nf, 8, K0), plane1(3, 6),
            (nc, 8, K0), (nf, 8, K0), plane(nf), plane(nf), plane(3, 16), (192, L0), (80, K0), (10, 8, 128),
            (8, 8, 128), plane1(3, 8), plane1(10), plane1(10), plane1(3, 4), (128, 128), (16, 128),
        ],
        own, left, right,
    )
    right = ring(to_left, "gx", gx, -1)
    left = ring(to_right, "gx", gx, 1)
    got = lax.all_to_all(pay, ("gx", "gy"), 0, 0)
    nx2, nx3, y2, l3 = 2 * gx, gx, 32 * gy, max(128, 16 * gy)
    plane2 = lambda *lead: (*lead, 8, y2)
    plane3 = lambda *lead: (*lead, 8, l3)
    (out,) = call(
        functools.partial(up_kernel, gx, gy),
        [(VEC * COMP * NZ * BX, BY)],
        [
            plane2(nx2 + 2), plane2(3, nx2), plane2(13, nx2), plane2(nx2), plane2(3, nx2), plane2(3, nx2 + 4), plane2(3, nx2 + 4),
            plane2(3, nx2), plane2(nx2 + 2), plane2(nx2 + 2), (32 * nx3, y2),
            plane3(nx3 + 2), plane3(13, nx3), plane3(3, nx3), plane3(3, nx3 + 2), plane3(3, nx3 + 2), plane3(nx3 + 2), plane3(nx3 + 2),
            (24 * nx3, l3), (288, y2), plane1(3, 10), plane1(3, 10), plane1(10), plane1(10), (4, 144, 128), (13, 10, 8, K0),
            plane(3, 12), plane(3, 12), plane(12), plane(12),
        ],
        got, left, right, *kept,
    )
    return out.reshape(right_side.shape)


def solution(mesh):
    gx, gy = mesh.shape["gx"], mesh.shape["gy"]
    spec = P(None, None, None, "gx", "gy")
    return jax.shard_map(
        functools.partial(per_device, gx, gy), mesh=mesh, in_specs=(spec, P(None, "gx", "gy")), out_specs=spec, check_vma=False
    )
```

```python
import functools

import jax
import jax.numpy as jnp
from jax import lax
from jax.experimental import pallas as pl
from jax.experimental.pallas import tpu as pltpu
from jax.sharding import PartitionSpec as P

RELAX = 0.6
MASS = 0.01
GRAD_DIV = 2.5
VEC, COMP, NZ, BX, BY = 4, 3, 8, 8, 128
COARSE = 6
UNROLL0, UNROLL1, UNROLL2 = 4, 4, 16
RIM = 16
LEFT = 11
PIECE = 108
SPLIT = 112
L0 = 5 * 128
K0 = 2 * 128
L1 = 2 * 128
FX = 6
CX = 7
F32 = jnp.float32


def iota(shape, dim):
    return lax.broadcasted_iota(jnp.int32, shape, dim)


def parts_of(value):
    high = value.astype(jnp.bfloat16)
    rest = value - high.astype(F32)
    mid = rest.astype(jnp.bfloat16)
    return high, mid, (rest - mid.astype(F32)).astype(jnp.bfloat16)


def exact_dot(parts, selector):
    out = [jnp.dot(p, selector, preferred_element_type=F32) for p in parts]
    return out[0] + out[1] + out[2]


class Level:
    def __init__(self, index, rows, width, kinds, length=None):
        self.scale = 0.25**index
        self.rows = rows
        self.width = width
        self.kinds = kinds
        row = iota((8, width), 0)
        self.has_zp, self.has_zm = row < 8 - rows, row >= rows
        self.has_yp = self.has_ym = None
        if length is not None:
            lane = iota((8, width), 1)
            self.has_yp, self.has_ym = lane < length - 1, lane > 0

    def lanes(self, tile):
        return pl.ds(tile * self.width, self.width)

    def yp(self, a):
        return pltpu.roll(a, self.width - 1, 1)

    def ym(self, a):
        return pltpu.roll(a, 1, 1)

    def zp(self, a):
        return pltpu.roll(a, 8 - self.rows, 0)

    def zm(self, a):
        return pltpu.roll(a, self.rows, 0)

    @staticmethod
    def keep(mask, a):
        return a if mask is None else jnp.where(mask, a, 0.0)

    def dy_of(self, up, down):
        return self.keep(self.has_yp, up) - self.keep(self.has_ym, down)

    def dz_of(self, up, down):
        return self.keep(self.has_zp, up) - self.keep(self.has_zm, down)

    @property
    def layered(self):
        return self.rows < 8

    def weights(self, coeff, at, k_ref, kat):
        gains, backs = [], []
        for kind in range(max(self.kinds) + 1):
            lanes = self.lanes(kind)
            c = coeff[at, :, lanes]
            near = [coeff[at + 1, :, lanes], coeff[at - 1, :, lanes]]
            near += [self.keep(self.has_yp, self.yp(c)), self.keep(self.has_ym, self.ym(c))]
            if self.layered:
                near += [self.keep(self.has_zp, self.zp(c)), self.keep(self.has_zm, self.zm(c))]
            total = near[0]
            for n in near[1:]:
                total = total + n
            diag = MASS + self.scale * (8.0 * c + 0.5 * total)
            gain = jnp.where(c > 0.0, RELAX / diag, 0.0)
            half = (0.5 * self.scale) * gain
            own = (GRAD_DIV * self.scale) * gain * c
            masks = [None, None, self.has_yp, self.has_ym, self.has_zp, self.has_zm]
            for i, n in enumerate(near):
                face = half * (c + n)
                k_ref[i, kat, :, lanes] = self.keep(masks[i], face)
                k_ref[6 + i, kat, :, lanes] = self.keep(masks[i], face + own)
            k_ref[12, kat, :, lanes] = 0.25 * own
            gains.append(gain)
            backs.append(diag * (1.0 / RELAX))
        return gains, backs

    def cross(self, u, at, t_ref, tat):
        for tile in range(len(self.kinds)):
            lanes = self.lanes(tile)
            uy = u[1, at, :, lanes]
            t = self.dy_of(self.yp(uy), self.ym(uy))
            if self.layered:
                uz = u[2, at, :, lanes]
                t = t + self.dz_of(self.zp(uz), self.zm(uz))
            t_ref[tat, :, lanes] = t

    def change(self, u, at, t_ref, px_ref, tat, k_ref, kat, x1, xat, write):
        for tile, kind in enumerate(self.kinds):
            lanes = self.lanes(tile)
            k = lambda i: k_ref[i, kat, :, self.lanes(kind)]
            mine = [u[c, at, :, lanes] for c in range(3)]
            fore = [u[c, at + 1, :, lanes] for c in range(3)]
            back = [u[c, at - 1, :, lanes] for c in range(3)]
            y_up = [self.yp(a) for a in mine]
            y_dn = [self.ym(a) for a in mine]
            dxx = fore[0] - back[0]
            dyy = self.dy_of(y_up[1], y_dn[1])
            side = dxx
            cross = dyy
            if self.layered:
                z_up = [self.zp(a) for a in mine]
                z_dn = [self.zm(a) for a in mine]
                dzz = self.dz_of(z_up[2], z_dn[2])
                side = dxx + dzz
                cross = dyy + dzz
            t_ref[tat, :, lanes] = cross
            mixed = [None, self.dy_of(self.yp(side), self.ym(side)), None]
            if self.layered:
                below = dxx + dyy
                mixed[2] = self.dz_of(self.zp(below), self.zm(below))
            for c in range(3):
                total = x1[c, xat, :, lanes] - RELAX * mine[c]
                total = total + (k(6 if c == 0 else 0) * fore[c] + k(7 if c == 0 else 1) * back[c])
                sides = k(8 if c == 1 else 2) * y_up[c] + k(9 if c == 1 else 3) * y_dn[c]
                if self.layered:
                    sides = sides + (k(10 if c == 2 else 4) * z_up[c] + k(11 if c == 2 else 5) * z_dn[c])
                if mixed[c] is not None:
                    sides = sides + k(12) * mixed[c]
                if c == 0:
                    px_ref[tat, :, lanes] = total + sides
                else:
                    write(c, tile, lanes, total + sides)

    def apply(self, u, uo, t_ref, px_ref, k_ref, ko, x1, xo, low, high, unroll, write):
        self.cross(u, low - 1 + uo, t_ref, 0)
        self.cross(u, high + uo, t_ref, high - low + 1)

        def one(p):
            def put(c, tile, lanes, d):
                write(c, p, tile, lanes, d)

            self.change(u, p + uo, t_ref, px_ref, p - low + 1, k_ref, p + ko, x1, p + xo, put)

        def mixed(p):
            at = p - low + 1
            for tile, kind in enumerate(self.kinds):
                lanes = self.lanes(tile)
                t = t_ref[at + 1, :, lanes] - t_ref[at - 1, :, lanes]
                write(0, p, tile, lanes, px_ref[at, :, lanes] + k_ref[12, p + ko, :, self.lanes(kind)] * t)

        each(low, high, unroll, one)
        each(low, high, 2 * unroll, mixed)


def each(low, high, unroll, body):
    count = high - low
    while count % unroll:
        unroll -= 1
    if count == unroll:
        for p in range(low, high):
            body(p)
        return

    def step(i, carry):
        for b in range(unroll):
            body(low + i * unroll + b)
        return carry

    lax.fori_loop(0, count // unroll, step, 0)


def tile_y(lane):
    return (lane & 127) - LEFT, PIECE + (lane & 31), (lane & 127) >> 5


def bf16(mask, value):
    return jnp.where(mask, value, 0.0).astype(jnp.bfloat16)


def rows_of(ref, group, x):
    return ref[pl.ds(group * 64 + x, 8, stride=8), :]


def coeff_rows(m_ref, x):
    return jnp.where(rows_of(m_ref, 0, x) == 1, 1.0, 0.05).astype(F32)


def edge_kernel(f_hbm, m_hbm, left_ref, right_ref, f_ref, m_ref, sems):
    copies = [pltpu.make_async_copy(m_hbm, m_ref, sems.at[0]), pltpu.make_async_copy(f_hbm, f_ref, sems.at[1])]
    for copy in copies:
        copy.start()
    for copy in copies:
        copy.wait()
    for x in range(BX):
        for v in range(VEC):
            for c in range(COMP):
                val = rows_of(f_ref, v * COMP + c, x)
                lanes = pl.ds((x // 4) * 64 + 16 * v, 16)
                left_ref[c * 4 + x % 4, :, lanes] = val[:, :RIM]
                right_ref[c * 4 + x % 4, :, lanes] = val[:, BY - RIM :]
        val = coeff_rows(m_ref, x)
        left_ref[12, :, pl.ds(16 * x, 16)] = val[:, :RIM]
        right_ref[12, :, pl.ds(16 * x, 16)] = val[:, BY - RIM :]


def at_coeff(base, x):
    piece = 8 + x // 4
    return base + x // 5, 128 * (x % 5), base + piece // 5, 128 * (piece % 5) + 32 * (x % 4)


def place_kernel(f_ref, m_ref, own_ref):
    def put(row, lane, piece_row, piece_lane, val):
        own_ref[row, :, pl.ds(lane + LEFT, 128 - LEFT)] = val[:, : 128 - LEFT]
        own_ref[piece_row, :, pl.ds(piece_lane, BY - PIECE)] = val[:, PIECE:]

    for x in range(BX):
        for c in range(COMP):
            for v in range(VEC):
                put(BX * c + x, 128 * v, BX * c + x, 512 + 32 * v, rows_of(f_ref, v * COMP + c, x))
        put(*at_coeff(COMP * BX, x), coeff_rows(m_ref, x))


def join_kernel(gy, placed_ref, l_ref, r_ref, own_ref, left_ref, right_ref):
    place = lax.axis_index("gy")
    from_left = (place > 0).astype(F32)
    from_right = (place < gy - 1).astype(F32)
    kept = BY - PIECE
    for i in range(COMP * BX + 2):
        own_ref[i] = placed_ref[i]

    def put(row, lane, piece_row, piece_lane, left, right):
        own_ref[row, :, pl.ds(lane, LEFT)] = left[:, RIM - LEFT :]
        own_ref[piece_row, :, pl.ds(piece_lane + kept, 32 - kept)] = right[:, : 32 - kept]

    for x in range(BX):
        for c in range(COMP):
            left = l_ref[c * 4 + x % 4] * from_left
            right = r_ref[c * 4 + x % 4] * from_right
            for v in range(VEC):
                at = (x // 4) * 64 + 16 * v
                put(BX * c + x, 128 * v, BX * c + x, 512 + 32 * v, left[:, at : at + RIM], right[:, at : at + RIM])
        left = l_ref[12, :, pl.ds(16 * x, 16)] * from_left
        right = r_ref[12, :, pl.ds(16 * x, 16)] * from_right
        put(*at_coeff(COMP * BX, x), left, right)
    for c in range(COMP):
        for x in range(FX):
            left_ref[c * FX + x] = own_ref[BX * c + x]
            right_ref[c * FX + x] = own_ref[BX * c + x + BX - FX]
    for i in range(2):
        left_ref[COMP * FX + i] = own_ref[COMP * BX + i]
        right_ref[COMP * FX + i] = own_ref[COMP * BX + i]


def down_kernel(
    gx, own_ref, l_ref, r_ref,
    pay_ref, send_l, send_r, x1_ref, x2_ref, c0_ref, y1, y2_ref, k1,
    x1, x2, k0, y2, cx, dr0, t0, p0, rest, stack, cstack, c1, dr1, f1, t1, p1, r1, stack1, pay,
):
    place = lax.axis_index("gx")
    from_left = (place > 0).astype(F32)
    from_right = (place < gx - 1).astype(F32)
    a = Level(0, 1, 128, (0, 0, 0, 0, 1))

    def spread(plane, ref, base, x, factor):
        row, lane, piece_row, piece_lane = at_coeff(base, x)
        val = ref[row, :, pl.ds(lane, 128)]
        end = ref[piece_row, :, pl.ds(piece_lane, 32)]
        if factor is not None:
            val, end = val * factor, end * factor
        cx[plane + CX, :, pl.ds(0, 128)] = val
        for v in range(VEC):
            cx[plane + CX, :, pl.ds(128 + 32 * v, 32)] = end

    for x in range(BX):
        spread(x, own_ref, COMP * BX, x, None)
    for x in range(CX):
        spread(x - CX, l_ref, COMP * FX, x + BX - CX, from_left)
        spread(x + BX, r_ref, COMP * FX, x, from_right)

    def start(low, high, load):
        def body(p):
            gain, back = a.weights(cx, p + CX, k0, p + FX)
            for kind in range(2):
                dr0[p + FX, :, a.lanes(kind)] = back[kind]
            for c in range(COMP):
                plane = load(c, p)
                for tile, kind in enumerate(a.kinds):
                    x1[c, p + FX, :, a.lanes(tile)] = gain[kind] * plane[:, 128 * tile : 128 * tile + 128]

        each(low, high, 4, body)

    start(-FX, 0, lambda c, p: l_ref[c * FX + p + FX])
    start(0, BX, lambda c, p: own_ref[BX * c + p])
    start(BX, BX + FX, lambda c, p: r_ref[c * FX + p - BX])

    def to_x2(c, p, tile, lanes, d):
        x2[c, p + FX, :, lanes] = x1[c, p + FX, :, lanes] + d

    a.apply(x1, FX, t0, p0, k0, FX, x1, FX, 1 - FX, BX + FX - 1, UNROLL0, to_x2)

    def to_rest(c, p, tile, lanes, d):
        rest[c, p + 4, :, lanes] = d * dr0[p + FX, :, a.lanes(a.kinds[tile])]

    a.apply(x2, FX, t0, p0, k0, FX, x1, FX, -4, BX + 4, UNROLL0, to_rest)

    for c in range(COMP):
        for i in range(8):
            plane = rest[c, 2 * i] + rest[c, 2 * i + 1]
            stack[pl.ds(64 * c + 8 * i, 8), :] = plane + a.zp(plane)
    for i in range(10):
        plane = cx[2 * i + 1] + cx[2 * i + 2]
        cstack[pl.ds(8 * i, 8), :] = plane + a.zp(plane)
    selectors = []
    row, col = iota((K0, 128), 0), iota((K0, 128), 1)
    y, y_piece, vec = tile_y(row)
    for v in range(VEC):
        own_tile = (row < 128) & (y >= -10) & (y < SPLIT) & ((y >> 1) + 32 == col)
        piece = (row >= 128) & (vec == v) & (y_piece >= SPLIT) & (y_piece < BY + 10) & ((y_piece >> 1) + 32 == col)
        selectors.append(bf16(own_tile | piece, 0.125))
    parts = parts_of(stack[...])
    coarse = [
        exact_dot([jnp.concatenate([p[:, 128 * v : 128 * v + 128], p[:, 512:]], axis=1) for p in parts], selectors[v])
        for v in range(VEC)
    ]
    coarse_c = exact_dot(parts_of(cstack[...]), selectors[0])
    even = (iota((8, 128), 0) & 1) == 0
    for c in range(COMP):
        for i in range(8):
            at = 64 * c + 8 * i
            for low in range(2):
                odd = pltpu.roll(coarse[2 + low][at : at + 8], 1, 0)
                f1[c, i, :, pl.ds(128 * low, 128)] = jnp.where(even, coarse[low][at : at + 8], odd)
    for i in range(10):
        block = coarse_c[8 * i : 8 * i + 8]
        c1[i] = jnp.where(even, block, pltpu.roll(block, 1, 0))

    b = Level(1, 2, 128, (0, 0))
    for p in range(-2, 6):
        gain, back = b.weights(c1, p + 3, k1, p + 2)
        dr1[p + 2] = back[0]
        for c in range(COMP):
            for tile in range(2):
                y1[c, p + 2, :, b.lanes(tile)] = gain[0] * f1[c, p + 2, :, b.lanes(tile)]

    def to_y2(c, p, tile, lanes, d):
        y2[c, p + 1, :, lanes] = y1[c, p + 2, :, lanes] + d

    b.apply(y1, 2, t1, p1, k1, 2, y1, 2, -1, 5, UNROLL1, to_y2)
    for c in range(COMP):
        for i in range(3):
            send_l[3 * c + i] = y2[c, 1 + i]
            send_r[3 * c + i] = y2[c, 2 + i]

    def to_r1(c, p, tile, lanes, d):
        r1[c, p, :, lanes] = d * dr1[p + 2]

    b.apply(y2, 1, t1, p1, k1, 2, y1, 2, 0, 4, UNROLL1, to_r1)

    for c in range(COMP):
        for i in range(2):
            plane = r1[c, 2 * i] + r1[c, 2 * i + 1]
            plane = plane + pltpu.roll(plane, 6, 0)
            stack1[pl.ds(8 * (2 * c + i), 8), :] = plane[:, :128]
            stack1[pl.ds(64 + 8 * (2 * c + i), 8), :] = plane[:, 128:]
    for i in range(2):
        plane = c1[2 * i + 3] + c1[2 * i + 4]
        plane = plane + b.zp(plane)
        stack1[pl.ds(8 * (6 + i), 8), :] = plane
        stack1[pl.ds(64 + 8 * (6 + i), 8), :] = plane
    lane = iota((128, 128), 0) - 32
    selector1 = bf16((lane >> 1 == iota((128, 128), 1)) & (lane >= 0) & (lane < 64), 0.125)
    coarse1 = exact_dot(parts_of(stack1[...]), selector1)
    first = (iota((8, 32), 0) & 2) == 0
    for g in range(8):
        low = coarse1[8 * g : 8 * g + 8]
        high = pltpu.roll(coarse1[64 + 8 * g : 72 + 8 * g], 2, 0)
        pay[pl.ds(8 * (g // 4), 8), pl.ds(32 * (g % 4), 32)] = jnp.where(first, low[:, :32], high[:, :32])
    packed = pay[...]

    def copy(i):
        pay_ref[i] = packed

    each(0, pay_ref.shape[0], 8, copy)
    for c in range(COMP):
        for i in range(10):
            x1_ref[c, i] = x1[c, i + 5]
        for i in range(12):
            x2_ref[c, i] = x2[c, i + 4]
        for i in range(4):
            y2_ref[c, i] = y2[c, i + 1]
    for i in range(12):
        c0_ref[i] = cx[i + 5]


def up_kernel(
    gx, gy, got_ref, l_ref, r_ref, x1, x2, c0_ref, y1, y2, k1, out_ref,
    c2, f2, k2, dr2, x1c, ua, ub, rc, t2, p2, s2, c3, k3, x1d, va, vb, t3, p3, s3, sw, w0, w1, t1, p1, sp, k0, u0, u1, t0, p0,
):
    nx2, nx3 = 2 * gx, gx
    yy2, l3 = 32 * gy, c3.shape[-1]
    place_x = lax.axis_index("gx")
    place_y = lax.axis_index("gy")
    from_left = (place_x > 0).astype(F32)
    from_right = (place_x < gx - 1).astype(F32)

    zero2 = jnp.zeros((8, yy2), F32)
    for ref in (ua, ub):
        for c in range(COMP):
            for i in (0, 1, nx2 + 2, nx2 + 3):
                ref[c, i] = zero2
    c2[0] = zero2
    c2[nx2 + 1] = zero2

    def unpack(i):
        for j in range(gy):
            for g in range(8):
                block = got_ref[i * gy + j, pl.ds(8 * (g // 4), 8), pl.ds(32 * (g % 4), 32)]
                if g < 6:
                    f2[g // 2, 2 * i + g % 2, :, pl.ds(32 * j, 32)] = block
                else:
                    c2[2 * i + g - 5, :, pl.ds(32 * j, 32)] = block

    each(0, gx, 8, unpack)
    m = Level(2, 4, yy2, (0,), yy2)

    def start2(p):
        gain, back = m.weights(c2, p + 1, k2, p)
        dr2[p] = back[0]
        for c in range(COMP):
            val = gain[0] * f2[c, p]
            x1c[c, p] = val
            ua[c, p + 2] = val

    each(0, nx2, 8, start2)

    def sweep2(src, dst):
        def write(c, p, tile, lanes, d):
            dst[c, p + 2] = src[c, p + 2] + d

        m.apply(src, 2, t2, p2, k2, 0, x1c, 0, 0, nx2, UNROLL2, write)

    sweep2(ua, ub)

    def to_rc(c, p, tile, lanes, d):
        rc[c, p] = d * dr2[p]

    m.apply(ub, 2, t2, p2, k2, 0, x1c, 0, 0, nx2, UNROLL2, to_rc)

    for i in range(nx3):
        for c in range(COMP):
            plane = rc[c, 2 * i] + rc[c, 2 * i + 1]
            s2[pl.ds(8 * (c * nx3 + i), 8), :] = plane + pltpu.roll(plane, 4, 0)
        plane = c2[2 * i + 1] + c2[2 * i + 2]
        s2[pl.ds(8 * (COMP * nx3 + i), 8), :] = plane + pltpu.roll(plane, 4, 0)
    selector = bf16((iota((yy2, l3), 0) >> 1) == iota((yy2, l3), 1), 0.125)
    coarse = exact_dot(parts_of(s2[...]), selector)
    zero3 = jnp.zeros((8, l3), F32)
    for ref in (va, vb):
        for c in range(COMP):
            ref[c, 0] = zero3
            ref[c, nx3 + 1] = zero3
    c3[0] = zero3
    c3[nx3 + 1] = zero3
    for i in range(nx3):
        c3[i + 1] = coarse[8 * (COMP * nx3 + i) : 8 * (COMP * nx3 + i) + 8]
    n = Level(3, 8, l3, (0,), 16 * gy)
    a = Level(0, 1, 128, (0, 0, 0, 0, 1))
    for p in range(nx3):
        gain, _ = n.weights(c3, p + 1, k3, p)
        for c in range(COMP):
            val = gain[0] * coarse[8 * (c * nx3 + p) : 8 * (c * nx3 + p) + 8]
            x1d[c, p] = val
            va[c, p + 1] = val
    src, dst = va, vb
    for sweep in range(COARSE - 1):

        def write3(c, p, tile, lanes, d, src=src, dst=dst):
            dst[c, p + 1] = src[c, p + 1] + d

        n.apply(src, 1, t3, p3, k3, 0, x1d, 0, 0, nx3, UNROLL2, write3)
        for p in (2 * sweep - 1, 2 * sweep):
            a.weights(c0_ref, p + 2, k0, p + 1)
        src, dst = dst, src
    for c in range(COMP):
        for i in range(nx3):
            s3[pl.ds(8 * (c * nx3 + i), 8), :] = src[c, i + 1]
    selector = bf16((iota((l3, yy2), 1) >> 1) == iota((l3, yy2), 0), 1.0)
    fine = exact_dot(parts_of(s3[...]), selector)
    for c in range(COMP):
        for i in range(nx3):
            block = fine[8 * (c * nx3 + i) : 8 * (c * nx3 + i) + 8]
            for j in range(2):
                ub[c, 2 * i + j + 2] = ub[c, 2 * i + j + 2] + block
    sweep2(ub, ua)
    sweep2(ua, ub)

    row = iota((8, yy2), 0)
    for c in range(COMP):
        for i in range(6):
            e = ub[c, 2 * place_x + i]
            at = 16 * (6 * c + i)
            sw[pl.ds(at, 8), :] = jnp.where((row & 2) == 0, e, pltpu.roll(e, 2, 0))
            sw[pl.ds(at + 8, 8), :] = jnp.where((row & 2) != 0, e, pltpu.roll(e, 6, 0))
    y1g = place_y * 64 + iota((yy2, 128), 1) - 32
    fine = exact_dot(parts_of(sw[...]), bf16((y1g >> 1) == iota((yy2, 128), 0), 1.0))
    for c in range(COMP):
        for p in range(-3, 7):
            if p < 0:
                val = l_ref[3 * c + p + 3] * from_left
            elif p < 4:
                val = y2[c, p]
            else:
                val = r_ref[3 * c + p - 4] * from_right
            at = 16 * (6 * c + (p + 4) // 2)
            w0[c, p + 3] = val + jnp.concatenate([fine[at : at + 8], fine[at + 8 : at + 16]], axis=1)
    b = Level(1, 2, 128, (0, 0))

    def write1(c, p, tile, lanes, d):
        w1[c, p + 3, :, lanes] = w0[c, p + 3, :, lanes] + d

    b.apply(w0, 3, t1, p1, k1, 2, y1, 2, -2, 6, UNROLL1, write1)
    odd = (iota((8, 128), 0) & 1) != 0

    def write1b(c, p, tile, lanes, d):
        e = w1[c, p + 3, :, lanes] + d
        rows = pl.ds(8 * (6 * c + p + 1), 8)
        sp[tile, rows, :] = jnp.where(odd, pltpu.roll(e, 1, 0), e)
        sp[2 + tile, rows, :] = jnp.where(odd, e, pltpu.roll(e, 7, 0))

    b.apply(w1, 3, t1, p1, k1, 2, y1, 2, -1, 5, 6, write1b)

    col = iota((128, K0), 1)
    y, y_piece, vec = tile_y(col)
    piece = None
    for v in range(VEC):
        parent = jnp.where(col < 128, y >> 1, y_piece >> 1) + 32
        selector = bf16((parent == iota((128, K0), 0)) & ((col < 128) | (vec == v)), 1.0)
        fine = exact_dot(parts_of(sp[v]), selector)
        piece = fine[:, 128:] if v == 0 else piece + fine[:, 128:]
        for c in range(COMP):
            for i in range(6):
                at = 8 * (6 * c + i)
                for j in range(2):
                    u0[c, 2 * i + j, :, pl.ds(128 * v, 128)] = x2[c, 2 * i + j, :, pl.ds(128 * v, 128)] + fine[at : at + 8, :128]
    for c in range(COMP):
        for i in range(6):
            at = 8 * (6 * c + i)
            for j in range(2):
                u0[c, 2 * i + j, :, pl.ds(512, 128)] = x2[c, 2 * i + j, :, pl.ds(512, 128)] + piece[at : at + 8]

    def write0(c, p, tile, lanes, d):
        u1[c, p + 2, :, lanes] = u0[c, p + 2, :, lanes] + d

    a.apply(u0, 2, t0, p0, k0, 1, x1, 1, -1, 9, UNROLL0, write0)

    def write_last(c, p, tile, lanes, d):
        u0[c, p + 2, :, lanes] = u1[c, p + 2, :, lanes] + d

    a.apply(u1, 2, t0, p0, k0, 1, x1, 1, 0, BX, UNROLL0, write_last)
    near = iota((8, 128), 1) < SPLIT
    for x in range(BX):
        for c in range(COMP):
            last = u0[c, x + 2, :, pl.ds(512, 128)]
            for v in range(VEC):
                main = pltpu.roll(u0[c, x + 2, :, pl.ds(128 * v, 128)], 128 - LEFT, 1)
                ends = pltpu.roll(last, (PIECE - 32 * v) % 128, 1)
                out_ref[pl.ds((v * COMP + c) * 64 + x, 8, stride=8), :] = jnp.where(near, main, ends)


def call(kernel, outs, scratch, *args):
    vmem = pl.BlockSpec(memory_space=pltpu.VMEM)
    shapes = [jax.ShapeDtypeStruct(s, F32) for s in outs]
    return pl.pallas_call(
        kernel,
        out_shape=shapes,
        in_specs=[vmem] * len(args),
        out_specs=[vmem] * len(outs),
        scratch_shapes=[pltpu.VMEM(s, F32) for s in scratch],
        compiler_params=pltpu.CompilerParams(vmem_limit_bytes=48 * 1024 * 1024),
    )(*args)


def per_device(gx, gy, right_side, material):
    def ring(value, axis, size, step):
        return lax.ppermute(value, axis, [(i, (i + step) % size) for i in range(size)])

    f = right_side.reshape(VEC * COMP * NZ * BX, BY)
    m = material.reshape(NZ * BX, BY)
    edge = (13, 8, 128)
    hbm, vmem = pl.BlockSpec(memory_space=pltpu.HBM), pl.BlockSpec(memory_space=pltpu.VMEM)
    to_left, to_right = pl.pallas_call(
        edge_kernel,
        out_shape=[jax.ShapeDtypeStruct(s, F32) for s in (edge, edge)],
        in_specs=[hbm] * 2,
        out_specs=[vmem] * 2,
        scratch_shapes=[pltpu.VMEM(f.shape, F32), pltpu.VMEM(m.shape, jnp.int32), pltpu.SemaphoreType.DMA((2,))],
        compiler_params=pltpu.CompilerParams(vmem_limit_bytes=61 * 1024 * 1024),
    )(f, m)
    right = ring(to_left, "gy", gy, -1)
    left = ring(to_right, "gy", gy, 1)
    side = (COMP * FX + 2, 8, L0)
    whole = (COMP * BX + 2, 8, L0)
    (own,) = call(place_kernel, [whole], [], f, m)
    own, to_left, to_right = call(functools.partial(join_kernel, gy), [whole, side, side], [], own, left, right)
    right = ring(to_left, "gx", gx, -1)
    left = ring(to_right, "gx", gx, 1)
    n = gx * gy
    plane = lambda *lead: (*lead, 8, L0)
    plane1 = lambda *lead: (*lead, 8, L1)
    nf, nc = BX + 2 * FX, BX + 2 * CX
    pay, to_left, to_right, *kept = call(
        functools.partial(down_kernel, gx),
        [
            (n, 16, 128), plane1(9), plane1(9), plane(3, 10), plane(3, 12), (12, 8, K0), plane1(3, 8), plane1(3, 4), (13, 8, 8, 128),
        ],
        [
            plane(3, nf), plane(3, nf), (13, nf, 8, K0), plane1(3, 6),
            (nc, 8, K0), (nf, 8, K0), plane(nf), plane(nf), plane(3, 16), (192, L0), (80, K0), (10, 8, 128),
            (8, 8, 128), plane1(3, 8), plane1(10), plane1(10), plane1(3, 4), (128, 128), (16, 128),
        ],
        own, left, right,
    )
    right = ring(to_left, "gx", gx, -1)
    left = ring(to_right, "gx", gx, 1)
    got = lax.all_to_all(pay, ("gx", "gy"), 0, 0)
    nx2, nx3, y2, l3 = 2 * gx, gx, 32 * gy, max(128, 16 * gy)
    plane2 = lambda *lead: (*lead, 8, y2)
    plane3 = lambda *lead: (*lead, 8, l3)
    (out,) = call(
        functools.partial(up_kernel, gx, gy),
        [(VEC * COMP * NZ * BX, BY)],
        [
            plane2(nx2 + 2), plane2(3, nx2), plane2(13, nx2), plane2(nx2), plane2(3, nx2), plane2(3, nx2 + 4), plane2(3, nx2 + 4),
            plane2(3, nx2), plane2(nx2 + 2), plane2(nx2 + 2), (32 * nx3, y2),
            plane3(nx3 + 2), plane3(13, nx3), plane3(3, nx3), plane3(3, nx3 + 2), plane3(3, nx3 + 2), plane3(nx3 + 2), plane3(nx3 + 2),
            (24 * nx3, l3), (288, y2), plane1(3, 10), plane1(3, 10), plane1(10), plane1(10), (4, 144, 128), (13, 10, 8, K0),
            plane(3, 12), plane(3, 12), plane(12), plane(12),
        ],
        got, left, right, *kept,
    )
    return out.reshape(right_side.shape)


def solution(mesh):
    gx, gy = mesh.shape["gx"], mesh.shape["gy"]
    spec = P(None, None, None, "gx", "gy")
    return jax.shard_map(
        functools.partial(per_device, gx, gy), mesh=mesh, in_specs=(spec, P(None, "gx", "gy")), out_specs=spec, check_vma=False
    )
```

```python
import functools

import jax
import jax.numpy as jnp
from jax import lax
from jax.experimental import pallas as pl
from jax.experimental.pallas import tpu as pltpu
from jax.sharding import PartitionSpec as P

RELAX = 0.6
MASS = 0.01
GRAD_DIV = 2.5
VEC, COMP, NZ, BX, BY = 4, 3, 8, 8, 128
COARSE = 6
UNROLL0, UNROLL1, UNROLL2 = 20, 8, 16
RIM = 16
LEFT = 11
PIECE = 108
SPLIT = 112
L0 = 5 * 128
K0 = 2 * 128
L1 = 2 * 128
FX = 6
CX = 7
F32 = jnp.float32


def iota(shape, dim):
    return lax.broadcasted_iota(jnp.int32, shape, dim)


def parts_of(value):
    high = value.astype(jnp.bfloat16)
    rest = value - high.astype(F32)
    mid = rest.astype(jnp.bfloat16)
    return high, mid, (rest - mid.astype(F32)).astype(jnp.bfloat16)


def exact_dot(parts, selector):
    out = [jnp.dot(p, selector, preferred_element_type=F32) for p in parts]
    return out[0] + out[1] + out[2]


class Level:
    def __init__(self, index, rows, width, kinds, length=None):
        self.scale = 0.25**index
        self.rows = rows
        self.width = width
        self.kinds = kinds
        row = iota((8, width), 0)
        self.has_zp, self.has_zm = row < 8 - rows, row >= rows
        self.has_yp = self.has_ym = None
        if length is not None:
            lane = iota((8, width), 1)
            self.has_yp, self.has_ym = lane < length - 1, lane > 0

    def lanes(self, tile):
        return pl.ds(tile * self.width, self.width)

    def yp(self, a):
        return pltpu.roll(a, self.width - 1, 1)

    def ym(self, a):
        return pltpu.roll(a, 1, 1)

    def zp(self, a):
        return pltpu.roll(a, 8 - self.rows, 0)

    def zm(self, a):
        return pltpu.roll(a, self.rows, 0)

    @staticmethod
    def keep(mask, a):
        return a if mask is None else jnp.where(mask, a, 0.0)

    def dy_of(self, up, down):
        return self.keep(self.has_yp, up) - self.keep(self.has_ym, down)

    def dz_of(self, up, down):
        return self.keep(self.has_zp, up) - self.keep(self.has_zm, down)

    @property
    def layered(self):
        return self.rows < 8

    def weights(self, coeff, at, k_ref, kat):
        gains, backs = [], []
        for kind in range(max(self.kinds) + 1):
            lanes = self.lanes(kind)
            c = coeff[at, :, lanes]
            near = [coeff[at + 1, :, lanes], coeff[at - 1, :, lanes]]
            near += [self.keep(self.has_yp, self.yp(c)), self.keep(self.has_ym, self.ym(c))]
            if self.layered:
                near += [self.keep(self.has_zp, self.zp(c)), self.keep(self.has_zm, self.zm(c))]
            total = near[0]
            for n in near[1:]:
                total = total + n
            diag = MASS + self.scale * (8.0 * c + 0.5 * total)
            gain = jnp.where(c > 0.0, RELAX / diag, 0.0)
            half = (0.5 * self.scale) * gain
            own = (GRAD_DIV * self.scale) * gain * c
            masks = [None, None, self.has_yp, self.has_ym, self.has_zp, self.has_zm]
            for i, n in enumerate(near):
                face = half * (c + n)
                k_ref[i, kat, :, lanes] = self.keep(masks[i], face)
                k_ref[6 + i, kat, :, lanes] = self.keep(masks[i], face + own)
            k_ref[12, kat, :, lanes] = 0.25 * own
            gains.append(gain)
            backs.append(diag * (1.0 / RELAX))
        return gains, backs

    def cross(self, u, at, t_ref, tat):
        for tile in range(len(self.kinds)):
            lanes = self.lanes(tile)
            uy = u[1, at, :, lanes]
            t = self.dy_of(self.yp(uy), self.ym(uy))
            if self.layered:
                uz = u[2, at, :, lanes]
                t = t + self.dz_of(self.zp(uz), self.zm(uz))
            t_ref[tat, :, lanes] = t

    def change(self, u, at, t_ref, px_ref, tat, k_ref, kat, x1, xat, write):
        for tile, kind in enumerate(self.kinds):
            lanes = self.lanes(tile)
            k = lambda i: k_ref[i, kat, :, self.lanes(kind)]
            mine = [u[c, at, :, lanes] for c in range(3)]
            fore = [u[c, at + 1, :, lanes] for c in range(3)]
            back = [u[c, at - 1, :, lanes] for c in range(3)]
            y_up = [self.yp(a) for a in mine]
            y_dn = [self.ym(a) for a in mine]
            dxx = fore[0] - back[0]
            dyy = self.dy_of(y_up[1], y_dn[1])
            side = dxx
            cross = dyy
            if self.layered:
                z_up = [self.zp(a) for a in mine]
                z_dn = [self.zm(a) for a in mine]
                dzz = self.dz_of(z_up[2], z_dn[2])
                side = dxx + dzz
                cross = dyy + dzz
            t_ref[tat, :, lanes] = cross
            mixed = [None, self.dy_of(self.yp(side), self.ym(side)), None]
            if self.layered:
                below = dxx + dyy
                mixed[2] = self.dz_of(self.zp(below), self.zm(below))
            for c in range(3):
                total = x1[c, xat, :, lanes] - RELAX * mine[c]
                total = total + (k(6 if c == 0 else 0) * fore[c] + k(7 if c == 0 else 1) * back[c])
                sides = k(8 if c == 1 else 2) * y_up[c] + k(9 if c == 1 else 3) * y_dn[c]
                if self.layered:
                    sides = sides + (k(10 if c == 2 else 4) * z_up[c] + k(11 if c == 2 else 5) * z_dn[c])
                if mixed[c] is not None:
                    sides = sides + k(12) * mixed[c]
                if c == 0:
                    px_ref[tat, :, lanes] = total + sides
                else:
                    write(c, tile, lanes, total + sides)

    def apply(self, u, uo, t_ref, px_ref, k_ref, ko, x1, xo, low, high, unroll, write):
        self.cross(u, low - 1 + uo, t_ref, 0)
        self.cross(u, high + uo, t_ref, high - low + 1)

        def one(p):
            def put(c, tile, lanes, d):
                write(c, p, tile, lanes, d)

            self.change(u, p + uo, t_ref, px_ref, p - low + 1, k_ref, p + ko, x1, p + xo, put)

        def mixed(p):
            at = p - low + 1
            for tile, kind in enumerate(self.kinds):
                lanes = self.lanes(tile)
                t = t_ref[at + 1, :, lanes] - t_ref[at - 1, :, lanes]
                write(0, p, tile, lanes, px_ref[at, :, lanes] + k_ref[12, p + ko, :, self.lanes(kind)] * t)

        each(low, high, unroll, one)
        each(low, high, 2 * unroll, mixed)


def each(low, high, unroll, body):
    count = high - low
    while count % unroll:
        unroll -= 1
    if count == unroll:
        for p in range(low, high):
            body(p)
        return

    def step(i, carry):
        for b in range(unroll):
            body(low + i * unroll + b)
        return carry

    lax.fori_loop(0, count // unroll, step, 0)


def tile_y(lane):
    return (lane & 127) - LEFT, PIECE + (lane & 31), (lane & 127) >> 5


def bf16(mask, value):
    return jnp.where(mask, value, 0.0).astype(jnp.bfloat16)


def rows_of(ref, group, x):
    return ref[pl.ds(group * 64 + x, 8, stride=8), :]


def coeff_rows(m_ref, x):
    return jnp.where(rows_of(m_ref, 0, x) == 1, 1.0, 0.05).astype(F32)


def edge_kernel(f_hbm, m_hbm, left_ref, right_ref, f_ref, m_ref, sems):
    step = f_ref.shape[0] // VEC
    copies = [pltpu.make_async_copy(f_hbm.at[pl.ds(step * v, step)], f_ref.at[pl.ds(step * v, step)], sems.at[v]) for v in range(VEC)]
    copies.append(pltpu.make_async_copy(m_hbm, m_ref, sems.at[VEC]))
    for copy in copies:
        copy.start()
    for v in range(VEC):
        copies[v].wait()
        for x in range(BX):
            for c in range(COMP):
                val = rows_of(f_ref, v * COMP + c, x)
                lanes = pl.ds((x // 4) * 64 + 16 * v, 16)
                left_ref[c * 4 + x % 4, :, lanes] = val[:, :RIM]
                right_ref[c * 4 + x % 4, :, lanes] = val[:, BY - RIM :]
    copies[VEC].wait()
    for x in range(BX):
        val = coeff_rows(m_ref, x)
        left_ref[12, :, pl.ds(16 * x, 16)] = val[:, :RIM]
        right_ref[12, :, pl.ds(16 * x, 16)] = val[:, BY - RIM :]


def at_coeff(base, x):
    piece = 8 + x // 4
    return base + x // 5, 128 * (x % 5), base + piece // 5, 128 * (piece % 5) + 32 * (x % 4)


def place_kernel(f_ref, m_ref, own_ref):
    def put(row, lane, piece_row, piece_lane, val):
        own_ref[row, :, pl.ds(lane + LEFT, 128 - LEFT)] = val[:, : 128 - LEFT]
        own_ref[piece_row, :, pl.ds(piece_lane, BY - PIECE)] = val[:, PIECE:]

    for x in range(BX):
        for c in range(COMP):
            for v in range(VEC):
                put(BX * c + x, 128 * v, BX * c + x, 512 + 32 * v, rows_of(f_ref, v * COMP + c, x))
        put(*at_coeff(COMP * BX, x), coeff_rows(m_ref, x))


def join_kernel(gy, placed_ref, l_ref, r_ref, own_ref, left_ref, right_ref):
    place = lax.axis_index("gy")
    from_left = (place > 0).astype(F32)
    from_right = (place < gy - 1).astype(F32)
    kept = BY - PIECE
    for i in range(COMP * BX + 2):
        own_ref[i] = placed_ref[i]

    def put(row, lane, piece_row, piece_lane, left, right):
        own_ref[row, :, pl.ds(lane, LEFT)] = left[:, RIM - LEFT :]
        own_ref[piece_row, :, pl.ds(piece_lane + kept, 32 - kept)] = right[:, : 32 - kept]

    for x in range(BX):
        for c in range(COMP):
            left = l_ref[c * 4 + x % 4] * from_left
            right = r_ref[c * 4 + x % 4] * from_right
            for v in range(VEC):
                at = (x // 4) * 64 + 16 * v
                put(BX * c + x, 128 * v, BX * c + x, 512 + 32 * v, left[:, at : at + RIM], right[:, at : at + RIM])
        left = l_ref[12, :, pl.ds(16 * x, 16)] * from_left
        right = r_ref[12, :, pl.ds(16 * x, 16)] * from_right
        put(*at_coeff(COMP * BX, x), left, right)
    for c in range(COMP):
        for x in range(FX):
            left_ref[c * FX + x] = own_ref[BX * c + x]
            right_ref[c * FX + x] = own_ref[BX * c + x + BX - FX]
    for i in range(2):
        left_ref[COMP * FX + i] = own_ref[COMP * BX + i]
        right_ref[COMP * FX + i] = own_ref[COMP * BX + i]


def down_kernel(
    gx, own_ref, l_ref, r_ref,
    pay_ref, send_l, send_r, x1_ref, x2_ref, c0_ref, y1, y2_ref, k1,
    x1, x2, k0, y2, cx, dr0, t0, p0, rest, stack, cstack, c1, dr1, f1, t1, p1, r1, stack1, pay,
):
    place = lax.axis_index("gx")
    from_left = (place > 0).astype(F32)
    from_right = (place < gx - 1).astype(F32)
    a = Level(0, 1, 128, (0, 0, 0, 0, 1))

    def spread(plane, ref, base, x, factor):
        row, lane, piece_row, piece_lane = at_coeff(base, x)
        val = ref[row, :, pl.ds(lane, 128)]
        end = ref[piece_row, :, pl.ds(piece_lane, 32)]
        if factor is not None:
            val, end = val * factor, end * factor
        cx[plane + CX, :, pl.ds(0, 128)] = val
        for v in range(VEC):
            cx[plane + CX, :, pl.ds(128 + 32 * v, 32)] = end

    for x in range(BX):
        spread(x, own_ref, COMP * BX, x, None)
    for x in range(CX):
        spread(x - CX, l_ref, COMP * FX, x + BX - CX, from_left)
        spread(x + BX, r_ref, COMP * FX, x, from_right)

    def start(low, high, load):
        def body(p):
            gain, back = a.weights(cx, p + CX, k0, p + FX)
            for kind in range(2):
                dr0[p + FX, :, a.lanes(kind)] = back[kind]
            for c in range(COMP):
                plane = load(c, p)
                for tile, kind in enumerate(a.kinds):
                    x1[c, p + FX, :, a.lanes(tile)] = gain[kind] * plane[:, 128 * tile : 128 * tile + 128]

        each(low, high, 4, body)

    start(-FX, 0, lambda c, p: l_ref[c * FX + p + FX])
    start(0, BX, lambda c, p: own_ref[BX * c + p])
    start(BX, BX + FX, lambda c, p: r_ref[c * FX + p - BX])

    def to_x2(c, p, tile, lanes, d):
        x2[c, p + FX, :, lanes] = x1[c, p + FX, :, lanes] + d

    a.apply(x1, FX, t0, p0, k0, FX, x1, FX, 1 - FX, BX + FX - 1, UNROLL0, to_x2)

    def to_rest(c, p, tile, lanes, d):
        rest[c, p + 4, :, lanes] = d * dr0[p + FX, :, a.lanes(a.kinds[tile])]

    a.apply(x2, FX, t0, p0, k0, FX, x1, FX, -4, BX + 4, UNROLL0, to_rest)

    for c in range(COMP):
        for i in range(8):
            plane = rest[c, 2 * i] + rest[c, 2 * i + 1]
            stack[pl.ds(64 * c + 8 * i, 8), :] = plane + a.zp(plane)
    for i in range(10):
        plane = cx[2 * i + 1] + cx[2 * i + 2]
        cstack[pl.ds(8 * i, 8), :] = plane + a.zp(plane)
    selectors = []
    row, col = iota((K0, 128), 0), iota((K0, 128), 1)
    y, y_piece, vec = tile_y(row)
    for v in range(VEC):
        own_tile = (row < 128) & (y >= -10) & (y < SPLIT) & ((y >> 1) + 32 == col)
        piece = (row >= 128) & (vec == v) & (y_piece >= SPLIT) & (y_piece < BY + 10) & ((y_piece >> 1) + 32 == col)
        selectors.append(bf16(own_tile | piece, 0.125))
    parts = parts_of(stack[...])
    coarse = [
        exact_dot([jnp.concatenate([p[:, 128 * v : 128 * v + 128], p[:, 512:]], axis=1) for p in parts], selectors[v])
        for v in range(VEC)
    ]
    coarse_c = exact_dot(parts_of(cstack[...]), selectors[0])
    even = (iota((8, 128), 0) & 1) == 0
    for c in range(COMP):
        for i in range(8):
            at = 64 * c + 8 * i
            for low in range(2):
                odd = pltpu.roll(coarse[2 + low][at : at + 8], 1, 0)
                f1[c, i, :, pl.ds(128 * low, 128)] = jnp.where(even, coarse[low][at : at + 8], odd)
    for i in range(10):
        block = coarse_c[8 * i : 8 * i + 8]
        c1[i] = jnp.where(even, block, pltpu.roll(block, 1, 0))

    b = Level(1, 2, 128, (0, 0))
    for p in range(-2, 6):
        gain, back = b.weights(c1, p + 3, k1, p + 2)
        dr1[p + 2] = back[0]
        for c in range(COMP):
            for tile in range(2):
                y1[c, p + 2, :, b.lanes(tile)] = gain[0] * f1[c, p + 2, :, b.lanes(tile)]

    def to_y2(c, p, tile, lanes, d):
        y2[c, p + 1, :, lanes] = y1[c, p + 2, :, lanes] + d

    b.apply(y1, 2, t1, p1, k1, 2, y1, 2, -1, 5, UNROLL1, to_y2)
    for c in range(COMP):
        for i in range(3):
            send_l[3 * c + i] = y2[c, 1 + i]
            send_r[3 * c + i] = y2[c, 2 + i]

    def to_r1(c, p, tile, lanes, d):
        r1[c, p, :, lanes] = d * dr1[p + 2]

    b.apply(y2, 1, t1, p1, k1, 2, y1, 2, 0, 4, UNROLL1, to_r1)

    for c in range(COMP):
        for i in range(2):
            plane = r1[c, 2 * i] + r1[c, 2 * i + 1]
            plane = plane + pltpu.roll(plane, 6, 0)
            stack1[pl.ds(8 * (2 * c + i), 8), :] = plane[:, :128]
            stack1[pl.ds(64 + 8 * (2 * c + i), 8), :] = plane[:, 128:]
    for i in range(2):
        plane = c1[2 * i + 3] + c1[2 * i + 4]
        plane = plane + b.zp(plane)
        stack1[pl.ds(8 * (6 + i), 8), :] = plane
        stack1[pl.ds(64 + 8 * (6 + i), 8), :] = plane
    lane = iota((128, 128), 0) - 32
    selector1 = bf16((lane >> 1 == iota((128, 128), 1)) & (lane >= 0) & (lane < 64), 0.125)
    coarse1 = exact_dot(parts_of(stack1[...]), selector1)
    first = (iota((8, 32), 0) & 2) == 0
    for g in range(8):
        low = coarse1[8 * g : 8 * g + 8]
        high = pltpu.roll(coarse1[64 + 8 * g : 72 + 8 * g], 2, 0)
        pay[pl.ds(8 * (g // 4), 8), pl.ds(32 * (g % 4), 32)] = jnp.where(first, low[:, :32], high[:, :32])
    packed = pay[...]

    def copy(i):
        pay_ref[i] = packed

    each(0, pay_ref.shape[0], 8, copy)
    for c in range(COMP):
        for i in range(10):
            x1_ref[c, i] = x1[c, i + 5]
        for i in range(12):
            x2_ref[c, i] = x2[c, i + 4]
        for i in range(4):
            y2_ref[c, i] = y2[c, i + 1]
    for i in range(12):
        c0_ref[i] = cx[i + 5]


def up_kernel(
    gx, gy, got_ref, l_ref, r_ref, x1, x2, c0_ref, y1, y2, k1, out_ref,
    c2, f2, k2, dr2, x1c, ua, ub, rc, t2, p2, s2, c3, k3, x1d, va, vb, t3, p3, s3, sw, w0, w1, t1, p1, sp, k0, u0, u1, t0, p0,
):
    nx2, nx3 = 2 * gx, gx
    yy2, l3 = 32 * gy, c3.shape[-1]
    place_x = lax.axis_index("gx")
    place_y = lax.axis_index("gy")
    from_left = (place_x > 0).astype(F32)
    from_right = (place_x < gx - 1).astype(F32)

    zero2 = jnp.zeros((8, yy2), F32)
    for ref in (ua, ub):
        for c in range(COMP):
            for i in (0, 1, nx2 + 2, nx2 + 3):
                ref[c, i] = zero2
    c2[0] = zero2
    c2[nx2 + 1] = zero2

    def unpack(i):
        for j in range(gy):
            for g in range(8):
                block = got_ref[i * gy + j, pl.ds(8 * (g // 4), 8), pl.ds(32 * (g % 4), 32)]
                if g < 6:
                    f2[g // 2, 2 * i + g % 2, :, pl.ds(32 * j, 32)] = block
                else:
                    c2[2 * i + g - 5, :, pl.ds(32 * j, 32)] = block

    each(0, gx, 8, unpack)
    m = Level(2, 4, yy2, (0,), yy2)

    def start2(p):
        gain, back = m.weights(c2, p + 1, k2, p)
        dr2[p] = back[0]
        for c in range(COMP):
            val = gain[0] * f2[c, p]
            x1c[c, p] = val
            ua[c, p + 2] = val

    each(0, nx2, 8, start2)

    def sweep2(src, dst):
        def write(c, p, tile, lanes, d):
            dst[c, p + 2] = src[c, p + 2] + d

        m.apply(src, 2, t2, p2, k2, 0, x1c, 0, 0, nx2, UNROLL2, write)

    sweep2(ua, ub)

    def to_rc(c, p, tile, lanes, d):
        rc[c, p] = d * dr2[p]

    m.apply(ub, 2, t2, p2, k2, 0, x1c, 0, 0, nx2, UNROLL2, to_rc)

    for i in range(nx3):
        for c in range(COMP):
            plane = rc[c, 2 * i] + rc[c, 2 * i + 1]
            s2[pl.ds(8 * (c * nx3 + i), 8), :] = plane + pltpu.roll(plane, 4, 0)
        plane = c2[2 * i + 1] + c2[2 * i + 2]
        s2[pl.ds(8 * (COMP * nx3 + i), 8), :] = plane + pltpu.roll(plane, 4, 0)
    selector = bf16((iota((yy2, l3), 0) >> 1) == iota((yy2, l3), 1), 0.125)
    coarse = exact_dot(parts_of(s2[...]), selector)
    zero3 = jnp.zeros((8, l3), F32)
    for ref in (va, vb):
        for c in range(COMP):
            ref[c, 0] = zero3
            ref[c, nx3 + 1] = zero3
    c3[0] = zero3
    c3[nx3 + 1] = zero3
    for i in range(nx3):
        c3[i + 1] = coarse[8 * (COMP * nx3 + i) : 8 * (COMP * nx3 + i) + 8]
    n = Level(3, 8, l3, (0,), 16 * gy)
    a = Level(0, 1, 128, (0, 0, 0, 0, 1))
    for p in range(nx3):
        gain, _ = n.weights(c3, p + 1, k3, p)
        for c in range(COMP):
            val = gain[0] * coarse[8 * (c * nx3 + p) : 8 * (c * nx3 + p) + 8]
            x1d[c, p] = val
            va[c, p + 1] = val
    src, dst = va, vb
    for sweep in range(COARSE - 1):

        def write3(c, p, tile, lanes, d, src=src, dst=dst):
            dst[c, p + 1] = src[c, p + 1] + d

        n.apply(src, 1, t3, p3, k3, 0, x1d, 0, 0, nx3, UNROLL2, write3)
        for p in (2 * sweep - 1, 2 * sweep):
            a.weights(c0_ref, p + 2, k0, p + 1)
        src, dst = dst, src
    for c in range(COMP):
        for i in range(nx3):
            s3[pl.ds(8 * (c * nx3 + i), 8), :] = src[c, i + 1]
    selector = bf16((iota((l3, yy2), 1) >> 1) == iota((l3, yy2), 0), 1.0)
    fine = exact_dot(parts_of(s3[...]), selector)
    for c in range(COMP):
        for i in range(nx3):
            block = fine[8 * (c * nx3 + i) : 8 * (c * nx3 + i) + 8]
            for j in range(2):
                ub[c, 2 * i + j + 2] = ub[c, 2 * i + j + 2] + block
    sweep2(ub, ua)
    sweep2(ua, ub)

    row = iota((8, yy2), 0)
    for c in range(COMP):
        for i in range(6):
            e = ub[c, 2 * place_x + i]
            at = 16 * (6 * c + i)
            sw[pl.ds(at, 8), :] = jnp.where((row & 2) == 0, e, pltpu.roll(e, 2, 0))
            sw[pl.ds(at + 8, 8), :] = jnp.where((row & 2) != 0, e, pltpu.roll(e, 6, 0))
    y1g = place_y * 64 + iota((yy2, 128), 1) - 32
    fine = exact_dot(parts_of(sw[...]), bf16((y1g >> 1) == iota((yy2, 128), 0), 1.0))
    for c in range(COMP):
        for p in range(-3, 7):
            if p < 0:
                val = l_ref[3 * c + p + 3] * from_left
            elif p < 4:
                val = y2[c, p]
            else:
                val = r_ref[3 * c + p - 4] * from_right
            at = 16 * (6 * c + (p + 4) // 2)
            w0[c, p + 3] = val + jnp.concatenate([fine[at : at + 8], fine[at + 8 : at + 16]], axis=1)
    b = Level(1, 2, 128, (0, 0))

    def write1(c, p, tile, lanes, d):
        w1[c, p + 3, :, lanes] = w0[c, p + 3, :, lanes] + d

    b.apply(w0, 3, t1, p1, k1, 2, y1, 2, -2, 6, UNROLL1, write1)
    odd = (iota((8, 128), 0) & 1) != 0

    def write1b(c, p, tile, lanes, d):
        e = w1[c, p + 3, :, lanes] + d
        rows = pl.ds(8 * (6 * c + p + 1), 8)
        sp[tile, rows, :] = jnp.where(odd, pltpu.roll(e, 1, 0), e)
        sp[2 + tile, rows, :] = jnp.where(odd, e, pltpu.roll(e, 7, 0))

    b.apply(w1, 3, t1, p1, k1, 2, y1, 2, -1, 5, 6, write1b)

    col = iota((128, K0), 1)
    y, y_piece, vec = tile_y(col)
    piece = None
    for v in range(VEC):
        parent = jnp.where(col < 128, y >> 1, y_piece >> 1) + 32
        selector = bf16((parent == iota((128, K0), 0)) & ((col < 128) | (vec == v)), 1.0)
        fine = exact_dot(parts_of(sp[v]), selector)
        piece = fine[:, 128:] if v == 0 else piece + fine[:, 128:]
        for c in range(COMP):
            for i in range(6):
                at = 8 * (6 * c + i)
                for j in range(2):
                    u0[c, 2 * i + j, :, pl.ds(128 * v, 128)] = x2[c, 2 * i + j, :, pl.ds(128 * v, 128)] + fine[at : at + 8, :128]
    for c in range(COMP):
        for i in range(6):
            at = 8 * (6 * c + i)
            for j in range(2):
                u0[c, 2 * i + j, :, pl.ds(512, 128)] = x2[c, 2 * i + j, :, pl.ds(512, 128)] + piece[at : at + 8]

    def write0(c, p, tile, lanes, d):
        u1[c, p + 2, :, lanes] = u0[c, p + 2, :, lanes] + d

    a.apply(u0, 2, t0, p0, k0, 1, x1, 1, -1, 9, UNROLL0, write0)

    def write_last(c, p, tile, lanes, d):
        u0[c, p + 2, :, lanes] = u1[c, p + 2, :, lanes] + d

    a.apply(u1, 2, t0, p0, k0, 1, x1, 1, 0, BX, UNROLL0, write_last)
    near = iota((8, 128), 1) < SPLIT
    for x in range(BX):
        for c in range(COMP):
            last = u0[c, x + 2, :, pl.ds(512, 128)]
            for v in range(VEC):
                main = pltpu.roll(u0[c, x + 2, :, pl.ds(128 * v, 128)], 128 - LEFT, 1)
                ends = pltpu.roll(last, (PIECE - 32 * v) % 128, 1)
                out_ref[pl.ds((v * COMP + c) * 64 + x, 8, stride=8), :] = jnp.where(near, main, ends)


def call(kernel, outs, scratch, *args):
    vmem = pl.BlockSpec(memory_space=pltpu.VMEM)
    shapes = [jax.ShapeDtypeStruct(s, F32) for s in outs]
    return pl.pallas_call(
        kernel,
        out_shape=shapes,
        in_specs=[vmem] * len(args),
        out_specs=[vmem] * len(outs),
        scratch_shapes=[pltpu.VMEM(s, F32) for s in scratch],
        compiler_params=pltpu.CompilerParams(vmem_limit_bytes=48 * 1024 * 1024),
    )(*args)


def per_device(gx, gy, right_side, material):
    def ring(value, axis, size, step):
        return lax.ppermute(value, axis, [(i, (i + step) % size) for i in range(size)])

    f = right_side.reshape(VEC * COMP * NZ * BX, BY)
    m = material.reshape(NZ * BX, BY)
    edge = (13, 8, 128)
    hbm, vmem = pl.BlockSpec(memory_space=pltpu.HBM), pl.BlockSpec(memory_space=pltpu.VMEM)
    to_left, to_right = pl.pallas_call(
        edge_kernel,
        out_shape=[jax.ShapeDtypeStruct(s, F32) for s in (edge, edge)],
        in_specs=[hbm] * 2,
        out_specs=[vmem] * 2,
        scratch_shapes=[pltpu.VMEM(f.shape, F32), pltpu.VMEM(m.shape, jnp.int32), pltpu.SemaphoreType.DMA((VEC + 1,))],
        compiler_params=pltpu.CompilerParams(vmem_limit_bytes=61 * 1024 * 1024),
    )(f, m)
    right = ring(to_left, "gy", gy, -1)
    left = ring(to_right, "gy", gy, 1)
    side = (COMP * FX + 2, 8, L0)
    whole = (COMP * BX + 2, 8, L0)
    (own,) = call(place_kernel, [whole], [], f, m)
    own, to_left, to_right = call(functools.partial(join_kernel, gy), [whole, side, side], [], own, left, right)
    right = ring(to_left, "gx", gx, -1)
    left = ring(to_right, "gx", gx, 1)
    n = gx * gy
    plane = lambda *lead: (*lead, 8, L0)
    plane1 = lambda *lead: (*lead, 8, L1)
    nf, nc = BX + 2 * FX, BX + 2 * CX
    pay, to_left, to_right, *kept = call(
        functools.partial(down_kernel, gx),
        [
            (n, 16, 128), plane1(9), plane1(9), plane(3, 10), plane(3, 12), (12, 8, K0), plane1(3, 8), plane1(3, 4), (13, 8, 8, 128),
        ],
        [
            plane(3, nf), plane(3, nf), (13, nf, 8, K0), plane1(3, 6),
            (nc, 8, K0), (nf, 8, K0), plane(nf), plane(nf), plane(3, 16), (192, L0), (80, K0), (10, 8, 128),
            (8, 8, 128), plane1(3, 8), plane1(10), plane1(10), plane1(3, 4), (128, 128), (16, 128),
        ],
        own, left, right,
    )
    right = ring(to_left, "gx", gx, -1)
    left = ring(to_right, "gx", gx, 1)
    got = lax.all_to_all(pay, ("gx", "gy"), 0, 0)
    nx2, nx3, y2, l3 = 2 * gx, gx, 32 * gy, max(128, 16 * gy)
    plane2 = lambda *lead: (*lead, 8, y2)
    plane3 = lambda *lead: (*lead, 8, l3)
    (out,) = call(
        functools.partial(up_kernel, gx, gy),
        [(VEC * COMP * NZ * BX, BY)],
        [
            plane2(nx2 + 2), plane2(3, nx2), plane2(13, nx2), plane2(nx2), plane2(3, nx2), plane2(3, nx2 + 4), plane2(3, nx2 + 4),
            plane2(3, nx2), plane2(nx2 + 2), plane2(nx2 + 2), (32 * nx3, y2),
            plane3(nx3 + 2), plane3(13, nx3), plane3(3, nx3), plane3(3, nx3 + 2), plane3(3, nx3 + 2), plane3(nx3 + 2), plane3(nx3 + 2),
            (24 * nx3, l3), (288, y2), plane1(3, 10), plane1(3, 10), plane1(10), plane1(10), (4, 144, 128), (13, 10, 8, K0),
            plane(3, 12), plane(3, 12), plane(12), plane(12),
        ],
        got, left, right, *kept,
    )
    return out.reshape(right_side.shape)


def solution(mesh):
    gx, gy = mesh.shape["gx"], mesh.shape["gy"]
    spec = P(None, None, None, "gx", "gy")
    return jax.shard_map(
        functools.partial(per_device, gx, gy), mesh=mesh, in_specs=(spec, P(None, "gx", "gy")), out_specs=spec, check_vma=False
    )
```

```python
import functools

import jax
import jax.numpy as jnp
from jax import lax
from jax.experimental import pallas as pl
from jax.experimental.pallas import tpu as pltpu
from jax.sharding import PartitionSpec as P

RELAX = 0.6
MASS = 0.01
GRAD_DIV = 2.5
VEC, COMP, NZ, BX, BY = 4, 3, 8, 8, 128
COARSE = 6
UNROLL0, UNROLL1, UNROLL2 = 20, 8, 16
RIM = 16
LEFT = 11
PIECE = 108
SPLIT = 112
L0 = 5 * 128
K0 = 2 * 128
L1 = 2 * 128
FX = 6
CX = 7
F32 = jnp.float32


def iota(shape, dim):
    return lax.broadcasted_iota(jnp.int32, shape, dim)


def parts_of(value):
    high = value.astype(jnp.bfloat16)
    rest = value - high.astype(F32)
    mid = rest.astype(jnp.bfloat16)
    return high, mid, (rest - mid.astype(F32)).astype(jnp.bfloat16)


def exact_dot(parts, selector):
    out = [jnp.dot(p, selector, preferred_element_type=F32) for p in parts]
    return out[0] + out[1] + out[2]


class Level:
    def __init__(self, index, rows, width, kinds, length=None):
        self.scale = 0.25**index
        self.rows = rows
        self.width = width
        self.kinds = kinds
        row = iota((8, width), 0)
        self.has_zp, self.has_zm = row < 8 - rows, row >= rows
        self.has_yp = self.has_ym = None
        if length is not None:
            lane = iota((8, width), 1)
            self.has_yp, self.has_ym = lane < length - 1, lane > 0

    def lanes(self, tile):
        return pl.ds(tile * self.width, self.width)

    def yp(self, a):
        return pltpu.roll(a, self.width - 1, 1)

    def ym(self, a):
        return pltpu.roll(a, 1, 1)

    def zp(self, a):
        return pltpu.roll(a, 8 - self.rows, 0)

    def zm(self, a):
        return pltpu.roll(a, self.rows, 0)

    @staticmethod
    def keep(mask, a):
        return a if mask is None else jnp.where(mask, a, 0.0)

    def dy_of(self, up, down):
        return self.keep(self.has_yp, up) - self.keep(self.has_ym, down)

    def dz_of(self, up, down):
        return self.keep(self.has_zp, up) - self.keep(self.has_zm, down)

    @property
    def layered(self):
        return self.rows < 8

    def weights(self, coeff, at, k_ref, kat):
        gains, backs = [], []
        for kind in range(max(self.kinds) + 1):
            lanes = self.lanes(kind)
            c = coeff[at, :, lanes]
            near = [coeff[at + 1, :, lanes], coeff[at - 1, :, lanes]]
            near += [self.keep(self.has_yp, self.yp(c)), self.keep(self.has_ym, self.ym(c))]
            if self.layered:
                near += [self.keep(self.has_zp, self.zp(c)), self.keep(self.has_zm, self.zm(c))]
            total = near[0]
            for n in near[1:]:
                total = total + n
            diag = MASS + self.scale * (8.0 * c + 0.5 * total)
            gain = jnp.where(c > 0.0, RELAX / diag, 0.0)
            half = (0.5 * self.scale) * gain
            own = (GRAD_DIV * self.scale) * gain * c
            masks = [None, None, self.has_yp, self.has_ym, self.has_zp, self.has_zm]
            for i, n in enumerate(near):
                face = half * (c + n)
                k_ref[i, kat, :, lanes] = self.keep(masks[i], face)
                k_ref[6 + i, kat, :, lanes] = self.keep(masks[i], face + own)
            k_ref[12, kat, :, lanes] = 0.25 * own
            gains.append(gain)
            backs.append(diag * (1.0 / RELAX))
        return gains, backs

    def cross(self, u, at, t_ref, tat):
        for tile in range(len(self.kinds)):
            lanes = self.lanes(tile)
            uy = u[1, at, :, lanes]
            t = self.dy_of(self.yp(uy), self.ym(uy))
            if self.layered:
                uz = u[2, at, :, lanes]
                t = t + self.dz_of(self.zp(uz), self.zm(uz))
            t_ref[tat, :, lanes] = t

    def change(self, u, at, t_ref, px_ref, tat, k_ref, kat, x1, xat, write):
        for tile, kind in enumerate(self.kinds):
            lanes = self.lanes(tile)
            k = lambda i: k_ref[i, kat, :, self.lanes(kind)]
            mine = [u[c, at, :, lanes] for c in range(3)]
            fore = [u[c, at + 1, :, lanes] for c in range(3)]
            back = [u[c, at - 1, :, lanes] for c in range(3)]
            y_up = [self.yp(a) for a in mine]
            y_dn = [self.ym(a) for a in mine]
            dxx = fore[0] - back[0]
            dyy = self.dy_of(y_up[1], y_dn[1])
            side = dxx
            cross = dyy
            if self.layered:
                z_up = [self.zp(a) for a in mine]
                z_dn = [self.zm(a) for a in mine]
                dzz = self.dz_of(z_up[2], z_dn[2])
                side = dxx + dzz
                cross = dyy + dzz
            t_ref[tat, :, lanes] = cross
            mixed = [None, self.dy_of(self.yp(side), self.ym(side)), None]
            if self.layered:
                below = dxx + dyy
                mixed[2] = self.dz_of(self.zp(below), self.zm(below))
            for c in range(3):
                total = x1[c, xat, :, lanes] - RELAX * mine[c]
                total = total + (k(6 if c == 0 else 0) * fore[c] + k(7 if c == 0 else 1) * back[c])
                sides = k(8 if c == 1 else 2) * y_up[c] + k(9 if c == 1 else 3) * y_dn[c]
                if self.layered:
                    sides = sides + (k(10 if c == 2 else 4) * z_up[c] + k(11 if c == 2 else 5) * z_dn[c])
                if mixed[c] is not None:
                    sides = sides + k(12) * mixed[c]
                if c == 0:
                    px_ref[tat, :, lanes] = total + sides
                else:
                    write(c, tile, lanes, total + sides)

    def apply(self, u, uo, t_ref, px_ref, k_ref, ko, x1, xo, low, high, unroll, write):
        self.cross(u, low - 1 + uo, t_ref, 0)
        self.cross(u, high + uo, t_ref, high - low + 1)

        def one(p):
            def put(c, tile, lanes, d):
                write(c, p, tile, lanes, d)

            self.change(u, p + uo, t_ref, px_ref, p - low + 1, k_ref, p + ko, x1, p + xo, put)

        def mixed(p):
            at = p - low + 1
            for tile, kind in enumerate(self.kinds):
                lanes = self.lanes(tile)
                t = t_ref[at + 1, :, lanes] - t_ref[at - 1, :, lanes]
                write(0, p, tile, lanes, px_ref[at, :, lanes] + k_ref[12, p + ko, :, self.lanes(kind)] * t)

        each(low, high, unroll, one)
        each(low, high, 2 * unroll, mixed)


def each(low, high, unroll, body):
    count = high - low
    while count % unroll:
        unroll -= 1
    if count == unroll:
        for p in range(low, high):
            body(p)
        return

    def step(i, carry):
        for b in range(unroll):
            body(low + i * unroll + b)
        return carry

    lax.fori_loop(0, count // unroll, step, 0)


def tile_y(lane):
    return (lane & 127) - LEFT, PIECE + (lane & 31), (lane & 127) >> 5


def bf16(mask, value):
    return jnp.where(mask, value, 0.0).astype(jnp.bfloat16)


def rows_of(ref, group, x):
    return ref[pl.ds(group * 64 + x, 8, stride=8), :]


def coeff_rows(m_ref, x):
    return jnp.where(rows_of(m_ref, 0, x) == 1, 1.0, 0.05).astype(F32)


def edge_kernel(f_hbm, m_hbm, left_ref, right_ref, f_ref, m_ref, sems):
    step = f_ref.shape[0] // VEC
    copies = [pltpu.make_async_copy(f_hbm.at[pl.ds(step * v, step)], f_ref.at[pl.ds(step * v, step)], sems.at[v]) for v in range(VEC)]
    copies.append(pltpu.make_async_copy(m_hbm, m_ref, sems.at[VEC]))
    for copy in copies:
        copy.start()
    for v in range(VEC):
        copies[v].wait()
        for x in range(BX):
            for c in range(COMP):
                val = rows_of(f_ref, v * COMP + c, x)
                lanes = pl.ds((x // 4) * 64 + 16 * v, 16)
                left_ref[c * 4 + x % 4, :, lanes] = val[:, :RIM]
                right_ref[c * 4 + x % 4, :, lanes] = val[:, BY - RIM :]
    copies[VEC].wait()
    for x in range(BX):
        val = coeff_rows(m_ref, x)
        left_ref[12, :, pl.ds(16 * x, 16)] = val[:, :RIM]
        right_ref[12, :, pl.ds(16 * x, 16)] = val[:, BY - RIM :]


def at_coeff(base, x):
    piece = 8 + x // 4
    return base + x // 5, 128 * (x % 5), base + piece // 5, 128 * (piece % 5) + 32 * (x % 4)


def place_kernel(f_ref, m_ref, own_ref):
    def put(row, lane, piece_row, piece_lane, val):
        own_ref[row, :, pl.ds(lane + LEFT, 128 - LEFT)] = val[:, : 128 - LEFT]
        own_ref[piece_row, :, pl.ds(piece_lane, BY - PIECE)] = val[:, PIECE:]

    for x in range(BX):
        for c in range(COMP):
            for v in range(VEC):
                put(BX * c + x, 128 * v, BX * c + x, 512 + 32 * v, rows_of(f_ref, v * COMP + c, x))
        put(*at_coeff(COMP * BX, x), coeff_rows(m_ref, x))


def join_kernel(gy, placed_ref, l_ref, r_ref, own_ref, left_ref, right_ref):
    place = lax.axis_index("gy")
    from_left = (place > 0).astype(F32)
    from_right = (place < gy - 1).astype(F32)
    kept = BY - PIECE
    for i in range(COMP * BX + 2):
        own_ref[i] = placed_ref[i]

    def put(row, lane, piece_row, piece_lane, left, right):
        own_ref[row, :, pl.ds(lane, LEFT)] = left[:, RIM - LEFT :]
        own_ref[piece_row, :, pl.ds(piece_lane + kept, 32 - kept)] = right[:, : 32 - kept]

    for x in range(BX):
        for c in range(COMP):
            left = l_ref[c * 4 + x % 4] * from_left
            right = r_ref[c * 4 + x % 4] * from_right
            for v in range(VEC):
                at = (x // 4) * 64 + 16 * v
                put(BX * c + x, 128 * v, BX * c + x, 512 + 32 * v, left[:, at : at + RIM], right[:, at : at + RIM])
        left = l_ref[12, :, pl.ds(16 * x, 16)] * from_left
        right = r_ref[12, :, pl.ds(16 * x, 16)] * from_right
        put(*at_coeff(COMP * BX, x), left, right)
    for c in range(COMP):
        for x in range(FX):
            left_ref[c * FX + x] = own_ref[BX * c + x]
            right_ref[c * FX + x] = own_ref[BX * c + x + BX - FX]
    for i in range(2):
        left_ref[COMP * FX + i] = own_ref[COMP * BX + i]
        right_ref[COMP * FX + i] = own_ref[COMP * BX + i]


def down_kernel(
    gx, own_ref, l_ref, r_ref,
    pay_ref, send_l, send_r, x1_ref, x2_ref, c0_ref, y1, y2_ref, k1,
    x1, x2, k0, y2, cx, dr0, t0, p0, rest, stack, cstack, c1, dr1, f1, t1, p1, r1, stack1, pay, many, sems,
):
    place = lax.axis_index("gx")
    from_left = (place > 0).astype(F32)
    from_right = (place < gx - 1).astype(F32)
    a = Level(0, 1, 128, (0, 0, 0, 0, 1))

    def spread(plane, ref, base, x, factor):
        row, lane, piece_row, piece_lane = at_coeff(base, x)
        val = ref[row, :, pl.ds(lane, 128)]
        end = ref[piece_row, :, pl.ds(piece_lane, 32)]
        if factor is not None:
            val, end = val * factor, end * factor
        cx[plane + CX, :, pl.ds(0, 128)] = val
        for v in range(VEC):
            cx[plane + CX, :, pl.ds(128 + 32 * v, 32)] = end

    for x in range(BX):
        spread(x, own_ref, COMP * BX, x, None)
    for x in range(CX):
        spread(x - CX, l_ref, COMP * FX, x + BX - CX, from_left)
        spread(x + BX, r_ref, COMP * FX, x, from_right)

    def start(low, high, load):
        def body(p):
            gain, back = a.weights(cx, p + CX, k0, p + FX)
            for kind in range(2):
                dr0[p + FX, :, a.lanes(kind)] = back[kind]
            for c in range(COMP):
                plane = load(c, p)
                for tile, kind in enumerate(a.kinds):
                    x1[c, p + FX, :, a.lanes(tile)] = gain[kind] * plane[:, 128 * tile : 128 * tile + 128]

        each(low, high, 4, body)

    start(-FX, 0, lambda c, p: l_ref[c * FX + p + FX])
    start(0, BX, lambda c, p: own_ref[BX * c + p])
    start(BX, BX + FX, lambda c, p: r_ref[c * FX + p - BX])

    def to_x2(c, p, tile, lanes, d):
        x2[c, p + FX, :, lanes] = x1[c, p + FX, :, lanes] + d

    a.apply(x1, FX, t0, p0, k0, FX, x1, FX, 1 - FX, BX + FX - 1, UNROLL0, to_x2)

    def to_rest(c, p, tile, lanes, d):
        rest[c, p + 4, :, lanes] = d * dr0[p + FX, :, a.lanes(a.kinds[tile])]

    a.apply(x2, FX, t0, p0, k0, FX, x1, FX, -4, BX + 4, UNROLL0, to_rest)

    for c in range(COMP):
        for i in range(8):
            plane = rest[c, 2 * i] + rest[c, 2 * i + 1]
            stack[pl.ds(64 * c + 8 * i, 8), :] = plane + a.zp(plane)
    for i in range(10):
        plane = cx[2 * i + 1] + cx[2 * i + 2]
        cstack[pl.ds(8 * i, 8), :] = plane + a.zp(plane)
    selectors = []
    row, col = iota((K0, 128), 0), iota((K0, 128), 1)
    y, y_piece, vec = tile_y(row)
    for v in range(VEC):
        own_tile = (row < 128) & (y >= -10) & (y < SPLIT) & ((y >> 1) + 32 == col)
        piece = (row >= 128) & (vec == v) & (y_piece >= SPLIT) & (y_piece < BY + 10) & ((y_piece >> 1) + 32 == col)
        selectors.append(bf16(own_tile | piece, 0.125))
    parts = parts_of(stack[...])
    coarse = [
        exact_dot([jnp.concatenate([p[:, 128 * v : 128 * v + 128], p[:, 512:]], axis=1) for p in parts], selectors[v])
        for v in range(VEC)
    ]
    coarse_c = exact_dot(parts_of(cstack[...]), selectors[0])
    even = (iota((8, 128), 0) & 1) == 0
    for c in range(COMP):
        for i in range(8):
            at = 64 * c + 8 * i
            for low in range(2):
                odd = pltpu.roll(coarse[2 + low][at : at + 8], 1, 0)
                f1[c, i, :, pl.ds(128 * low, 128)] = jnp.where(even, coarse[low][at : at + 8], odd)
    for i in range(10):
        block = coarse_c[8 * i : 8 * i + 8]
        c1[i] = jnp.where(even, block, pltpu.roll(block, 1, 0))

    b = Level(1, 2, 128, (0, 0))
    for p in range(-2, 6):
        gain, back = b.weights(c1, p + 3, k1, p + 2)
        dr1[p + 2] = back[0]
        for c in range(COMP):
            for tile in range(2):
                y1[c, p + 2, :, b.lanes(tile)] = gain[0] * f1[c, p + 2, :, b.lanes(tile)]

    def to_y2(c, p, tile, lanes, d):
        y2[c, p + 1, :, lanes] = y1[c, p + 2, :, lanes] + d

    b.apply(y1, 2, t1, p1, k1, 2, y1, 2, -1, 5, UNROLL1, to_y2)
    for c in range(COMP):
        for i in range(3):
            send_l[3 * c + i] = y2[c, 1 + i]
            send_r[3 * c + i] = y2[c, 2 + i]

    def to_r1(c, p, tile, lanes, d):
        r1[c, p, :, lanes] = d * dr1[p + 2]

    b.apply(y2, 1, t1, p1, k1, 2, y1, 2, 0, 4, UNROLL1, to_r1)

    for c in range(COMP):
        for i in range(2):
            plane = r1[c, 2 * i] + r1[c, 2 * i + 1]
            plane = plane + pltpu.roll(plane, 6, 0)
            stack1[pl.ds(8 * (2 * c + i), 8), :] = plane[:, :128]
            stack1[pl.ds(64 + 8 * (2 * c + i), 8), :] = plane[:, 128:]
    for i in range(2):
        plane = c1[2 * i + 3] + c1[2 * i + 4]
        plane = plane + b.zp(plane)
        stack1[pl.ds(8 * (6 + i), 8), :] = plane
        stack1[pl.ds(64 + 8 * (6 + i), 8), :] = plane
    lane = iota((128, 128), 0) - 32
    selector1 = bf16((lane >> 1 == iota((128, 128), 1)) & (lane >= 0) & (lane < 64), 0.125)
    coarse1 = exact_dot(parts_of(stack1[...]), selector1)
    first = (iota((8, 32), 0) & 2) == 0
    for g in range(8):
        low = coarse1[8 * g : 8 * g + 8]
        high = pltpu.roll(coarse1[64 + 8 * g : 72 + 8 * g], 2, 0)
        pay[pl.ds(8 * (g // 4), 8), pl.ds(32 * (g % 4), 32)] = jnp.where(first, low[:, :32], high[:, :32])
    packed = pay[...]
    batch = many.shape[0]
    for i in range(batch):
        many[i] = packed
    copies = []
    for i in range(pay_ref.shape[0] // batch):
        copies.append(pltpu.make_async_copy(many, pay_ref.at[pl.ds(batch * i, batch)], sems.at[i]))
        copies[-1].start()
    for c in range(COMP):
        for i in range(10):
            x1_ref[c, i] = x1[c, i + 5]
        for i in range(12):
            x2_ref[c, i] = x2[c, i + 4]
        for i in range(4):
            y2_ref[c, i] = y2[c, i + 1]
    for i in range(12):
        c0_ref[i] = cx[i + 5]
    for copy in copies:
        copy.wait()


def up_kernel(
    gx, gy, got_ref, l_ref, r_ref, x1, x2, c0_ref, y1, y2, k1, out_hbm,
    c2, f2, k2, dr2, x1c, ua, ub, rc, t2, p2, s2, c3, k3, x1d, va, vb, t3, p3, s3, sw, w0, w1, t1, p1, sp, k0, u0, u1, t0, p0, out_ref, sems,
):
    nx2, nx3 = 2 * gx, gx
    yy2, l3 = 32 * gy, c3.shape[-1]
    place_x = lax.axis_index("gx")
    place_y = lax.axis_index("gy")
    from_left = (place_x > 0).astype(F32)
    from_right = (place_x < gx - 1).astype(F32)

    zero2 = jnp.zeros((8, yy2), F32)
    for ref in (ua, ub):
        for c in range(COMP):
            for i in (0, 1, nx2 + 2, nx2 + 3):
                ref[c, i] = zero2
    c2[0] = zero2
    c2[nx2 + 1] = zero2

    def unpack(i):
        for j in range(gy):
            for g in range(8):
                block = got_ref[i * gy + j, pl.ds(8 * (g // 4), 8), pl.ds(32 * (g % 4), 32)]
                if g < 6:
                    f2[g // 2, 2 * i + g % 2, :, pl.ds(32 * j, 32)] = block
                else:
                    c2[2 * i + g - 5, :, pl.ds(32 * j, 32)] = block

    each(0, gx, 8, unpack)
    m = Level(2, 4, yy2, (0,), yy2)

    def start2(p):
        gain, back = m.weights(c2, p + 1, k2, p)
        dr2[p] = back[0]
        for c in range(COMP):
            val = gain[0] * f2[c, p]
            x1c[c, p] = val
            ua[c, p + 2] = val

    each(0, nx2, 8, start2)

    def sweep2(src, dst):
        def write(c, p, tile, lanes, d):
            dst[c, p + 2] = src[c, p + 2] + d

        m.apply(src, 2, t2, p2, k2, 0, x1c, 0, 0, nx2, UNROLL2, write)

    sweep2(ua, ub)

    def to_rc(c, p, tile, lanes, d):
        rc[c, p] = d * dr2[p]

    m.apply(ub, 2, t2, p2, k2, 0, x1c, 0, 0, nx2, UNROLL2, to_rc)

    for i in range(nx3):
        for c in range(COMP):
            plane = rc[c, 2 * i] + rc[c, 2 * i + 1]
            s2[pl.ds(8 * (c * nx3 + i), 8), :] = plane + pltpu.roll(plane, 4, 0)
        plane = c2[2 * i + 1] + c2[2 * i + 2]
        s2[pl.ds(8 * (COMP * nx3 + i), 8), :] = plane + pltpu.roll(plane, 4, 0)
    selector = bf16((iota((yy2, l3), 0) >> 1) == iota((yy2, l3), 1), 0.125)
    coarse = exact_dot(parts_of(s2[...]), selector)
    zero3 = jnp.zeros((8, l3), F32)
    for ref in (va, vb):
        for c in range(COMP):
            ref[c, 0] = zero3
            ref[c, nx3 + 1] = zero3
    c3[0] = zero3
    c3[nx3 + 1] = zero3
    for i in range(nx3):
        c3[i + 1] = coarse[8 * (COMP * nx3 + i) : 8 * (COMP * nx3 + i) + 8]
    n = Level(3, 8, l3, (0,), 16 * gy)
    a = Level(0, 1, 128, (0, 0, 0, 0, 1))
    for p in range(nx3):
        gain, _ = n.weights(c3, p + 1, k3, p)
        for c in range(COMP):
            val = gain[0] * coarse[8 * (c * nx3 + p) : 8 * (c * nx3 + p) + 8]
            x1d[c, p] = val
            va[c, p + 1] = val
    src, dst = va, vb
    for sweep in range(COARSE - 1):

        def write3(c, p, tile, lanes, d, src=src, dst=dst):
            dst[c, p + 1] = src[c, p + 1] + d

        n.apply(src, 1, t3, p3, k3, 0, x1d, 0, 0, nx3, UNROLL2, write3)
        for p in (2 * sweep - 1, 2 * sweep):
            a.weights(c0_ref, p + 2, k0, p + 1)
        src, dst = dst, src
    for c in range(COMP):
        for i in range(nx3):
            s3[pl.ds(8 * (c * nx3 + i), 8), :] = src[c, i + 1]
    selector = bf16((iota((l3, yy2), 1) >> 1) == iota((l3, yy2), 0), 1.0)
    fine = exact_dot(parts_of(s3[...]), selector)
    for c in range(COMP):
        for i in range(nx3):
            block = fine[8 * (c * nx3 + i) : 8 * (c * nx3 + i) + 8]
            for j in range(2):
                ub[c, 2 * i + j + 2] = ub[c, 2 * i + j + 2] + block
    sweep2(ub, ua)
    sweep2(ua, ub)

    row = iota((8, yy2), 0)
    for c in range(COMP):
        for i in range(6):
            e = ub[c, 2 * place_x + i]
            at = 16 * (6 * c + i)
            sw[pl.ds(at, 8), :] = jnp.where((row & 2) == 0, e, pltpu.roll(e, 2, 0))
            sw[pl.ds(at + 8, 8), :] = jnp.where((row & 2) != 0, e, pltpu.roll(e, 6, 0))
    y1g = place_y * 64 + iota((yy2, 128), 1) - 32
    fine = exact_dot(parts_of(sw[...]), bf16((y1g >> 1) == iota((yy2, 128), 0), 1.0))
    for c in range(COMP):
        for p in range(-3, 7):
            if p < 0:
                val = l_ref[3 * c + p + 3] * from_left
            elif p < 4:
                val = y2[c, p]
            else:
                val = r_ref[3 * c + p - 4] * from_right
            at = 16 * (6 * c + (p + 4) // 2)
            w0[c, p + 3] = val + jnp.concatenate([fine[at : at + 8], fine[at + 8 : at + 16]], axis=1)
    b = Level(1, 2, 128, (0, 0))

    def write1(c, p, tile, lanes, d):
        w1[c, p + 3, :, lanes] = w0[c, p + 3, :, lanes] + d

    b.apply(w0, 3, t1, p1, k1, 2, y1, 2, -2, 6, UNROLL1, write1)
    odd = (iota((8, 128), 0) & 1) != 0

    def write1b(c, p, tile, lanes, d):
        e = w1[c, p + 3, :, lanes] + d
        rows = pl.ds(8 * (6 * c + p + 1), 8)
        sp[tile, rows, :] = jnp.where(odd, pltpu.roll(e, 1, 0), e)
        sp[2 + tile, rows, :] = jnp.where(odd, e, pltpu.roll(e, 7, 0))

    b.apply(w1, 3, t1, p1, k1, 2, y1, 2, -1, 5, 6, write1b)

    col = iota((128, K0), 1)
    y, y_piece, vec = tile_y(col)
    piece = None
    for v in range(VEC):
        parent = jnp.where(col < 128, y >> 1, y_piece >> 1) + 32
        selector = bf16((parent == iota((128, K0), 0)) & ((col < 128) | (vec == v)), 1.0)
        fine = exact_dot(parts_of(sp[v]), selector)
        piece = fine[:, 128:] if v == 0 else piece + fine[:, 128:]
        for c in range(COMP):
            for i in range(6):
                at = 8 * (6 * c + i)
                for j in range(2):
                    u0[c, 2 * i + j, :, pl.ds(128 * v, 128)] = x2[c, 2 * i + j, :, pl.ds(128 * v, 128)] + fine[at : at + 8, :128]
    for c in range(COMP):
        for i in range(6):
            at = 8 * (6 * c + i)
            for j in range(2):
                u0[c, 2 * i + j, :, pl.ds(512, 128)] = x2[c, 2 * i + j, :, pl.ds(512, 128)] + piece[at : at + 8]

    def write0(c, p, tile, lanes, d):
        u1[c, p + 2, :, lanes] = u0[c, p + 2, :, lanes] + d

    a.apply(u0, 2, t0, p0, k0, 1, x1, 1, -1, 9, UNROLL0, write0)

    def write_last(c, p, tile, lanes, d):
        u0[c, p + 2, :, lanes] = u1[c, p + 2, :, lanes] + d

    a.apply(u1, 2, t0, p0, k0, 1, x1, 1, 0, BX, UNROLL0, write_last)
    near = iota((8, 128), 1) < SPLIT
    copies = []
    for v in range(VEC):
        for c in range(COMP):
            group = v * COMP + c
            for x in range(BX):
                main = pltpu.roll(u0[c, x + 2, :, pl.ds(128 * v, 128)], 128 - LEFT, 1)
                ends = pltpu.roll(u0[c, x + 2, :, pl.ds(512, 128)], (PIECE - 32 * v) % 128, 1)
                out_ref[pl.ds(group * 64 + x, 8, stride=8), :] = jnp.where(near, main, ends)
            rows = pl.ds(group * 64, 64)
            copies.append(pltpu.make_async_copy(out_ref.at[rows], out_hbm.at[rows], sems.at[group]))
            copies[-1].start()
    for copy in copies:
        copy.wait()


def call(kernel, outs, scratch, *args, far=False):
    vmem = pl.BlockSpec(memory_space=pltpu.VMEM)
    shapes = [jax.ShapeDtypeStruct(s, F32) for s in outs]
    return pl.pallas_call(
        kernel,
        out_shape=shapes,
        in_specs=[vmem] * len(args),
        out_specs=[pl.BlockSpec(memory_space=pltpu.HBM) if far and i == 0 else vmem for i in range(len(outs))],
        scratch_shapes=[pltpu.VMEM(s, F32) if isinstance(s, tuple) else s for s in scratch],
        compiler_params=pltpu.CompilerParams(vmem_limit_bytes=48 * 1024 * 1024),
    )(*args)


def per_device(gx, gy, right_side, material):
    def ring(value, axis, size, step):
        return lax.ppermute(value, axis, [(i, (i + step) % size) for i in range(size)])

    f = right_side.reshape(VEC * COMP * NZ * BX, BY)
    m = material.reshape(NZ * BX, BY)
    edge = (13, 8, 128)
    hbm, vmem = pl.BlockSpec(memory_space=pltpu.HBM), pl.BlockSpec(memory_space=pltpu.VMEM)
    to_left, to_right = pl.pallas_call(
        edge_kernel,
        out_shape=[jax.ShapeDtypeStruct(s, F32) for s in (edge, edge)],
        in_specs=[hbm] * 2,
        out_specs=[vmem] * 2,
        scratch_shapes=[pltpu.VMEM(f.shape, F32), pltpu.VMEM(m.shape, jnp.int32), pltpu.SemaphoreType.DMA((VEC + 1,))],
        compiler_params=pltpu.CompilerParams(vmem_limit_bytes=65126 * 1024),
    )(f, m)
    right = ring(to_left, "gy", gy, -1)
    left = ring(to_right, "gy", gy, 1)
    side = (COMP * FX + 2, 8, L0)
    whole = (COMP * BX + 2, 8, L0)
    (own,) = call(place_kernel, [whole], [], f, m)
    own, to_left, to_right = call(functools.partial(join_kernel, gy), [whole, side, side], [], own, left, right)
    right = ring(to_left, "gx", gx, -1)
    left = ring(to_right, "gx", gx, 1)
    n = gx * gy
    plane = lambda *lead: (*lead, 8, L0)
    plane1 = lambda *lead: (*lead, 8, L1)
    nf, nc = BX + 2 * FX, BX + 2 * CX
    pay, to_left, to_right, *kept = call(
        functools.partial(down_kernel, gx),
        [
            (n, 16, 128), plane1(9), plane1(9), plane(3, 10), plane(3, 12), (12, 8, K0), plane1(3, 8), plane1(3, 4), (13, 8, 8, 128),
        ],
        [
            plane(3, nf), plane(3, nf), (13, nf, 8, K0), plane1(3, 6),
            (nc, 8, K0), (nf, 8, K0), plane(nf), plane(nf), plane(3, 16), (192, L0), (80, K0), (10, 8, 128),
            (8, 8, 128), plane1(3, 8), plane1(10), plane1(10), plane1(3, 4), (128, 128), (16, 128), (8, 16, 128), pltpu.SemaphoreType.DMA((n // 8,)),
        ],
        own, left, right, far=True,
    )
    right = ring(to_left, "gx", gx, -1)
    left = ring(to_right, "gx", gx, 1)
    got = lax.all_to_all(pay, ("gx", "gy"), 0, 0)
    nx2, nx3, y2, l3 = 2 * gx, gx, 32 * gy, max(128, 16 * gy)
    plane2 = lambda *lead: (*lead, 8, y2)
    plane3 = lambda *lead: (*lead, 8, l3)
    (out,) = call(
        functools.partial(up_kernel, gx, gy),
        [(VEC * COMP * NZ * BX, BY)],
        [
            plane2(nx2 + 2), plane2(3, nx2), plane2(13, nx2), plane2(nx2), plane2(3, nx2), plane2(3, nx2 + 4), plane2(3, nx2 + 4),
            plane2(3, nx2), plane2(nx2 + 2), plane2(nx2 + 2), (32 * nx3, y2),
            plane3(nx3 + 2), plane3(13, nx3), plane3(3, nx3), plane3(3, nx3 + 2), plane3(3, nx3 + 2), plane3(nx3 + 2), plane3(nx3 + 2),
            (24 * nx3, l3), (288, y2), plane1(3, 10), plane1(3, 10), plane1(10), plane1(10), (4, 144, 128), (13, 10, 8, K0),
            plane(3, 12), plane(3, 12), plane(12), plane(12), f.shape, pltpu.SemaphoreType.DMA((VEC * COMP,)),
        ],
        got, left, right, *kept, far=True,
    )
    return out.reshape(right_side.shape)


def solution(mesh):
    gx, gy = mesh.shape["gx"], mesh.shape["gy"]
    spec = P(None, None, None, "gx", "gy")
    return jax.shard_map(
        functools.partial(per_device, gx, gy), mesh=mesh, in_specs=(spec, P(None, "gx", "gy")), out_specs=spec, check_vma=False
    )
```

```python
import functools

import jax
import jax.numpy as jnp
from jax import lax
from jax.experimental import pallas as pl
from jax.experimental.pallas import tpu as pltpu
from jax.sharding import PartitionSpec as P

RELAX = 0.6
MASS = 0.01
GRAD_DIV = 2.5
VEC, COMP, NZ, BX, BY = 4, 3, 8, 8, 128
COARSE = 6
UNROLL0, UNROLL1, UNROLL2 = 20, 8, 16
RIM = 16
LEFT = 11
PIECE = 108
SPLIT = 112
L0 = 5 * 128
K0 = 2 * 128
PAY = 13
L1 = 2 * 128
FX = 6
CX = 7
F32 = jnp.float32


def iota(shape, dim):
    return lax.broadcasted_iota(jnp.int32, shape, dim)


def parts_of(value):
    high = value.astype(jnp.bfloat16)
    rest = value - high.astype(F32)
    mid = rest.astype(jnp.bfloat16)
    return high, mid, (rest - mid.astype(F32)).astype(jnp.bfloat16)


def exact_dot(parts, selector):
    out = [jnp.dot(p, selector, preferred_element_type=F32) for p in parts]
    return out[0] + out[1] + out[2]


class Level:
    def __init__(self, index, rows, width, kinds, length=None):
        self.scale = 0.25**index
        self.rows = rows
        self.width = width
        self.kinds = kinds
        row = iota((8, width), 0)
        self.has_zp, self.has_zm = row < 8 - rows, row >= rows
        self.has_yp = self.has_ym = None
        if length is not None:
            lane = iota((8, width), 1)
            self.has_yp, self.has_ym = lane < length - 1, lane > 0

    def lanes(self, tile):
        return pl.ds(tile * self.width, self.width)

    def yp(self, a):
        return pltpu.roll(a, self.width - 1, 1)

    def ym(self, a):
        return pltpu.roll(a, 1, 1)

    def zp(self, a):
        return pltpu.roll(a, 8 - self.rows, 0)

    def zm(self, a):
        return pltpu.roll(a, self.rows, 0)

    @staticmethod
    def keep(mask, a):
        return a if mask is None else jnp.where(mask, a, 0.0)

    def dy_of(self, up, down):
        return self.keep(self.has_yp, up) - self.keep(self.has_ym, down)

    def dz_of(self, up, down):
        return self.keep(self.has_zp, up) - self.keep(self.has_zm, down)

    @property
    def layered(self):
        return self.rows < 8

    def weights(self, coeff, at, k_ref, kat):
        gains, backs = [], []
        for kind in range(max(self.kinds) + 1):
            lanes = self.lanes(kind)
            c = coeff[at, :, lanes]
            near = [coeff[at + 1, :, lanes], coeff[at - 1, :, lanes]]
            near += [self.keep(self.has_yp, self.yp(c)), self.keep(self.has_ym, self.ym(c))]
            if self.layered:
                near += [self.keep(self.has_zp, self.zp(c)), self.keep(self.has_zm, self.zm(c))]
            total = near[0]
            for n in near[1:]:
                total = total + n
            diag = MASS + self.scale * (8.0 * c + 0.5 * total)
            gain = jnp.where(c > 0.0, RELAX / diag, 0.0)
            half = (0.5 * self.scale) * gain
            own = (GRAD_DIV * self.scale) * gain * c
            masks = [None, None, self.has_yp, self.has_ym, self.has_zp, self.has_zm]
            for i, n in enumerate(near):
                face = half * (c + n)
                k_ref[i, kat, :, lanes] = self.keep(masks[i], face)
                k_ref[6 + i, kat, :, lanes] = self.keep(masks[i], face + own)
            k_ref[12, kat, :, lanes] = 0.25 * own
            gains.append(gain)
            backs.append(diag * (1.0 / RELAX))
        return gains, backs

    def cross(self, u, at, t_ref, tat):
        for tile in range(len(self.kinds)):
            lanes = self.lanes(tile)
            uy = u[1, at, :, lanes]
            t = self.dy_of(self.yp(uy), self.ym(uy))
            if self.layered:
                uz = u[2, at, :, lanes]
                t = t + self.dz_of(self.zp(uz), self.zm(uz))
            t_ref[tat, :, lanes] = t

    def change(self, u, at, t_ref, px_ref, tat, k_ref, kat, x1, xat, write):
        for tile, kind in enumerate(self.kinds):
            lanes = self.lanes(tile)
            k = lambda i: k_ref[i, kat, :, self.lanes(kind)]
            mine = [u[c, at, :, lanes] for c in range(3)]
            fore = [u[c, at + 1, :, lanes] for c in range(3)]
            back = [u[c, at - 1, :, lanes] for c in range(3)]
            y_up = [self.yp(a) for a in mine]
            y_dn = [self.ym(a) for a in mine]
            dxx = fore[0] - back[0]
            dyy = self.dy_of(y_up[1], y_dn[1])
            side = dxx
            cross = dyy
            if self.layered:
                z_up = [self.zp(a) for a in mine]
                z_dn = [self.zm(a) for a in mine]
                dzz = self.dz_of(z_up[2], z_dn[2])
                side = dxx + dzz
                cross = dyy + dzz
            t_ref[tat, :, lanes] = cross
            mixed = [None, self.dy_of(self.yp(side), self.ym(side)), None]
            if self.layered:
                below = dxx + dyy
                mixed[2] = self.dz_of(self.zp(below), self.zm(below))
            for c in range(3):
                total = x1[c, xat, :, lanes] - RELAX * mine[c]
                total = total + (k(6 if c == 0 else 0) * fore[c] + k(7 if c == 0 else 1) * back[c])
                sides = k(8 if c == 1 else 2) * y_up[c] + k(9 if c == 1 else 3) * y_dn[c]
                if self.layered:
                    sides = sides + (k(10 if c == 2 else 4) * z_up[c] + k(11 if c == 2 else 5) * z_dn[c])
                if mixed[c] is not None:
                    sides = sides + k(12) * mixed[c]
                if c == 0:
                    px_ref[tat, :, lanes] = total + sides
                else:
                    write(c, tile, lanes, total + sides)

    def apply(self, u, uo, t_ref, px_ref, k_ref, ko, x1, xo, low, high, unroll, write):
        self.cross(u, low - 1 + uo, t_ref, 0)
        self.cross(u, high + uo, t_ref, high - low + 1)

        def one(p):
            def put(c, tile, lanes, d):
                write(c, p, tile, lanes, d)

            self.change(u, p + uo, t_ref, px_ref, p - low + 1, k_ref, p + ko, x1, p + xo, put)

        def mixed(p):
            at = p - low + 1
            for tile, kind in enumerate(self.kinds):
                lanes = self.lanes(tile)
                t = t_ref[at + 1, :, lanes] - t_ref[at - 1, :, lanes]
                write(0, p, tile, lanes, px_ref[at, :, lanes] + k_ref[12, p + ko, :, self.lanes(kind)] * t)

        each(low, high, unroll, one)
        each(low, high, 2 * unroll, mixed)


def each(low, high, unroll, body):
    count = high - low
    while count % unroll:
        unroll -= 1
    if count == unroll:
        for p in range(low, high):
            body(p)
        return

    def step(i, carry):
        for b in range(unroll):
            body(low + i * unroll + b)
        return carry

    lax.fori_loop(0, count // unroll, step, 0)


def tile_y(lane):
    return (lane & 127) - LEFT, PIECE + (lane & 31), (lane & 127) >> 5


def bf16(mask, value):
    return jnp.where(mask, value, 0.0).astype(jnp.bfloat16)


def rows_of(ref, group, x):
    return ref[pl.ds(group * 64 + x, 8, stride=8), :]


def coeff_rows(m_ref, x):
    return jnp.where(rows_of(m_ref, 0, x) == 1, 1.0, 0.05).astype(F32)


def edge_kernel(f_hbm, m_hbm, left_ref, right_ref, f_ref, m_ref, sems):
    step = f_ref.shape[0] // VEC
    copies = [pltpu.make_async_copy(f_hbm.at[pl.ds(step * v, step)], f_ref.at[pl.ds(step * v, step)], sems.at[v]) for v in range(VEC)]
    copies.append(pltpu.make_async_copy(m_hbm, m_ref, sems.at[VEC]))
    for copy in copies:
        copy.start()
    for v in range(VEC):
        copies[v].wait()
        for x in range(BX):
            for c in range(COMP):
                val = rows_of(f_ref, v * COMP + c, x)
                lanes = pl.ds((x // 4) * 64 + 16 * v, 16)
                left_ref[c * 4 + x % 4, :, lanes] = val[:, :RIM]
                right_ref[c * 4 + x % 4, :, lanes] = val[:, BY - RIM :]
    copies[VEC].wait()
    for x in range(BX):
        val = coeff_rows(m_ref, x)
        left_ref[12, :, pl.ds(16 * x, 16)] = val[:, :RIM]
        right_ref[12, :, pl.ds(16 * x, 16)] = val[:, BY - RIM :]


def at_coeff(base, x):
    piece = 8 + x // 4
    return base + x // 5, 128 * (x % 5), base + piece // 5, 128 * (piece % 5) + 32 * (x % 4)


def place_kernel(f_ref, m_ref, own_ref):
    def put(row, lane, piece_row, piece_lane, val):
        own_ref[row, :, pl.ds(lane + LEFT, 128 - LEFT)] = val[:, : 128 - LEFT]
        own_ref[piece_row, :, pl.ds(piece_lane, BY - PIECE)] = val[:, PIECE:]

    for x in range(BX):
        for c in range(COMP):
            for v in range(VEC):
                put(BX * c + x, 128 * v, BX * c + x, 512 + 32 * v, rows_of(f_ref, v * COMP + c, x))
        put(*at_coeff(COMP * BX, x), coeff_rows(m_ref, x))


def join_kernel(gy, placed_ref, l_ref, r_ref, own_ref, left_ref, right_ref):
    place = lax.axis_index("gy")
    from_left = (place > 0).astype(F32)
    from_right = (place < gy - 1).astype(F32)
    kept = BY - PIECE
    for i in range(COMP * BX + 2):
        own_ref[i] = placed_ref[i]

    def put(row, lane, piece_row, piece_lane, left, right):
        own_ref[row, :, pl.ds(lane, LEFT)] = left[:, RIM - LEFT :]
        own_ref[piece_row, :, pl.ds(piece_lane + kept, 32 - kept)] = right[:, : 32 - kept]

    for x in range(BX):
        for c in range(COMP):
            left = l_ref[c * 4 + x % 4] * from_left
            right = r_ref[c * 4 + x % 4] * from_right
            for v in range(VEC):
                at = (x // 4) * 64 + 16 * v
                put(BX * c + x, 128 * v, BX * c + x, 512 + 32 * v, left[:, at : at + RIM], right[:, at : at + RIM])
        left = l_ref[12, :, pl.ds(16 * x, 16)] * from_left
        right = r_ref[12, :, pl.ds(16 * x, 16)] * from_right
        put(*at_coeff(COMP * BX, x), left, right)
    for c in range(COMP):
        for x in range(FX):
            left_ref[c * FX + x] = own_ref[BX * c + x]
            right_ref[c * FX + x] = own_ref[BX * c + x + BX - FX]
    for i in range(2):
        left_ref[COMP * FX + i] = own_ref[COMP * BX + i]
        right_ref[COMP * FX + i] = own_ref[COMP * BX + i]


def down_kernel(
    gx, own_ref, l_ref, r_ref,
    pay_ref, send_l, send_r, x1_ref, x2_ref, c0_ref, y1, y2_ref, k1,
    x1, x2, k0, y2, cx, dr0, t0, p0, rest, stack, cstack, c1, dr1, f1, t1, p1, r1, stack1, pay, many, sems,
):
    place = lax.axis_index("gx")
    from_left = (place > 0).astype(F32)
    from_right = (place < gx - 1).astype(F32)
    a = Level(0, 1, 128, (0, 0, 0, 0, 1))

    def spread(plane, ref, base, x, factor):
        row, lane, piece_row, piece_lane = at_coeff(base, x)
        val = ref[row, :, pl.ds(lane, 128)]
        end = ref[piece_row, :, pl.ds(piece_lane, 32)]
        if factor is not None:
            val, end = val * factor, end * factor
        cx[plane + CX, :, pl.ds(0, 128)] = val
        for v in range(VEC):
            cx[plane + CX, :, pl.ds(128 + 32 * v, 32)] = end

    for x in range(BX):
        spread(x, own_ref, COMP * BX, x, None)
    for x in range(CX):
        spread(x - CX, l_ref, COMP * FX, x + BX - CX, from_left)
        spread(x + BX, r_ref, COMP * FX, x, from_right)

    def start(low, high, load):
        def body(p):
            gain, back = a.weights(cx, p + CX, k0, p + FX)
            for kind in range(2):
                dr0[p + FX, :, a.lanes(kind)] = back[kind]
            for c in range(COMP):
                plane = load(c, p)
                for tile, kind in enumerate(a.kinds):
                    x1[c, p + FX, :, a.lanes(tile)] = gain[kind] * plane[:, 128 * tile : 128 * tile + 128]

        each(low, high, 4, body)

    start(-FX, 0, lambda c, p: l_ref[c * FX + p + FX])
    start(0, BX, lambda c, p: own_ref[BX * c + p])
    start(BX, BX + FX, lambda c, p: r_ref[c * FX + p - BX])

    def to_x2(c, p, tile, lanes, d):
        x2[c, p + FX, :, lanes] = x1[c, p + FX, :, lanes] + d

    a.apply(x1, FX, t0, p0, k0, FX, x1, FX, 1 - FX, BX + FX - 1, UNROLL0, to_x2)

    def to_rest(c, p, tile, lanes, d):
        rest[c, p + 4, :, lanes] = d * dr0[p + FX, :, a.lanes(a.kinds[tile])]

    a.apply(x2, FX, t0, p0, k0, FX, x1, FX, -4, BX + 4, UNROLL0, to_rest)

    for c in range(COMP):
        for i in range(8):
            plane = rest[c, 2 * i] + rest[c, 2 * i + 1]
            stack[pl.ds(64 * c + 8 * i, 8), :] = plane + a.zp(plane)
    for i in range(10):
        plane = cx[2 * i + 1] + cx[2 * i + 2]
        cstack[pl.ds(8 * i, 8), :] = plane + a.zp(plane)
    selectors = []
    row, col = iota((K0, 128), 0), iota((K0, 128), 1)
    y, y_piece, vec = tile_y(row)
    for v in range(VEC):
        own_tile = (row < 128) & (y >= -10) & (y < SPLIT) & ((y >> 1) + 32 == col)
        piece = (row >= 128) & (vec == v) & (y_piece >= SPLIT) & (y_piece < BY + 10) & ((y_piece >> 1) + 32 == col)
        selectors.append(bf16(own_tile | piece, 0.125))
    parts = parts_of(stack[...])
    coarse = [
        exact_dot([jnp.concatenate([p[:, 128 * v : 128 * v + 128], p[:, 512:]], axis=1) for p in parts], selectors[v])
        for v in range(VEC)
    ]
    coarse_c = exact_dot(parts_of(cstack[...]), selectors[0])
    even = (iota((8, 128), 0) & 1) == 0
    for c in range(COMP):
        for i in range(8):
            at = 64 * c + 8 * i
            for low in range(2):
                odd = pltpu.roll(coarse[2 + low][at : at + 8], 1, 0)
                f1[c, i, :, pl.ds(128 * low, 128)] = jnp.where(even, coarse[low][at : at + 8], odd)
    for i in range(10):
        block = coarse_c[8 * i : 8 * i + 8]
        c1[i] = jnp.where(even, block, pltpu.roll(block, 1, 0))

    b = Level(1, 2, 128, (0, 0))
    for p in range(-2, 6):
        gain, back = b.weights(c1, p + 3, k1, p + 2)
        dr1[p + 2] = back[0]
        for c in range(COMP):
            for tile in range(2):
                y1[c, p + 2, :, b.lanes(tile)] = gain[0] * f1[c, p + 2, :, b.lanes(tile)]

    def to_y2(c, p, tile, lanes, d):
        y2[c, p + 1, :, lanes] = y1[c, p + 2, :, lanes] + d

    b.apply(y1, 2, t1, p1, k1, 2, y1, 2, -1, 5, UNROLL1, to_y2)
    for c in range(COMP):
        for i in range(3):
            send_l[3 * c + i] = y2[c, 1 + i]
            send_r[3 * c + i] = y2[c, 2 + i]

    def to_r1(c, p, tile, lanes, d):
        r1[c, p, :, lanes] = d * dr1[p + 2]

    b.apply(y2, 1, t1, p1, k1, 2, y1, 2, 0, 4, UNROLL1, to_r1)

    for c in range(COMP):
        for i in range(2):
            plane = r1[c, 2 * i] + r1[c, 2 * i + 1]
            plane = plane + pltpu.roll(plane, 6, 0)
            stack1[pl.ds(8 * (2 * c + i), 8), :] = plane[:, :128]
            stack1[pl.ds(64 + 8 * (2 * c + i), 8), :] = plane[:, 128:]
    for i in range(2):
        plane = c1[2 * i + 3] + c1[2 * i + 4]
        plane = plane + b.zp(plane)
        stack1[pl.ds(8 * (6 + i), 8), :] = plane
        stack1[pl.ds(64 + 8 * (6 + i), 8), :] = plane
    lane = iota((128, 128), 0) - 32
    selector1 = bf16((lane >> 1 == iota((128, 128), 1)) & (lane >= 0) & (lane < 64), 0.125)
    coarse1 = exact_dot(parts_of(stack1[...]), selector1)
    first = (iota((8, 32), 0) & 2) == 0
    blocks = []
    for g in range(8):
        low = coarse1[8 * g : 8 * g + 8]
        high = pltpu.roll(coarse1[64 + 8 * g : 72 + 8 * g], 2, 0)
        blocks.append(jnp.where(first, low[:, :32], high[:, :32]))
    for g in range(4):
        pay[pl.ds(0, 8), pl.ds(32 * g, 32)] = blocks[g]
    for g in range(2):
        pay[pl.ds(8, 4), pl.ds(32 * g, 32)] = blocks[4 + g][:4]
        pay[pl.ds(8, 4), pl.ds(64 + 32 * g, 32)] = blocks[4 + g][4:]
        pay[pl.ds(12, 1), pl.ds(64 * g, 32)] = blocks[6 + g][:1]
        pay[pl.ds(12, 1), pl.ds(64 * g + 32, 32)] = blocks[6 + g][4:5]
    batch = many.shape[0]
    for r in range(PAY):
        row = pay[pl.ds(r, 1), :]
        for i in range(batch):
            many[i, :, pl.ds(128 * r, 128)] = row
    copies = []
    for i in range(pay_ref.shape[0] // batch):
        copies.append(pltpu.make_async_copy(many, pay_ref.at[pl.ds(batch * i, batch)], sems.at[i]))
        copies[-1].start()
    for c in range(COMP):
        for i in range(10):
            x1_ref[c, i] = x1[c, i + 5]
        for i in range(12):
            x2_ref[c, i] = x2[c, i + 4]
        for i in range(4):
            y2_ref[c, i] = y2[c, i + 1]
    for i in range(12):
        c0_ref[i] = cx[i + 5]
    for copy in copies:
        copy.wait()


def up_kernel(
    gx, gy, got_ref, l_ref, r_ref, x1, x2, c0_ref, y1, y2, k1, out_ref,
    c2, f2, k2, dr2, x1c, ua, ub, rc, t2, p2, s2, c3, k3, x1d, va, vb, t3, p3, s3, sw, w0, w1, t1, p1, sp, k0, u0, u1, t0, p0, gs,
):
    nx2, nx3 = 2 * gx, gx
    yy2, l3 = 32 * gy, c3.shape[-1]
    place_x = lax.axis_index("gx")
    place_y = lax.axis_index("gy")
    from_left = (place_x > 0).astype(F32)
    from_right = (place_x < gx - 1).astype(F32)

    zero2 = jnp.zeros((8, yy2), F32)
    for ref in (ua, ub):
        for c in range(COMP):
            for i in (0, 1, nx2 + 2, nx2 + 3):
                ref[c, i] = zero2
    c2[0] = zero2
    c2[nx2 + 1] = zero2

    def unpack(i):
        for j in range(gy):
            at, lanes = i * gy + j, pl.ds(32 * j, 32)
            for r in range(PAY - 1):
                gs[at, pl.ds(r, 1), :] = got_ref[at, :, pl.ds(128 * r, 128)]
            for g in range(4):
                f2[g // 2, 2 * i + g % 2, :, lanes] = gs[at, pl.ds(0, 8), pl.ds(32 * g, 32)]
            for g in range(2):
                for half in range(2):
                    f2[2, 2 * i + g, pl.ds(4 * half, 4), lanes] = gs[at, pl.ds(8, 4), pl.ds(64 * half + 32 * g, 32)]
                    row = got_ref[at, :, pl.ds(128 * (PAY - 1) + 64 * g + 32 * half, 32)]
                    c2[2 * i + g + 1, pl.ds(4 * half, 4), lanes] = jnp.broadcast_to(row, (4, 32))

    each(0, gx, 8, unpack)
    m = Level(2, 4, yy2, (0,), yy2)

    def start2(p):
        gain, back = m.weights(c2, p + 1, k2, p)
        dr2[p] = back[0]
        for c in range(COMP):
            val = gain[0] * f2[c, p]
            x1c[c, p] = val
            ua[c, p + 2] = val

    each(0, nx2, 8, start2)

    def sweep2(src, dst):
        def write(c, p, tile, lanes, d):
            dst[c, p + 2] = src[c, p + 2] + d

        m.apply(src, 2, t2, p2, k2, 0, x1c, 0, 0, nx2, UNROLL2, write)

    sweep2(ua, ub)

    def to_rc(c, p, tile, lanes, d):
        rc[c, p] = d * dr2[p]

    m.apply(ub, 2, t2, p2, k2, 0, x1c, 0, 0, nx2, UNROLL2, to_rc)

    for i in range(nx3):
        for c in range(COMP):
            plane = rc[c, 2 * i] + rc[c, 2 * i + 1]
            s2[pl.ds(8 * (c * nx3 + i), 8), :] = plane + pltpu.roll(plane, 4, 0)
        plane = c2[2 * i + 1] + c2[2 * i + 2]
        s2[pl.ds(8 * (COMP * nx3 + i), 8), :] = plane + pltpu.roll(plane, 4, 0)
    selector = bf16((iota((yy2, l3), 0) >> 1) == iota((yy2, l3), 1), 0.125)
    coarse = exact_dot(parts_of(s2[...]), selector)
    zero3 = jnp.zeros((8, l3), F32)
    for ref in (va, vb):
        for c in range(COMP):
            ref[c, 0] = zero3
            ref[c, nx3 + 1] = zero3
    c3[0] = zero3
    c3[nx3 + 1] = zero3
    for i in range(nx3):
        c3[i + 1] = coarse[8 * (COMP * nx3 + i) : 8 * (COMP * nx3 + i) + 8]
    n = Level(3, 8, l3, (0,), 16 * gy)
    a = Level(0, 1, 128, (0, 0, 0, 0, 1))
    for p in range(nx3):
        gain, _ = n.weights(c3, p + 1, k3, p)
        for c in range(COMP):
            val = gain[0] * coarse[8 * (c * nx3 + p) : 8 * (c * nx3 + p) + 8]
            x1d[c, p] = val
            va[c, p + 1] = val
    src, dst = va, vb
    for sweep in range(COARSE - 1):

        def write3(c, p, tile, lanes, d, src=src, dst=dst):
            dst[c, p + 1] = src[c, p + 1] + d

        n.apply(src, 1, t3, p3, k3, 0, x1d, 0, 0, nx3, UNROLL2, write3)
        for p in (2 * sweep - 1, 2 * sweep):
            a.weights(c0_ref, p + 2, k0, p + 1)
        src, dst = dst, src
    for c in range(COMP):
        for i in range(nx3):
            s3[pl.ds(8 * (c * nx3 + i), 8), :] = src[c, i + 1]
    selector = bf16((iota((l3, yy2), 1) >> 1) == iota((l3, yy2), 0), 1.0)
    fine = exact_dot(parts_of(s3[...]), selector)
    for c in range(COMP):
        for i in range(nx3):
            block = fine[8 * (c * nx3 + i) : 8 * (c * nx3 + i) + 8]
            for j in range(2):
                ub[c, 2 * i + j + 2] = ub[c, 2 * i + j + 2] + block
    sweep2(ub, ua)
    sweep2(ua, ub)

    row = iota((8, yy2), 0)
    for c in range(COMP):
        for i in range(6):
            e = ub[c, 2 * place_x + i]
            at = 16 * (6 * c + i)
            sw[pl.ds(at, 8), :] = jnp.where((row & 2) == 0, e, pltpu.roll(e, 2, 0))
            sw[pl.ds(at + 8, 8), :] = jnp.where((row & 2) != 0, e, pltpu.roll(e, 6, 0))
    y1g = place_y * 64 + iota((yy2, 128), 1) - 32
    fine = exact_dot(parts_of(sw[...]), bf16((y1g >> 1) == iota((yy2, 128), 0), 1.0))
    for c in range(COMP):
        for p in range(-3, 7):
            if p < 0:
                val = l_ref[3 * c + p + 3] * from_left
            elif p < 4:
                val = y2[c, p]
            else:
                val = r_ref[3 * c + p - 4] * from_right
            at = 16 * (6 * c + (p + 4) // 2)
            w0[c, p + 3] = val + jnp.concatenate([fine[at : at + 8], fine[at + 8 : at + 16]], axis=1)
    b = Level(1, 2, 128, (0, 0))

    def write1(c, p, tile, lanes, d):
        w1[c, p + 3, :, lanes] = w0[c, p + 3, :, lanes] + d

    b.apply(w0, 3, t1, p1, k1, 2, y1, 2, -2, 6, UNROLL1, write1)
    odd = (iota((8, 128), 0) & 1) != 0

    def write1b(c, p, tile, lanes, d):
        e = w1[c, p + 3, :, lanes] + d
        rows = pl.ds(8 * (6 * c + p + 1), 8)
        sp[tile, rows, :] = jnp.where(odd, pltpu.roll(e, 1, 0), e)
        sp[2 + tile, rows, :] = jnp.where(odd, e, pltpu.roll(e, 7, 0))

    b.apply(w1, 3, t1, p1, k1, 2, y1, 2, -1, 5, 6, write1b)

    col = iota((128, K0), 1)
    y, y_piece, vec = tile_y(col)
    piece = None
    for v in range(VEC):
        parent = jnp.where(col < 128, y >> 1, y_piece >> 1) + 32
        selector = bf16((parent == iota((128, K0), 0)) & ((col < 128) | (vec == v)), 1.0)
        fine = exact_dot(parts_of(sp[v]), selector)
        piece = fine[:, 128:] if v == 0 else piece + fine[:, 128:]
        for c in range(COMP):
            for i in range(6):
                at = 8 * (6 * c + i)
                for j in range(2):
                    u0[c, 2 * i + j, :, pl.ds(128 * v, 128)] = x2[c, 2 * i + j, :, pl.ds(128 * v, 128)] + fine[at : at + 8, :128]
    for c in range(COMP):
        for i in range(6):
            at = 8 * (6 * c + i)
            for j in range(2):
                u0[c, 2 * i + j, :, pl.ds(512, 128)] = x2[c, 2 * i + j, :, pl.ds(512, 128)] + piece[at : at + 8]

    def write0(c, p, tile, lanes, d):
        u1[c, p + 2, :, lanes] = u0[c, p + 2, :, lanes] + d

    a.apply(u0, 2, t0, p0, k0, 1, x1, 1, -1, 9, UNROLL0, write0)

    def write_last(c, p, tile, lanes, d):
        u0[c, p + 2, :, lanes] = u1[c, p + 2, :, lanes] + d

    a.apply(u1, 2, t0, p0, k0, 1, x1, 1, 0, BX, UNROLL0, write_last)
    near = iota((8, 128), 1) < SPLIT
    for x in range(BX):
        for c in range(COMP):
            last = u0[c, x + 2, :, pl.ds(512, 128)]
            for v in range(VEC):
                main = pltpu.roll(u0[c, x + 2, :, pl.ds(128 * v, 128)], 128 - LEFT, 1)
                ends = pltpu.roll(last, (PIECE - 32 * v) % 128, 1)
                out_ref[pl.ds((v * COMP + c) * 64 + x, 8, stride=8), :] = jnp.where(near, main, ends)


def call(kernel, outs, scratch, *args, far=False):
    vmem = pl.BlockSpec(memory_space=pltpu.VMEM)
    shapes = [jax.ShapeDtypeStruct(s, F32) for s in outs]
    return pl.pallas_call(
        kernel,
        out_shape=shapes,
        in_specs=[vmem] * len(args),
        out_specs=[pl.BlockSpec(memory_space=pltpu.HBM) if far and i == 0 else vmem for i in range(len(outs))],
        scratch_shapes=[pltpu.VMEM(s, F32) if isinstance(s, tuple) else s for s in scratch],
        compiler_params=pltpu.CompilerParams(vmem_limit_bytes=48 * 1024 * 1024),
    )(*args)


def per_device(gx, gy, right_side, material):
    def ring(value, axis, size, step):
        return lax.ppermute(value, axis, [(i, (i + step) % size) for i in range(size)])

    f = right_side.reshape(VEC * COMP * NZ * BX, BY)
    m = material.reshape(NZ * BX, BY)
    edge = (13, 8, 128)
    hbm, vmem = pl.BlockSpec(memory_space=pltpu.HBM), pl.BlockSpec(memory_space=pltpu.VMEM)
    to_left, to_right = pl.pallas_call(
        edge_kernel,
        out_shape=[jax.ShapeDtypeStruct(s, F32) for s in (edge, edge)],
        in_specs=[hbm] * 2,
        out_specs=[vmem] * 2,
        scratch_shapes=[pltpu.VMEM(f.shape, F32), pltpu.VMEM(m.shape, jnp.int32), pltpu.SemaphoreType.DMA((VEC + 1,))],
        compiler_params=pltpu.CompilerParams(vmem_limit_bytes=65126 * 1024),
    )(f, m)
    right = ring(to_left, "gy", gy, -1)
    left = ring(to_right, "gy", gy, 1)
    side = (COMP * FX + 2, 8, L0)
    whole = (COMP * BX + 2, 8, L0)
    (own,) = call(place_kernel, [whole], [], f, m)
    own, to_left, to_right = call(functools.partial(join_kernel, gy), [whole, side, side], [], own, left, right)
    right = ring(to_left, "gx", gx, -1)
    left = ring(to_right, "gx", gx, 1)
    n = gx * gy
    plane = lambda *lead: (*lead, 8, L0)
    plane1 = lambda *lead: (*lead, 8, L1)
    nf, nc = BX + 2 * FX, BX + 2 * CX
    pay, to_left, to_right, *kept = call(
        functools.partial(down_kernel, gx),
        [
            (n, 1, 128 * PAY), plane1(9), plane1(9), plane(3, 10), plane(3, 12), (12, 8, K0), plane1(3, 8), plane1(3, 4), (13, 8, 8, 128),
        ],
        [
            plane(3, nf), plane(3, nf), (13, nf, 8, K0), plane1(3, 6),
            (nc, 8, K0), (nf, 8, K0), plane(nf), plane(nf), plane(3, 16), (192, L0), (80, K0), (10, 8, 128),
            (8, 8, 128), plane1(3, 8), plane1(10), plane1(10), plane1(3, 4), (128, 128), (16, 128), (8, 1, 128 * PAY), pltpu.SemaphoreType.DMA((n // 8,)),
        ],
        own, left, right, far=True,
    )
    right = ring(to_left, "gx", gx, -1)
    left = ring(to_right, "gx", gx, 1)
    got = lax.all_to_all(pay, ("gx", "gy"), 0, 0)
    nx2, nx3, y2, l3 = 2 * gx, gx, 32 * gy, max(128, 16 * gy)
    plane2 = lambda *lead: (*lead, 8, y2)
    plane3 = lambda *lead: (*lead, 8, l3)
    (out,) = call(
        functools.partial(up_kernel, gx, gy),
        [(VEC * COMP * NZ * BX, BY)],
        [
            plane2(nx2 + 2), plane2(3, nx2), plane2(13, nx2), plane2(nx2), plane2(3, nx2), plane2(3, nx2 + 4), plane2(3, nx2 + 4),
            plane2(3, nx2), plane2(nx2 + 2), plane2(nx2 + 2), (32 * nx3, y2),
            plane3(nx3 + 2), plane3(13, nx3), plane3(3, nx3), plane3(3, nx3 + 2), plane3(3, nx3 + 2), plane3(nx3 + 2), plane3(nx3 + 2),
            (24 * nx3, l3), (288, y2), plane1(3, 10), plane1(3, 10), plane1(10), plane1(10), (4, 144, 128), (13, 10, 8, K0),
            plane(3, 12), plane(3, 12), plane(12), plane(12), (n, 16, 128),
        ],
        got, left, right, *kept,
    )
    return out.reshape(right_side.shape)


def solution(mesh):
    gx, gy = mesh.shape["gx"], mesh.shape["gy"]
    spec = P(None, None, None, "gx", "gy")
    return jax.shard_map(
        functools.partial(per_device, gx, gy), mesh=mesh, in_specs=(spec, P(None, "gx", "gy")), out_specs=spec, check_vma=False
    )
```

```python
import functools

import jax
import jax.numpy as jnp
from jax import lax
from jax.experimental import pallas as pl
from jax.experimental.pallas import tpu as pltpu
from jax.sharding import PartitionSpec as P

RELAX = 0.6
MASS = 0.01
GRAD_DIV = 2.5
VEC, COMP, NZ, BX, BY = 4, 3, 8, 8, 128
COARSE = 6
UNROLL0, UNROLL1, UNROLL2 = 20, 8, 16
RIM = 16
LEFT = 11
PIECE = 108
SPLIT = 112
L0 = 5 * 128
K0 = 2 * 128
PAY = 13
L1 = 2 * 128
FX = 6
CX = 7
F32 = jnp.float32


def iota(shape, dim):
    return lax.broadcasted_iota(jnp.int32, shape, dim)


def parts_of(value):
    high = value.astype(jnp.bfloat16)
    rest = value - high.astype(F32)
    mid = rest.astype(jnp.bfloat16)
    return high, mid, (rest - mid.astype(F32)).astype(jnp.bfloat16)


def exact_dot(parts, selector):
    out = [jnp.dot(p, selector, preferred_element_type=F32) for p in parts]
    return out[0] + out[1] + out[2]


class Level:
    def __init__(self, index, rows, width, kinds, length=None):
        self.scale = 0.25**index
        self.rows = rows
        self.width = width
        self.kinds = kinds
        row = iota((8, width), 0)
        self.has_zp, self.has_zm = row < 8 - rows, row >= rows
        self.has_yp = self.has_ym = None
        if length is not None:
            lane = iota((8, width), 1)
            self.has_yp, self.has_ym = lane < length - 1, lane > 0

    def lanes(self, tile):
        return pl.ds(tile * self.width, self.width)

    def yp(self, a):
        return pltpu.roll(a, self.width - 1, 1)

    def ym(self, a):
        return pltpu.roll(a, 1, 1)

    def zp(self, a):
        return pltpu.roll(a, 8 - self.rows, 0)

    def zm(self, a):
        return pltpu.roll(a, self.rows, 0)

    @staticmethod
    def keep(mask, a):
        return a if mask is None else jnp.where(mask, a, 0.0)

    def dy_of(self, up, down):
        return self.keep(self.has_yp, up) - self.keep(self.has_ym, down)

    def dz_of(self, up, down):
        return self.keep(self.has_zp, up) - self.keep(self.has_zm, down)

    @property
    def layered(self):
        return self.rows < 8

    def weights(self, coeff, at, k_ref, kat):
        gains, backs = [], []
        for kind in range(max(self.kinds) + 1):
            lanes = self.lanes(kind)
            c = coeff[at, :, lanes]
            near = [coeff[at + 1, :, lanes], coeff[at - 1, :, lanes]]
            near += [self.keep(self.has_yp, self.yp(c)), self.keep(self.has_ym, self.ym(c))]
            if self.layered:
                near += [self.keep(self.has_zp, self.zp(c)), self.keep(self.has_zm, self.zm(c))]
            total = near[0]
            for n in near[1:]:
                total = total + n
            diag = MASS + self.scale * (8.0 * c + 0.5 * total)
            gain = jnp.where(c > 0.0, RELAX / diag, 0.0)
            half = (0.5 * self.scale) * gain
            own = (GRAD_DIV * self.scale) * gain * c
            masks = [None, None, self.has_yp, self.has_ym, self.has_zp, self.has_zm]
            for i, n in enumerate(near):
                face = half * (c + n)
                k_ref[i, kat, :, lanes] = self.keep(masks[i], face)
                k_ref[6 + i, kat, :, lanes] = self.keep(masks[i], face + own)
            k_ref[12, kat, :, lanes] = 0.25 * own
            gains.append(gain)
            backs.append(diag * (1.0 / RELAX))
        return gains, backs

    def cross(self, u, at, t_ref, tat):
        for tile in range(len(self.kinds)):
            lanes = self.lanes(tile)
            uy = u[1, at, :, lanes]
            t = self.dy_of(self.yp(uy), self.ym(uy))
            if self.layered:
                uz = u[2, at, :, lanes]
                t = t + self.dz_of(self.zp(uz), self.zm(uz))
            t_ref[tat, :, lanes] = t

    def change(self, u, at, t_ref, px_ref, tat, k_ref, kat, x1, xat, write):
        for tile, kind in enumerate(self.kinds):
            lanes = self.lanes(tile)
            k = lambda i: k_ref[i, kat, :, self.lanes(kind)]
            mine = [u[c, at, :, lanes] for c in range(3)]
            fore = [u[c, at + 1, :, lanes] for c in range(3)]
            back = [u[c, at - 1, :, lanes] for c in range(3)]
            y_up = [self.yp(a) for a in mine]
            y_dn = [self.ym(a) for a in mine]
            dxx = fore[0] - back[0]
            dyy = self.dy_of(y_up[1], y_dn[1])
            side = dxx
            cross = dyy
            if self.layered:
                z_up = [self.zp(a) for a in mine]
                z_dn = [self.zm(a) for a in mine]
                dzz = self.dz_of(z_up[2], z_dn[2])
                side = dxx + dzz
                cross = dyy + dzz
            t_ref[tat, :, lanes] = cross
            mixed = [None, self.dy_of(self.yp(side), self.ym(side)), None]
            if self.layered:
                below = dxx + dyy
                mixed[2] = self.dz_of(self.zp(below), self.zm(below))
            for c in range(3):
                total = x1[c, xat, :, lanes] - RELAX * mine[c]
                total = total + (k(6 if c == 0 else 0) * fore[c] + k(7 if c == 0 else 1) * back[c])
                sides = k(8 if c == 1 else 2) * y_up[c] + k(9 if c == 1 else 3) * y_dn[c]
                if self.layered:
                    sides = sides + (k(10 if c == 2 else 4) * z_up[c] + k(11 if c == 2 else 5) * z_dn[c])
                if mixed[c] is not None:
                    sides = sides + k(12) * mixed[c]
                if c == 0:
                    px_ref[tat, :, lanes] = total + sides
                else:
                    write(c, tile, lanes, total + sides)

    def apply(self, u, uo, t_ref, px_ref, k_ref, ko, x1, xo, low, high, unroll, write):
        self.cross(u, low - 1 + uo, t_ref, 0)
        self.cross(u, high + uo, t_ref, high - low + 1)

        def one(p):
            def put(c, tile, lanes, d):
                write(c, p, tile, lanes, d)

            self.change(u, p + uo, t_ref, px_ref, p - low + 1, k_ref, p + ko, x1, p + xo, put)

        def mixed(p):
            at = p - low + 1
            for tile, kind in enumerate(self.kinds):
                lanes = self.lanes(tile)
                t = t_ref[at + 1, :, lanes] - t_ref[at - 1, :, lanes]
                write(0, p, tile, lanes, px_ref[at, :, lanes] + k_ref[12, p + ko, :, self.lanes(kind)] * t)

        each(low, high, unroll, one)
        each(low, high, 2 * unroll, mixed)


def each(low, high, unroll, body):
    count = high - low
    while count % unroll:
        unroll -= 1
    if count == unroll:
        for p in range(low, high):
            body(p)
        return

    def step(i, carry):
        for b in range(unroll):
            body(low + i * unroll + b)
        return carry

    lax.fori_loop(0, count // unroll, step, 0)


def tile_y(lane):
    return (lane & 127) - LEFT, PIECE + (lane & 31), (lane & 127) >> 5


def bf16(mask, value):
    return jnp.where(mask, value, 0.0).astype(jnp.bfloat16)


def rows_of(ref, group, x):
    return ref[pl.ds(group * 64 + x, 8, stride=8), :]


def edge_kernel(f_ref, left_ref, right_ref):
    for x in range(BX):
        for v in range(VEC):
            for c in range(COMP):
                val = rows_of(f_ref, v * COMP + c, x)
                lanes = pl.ds((x // 4) * 64 + 16 * v, 16)
                left_ref[c * 4 + x % 4, :, lanes] = val[:, :RIM]
                right_ref[c * 4 + x % 4, :, lanes] = val[:, BY - RIM :]
        val = rows_of(f_ref, VEC * COMP, x)
        left_ref[12, :, pl.ds(16 * x, 16)] = val[:, :RIM]
        right_ref[12, :, pl.ds(16 * x, 16)] = val[:, BY - RIM :]


def at_coeff(base, x):
    piece = 8 + x // 4
    return base + x // 5, 128 * (x % 5), base + piece // 5, 128 * (piece % 5) + 32 * (x % 4)


def place_kernel(f_ref, own_ref):
    def put(row, lane, piece_row, piece_lane, val):
        own_ref[row, :, pl.ds(lane + LEFT, 128 - LEFT)] = val[:, : 128 - LEFT]
        own_ref[piece_row, :, pl.ds(piece_lane, BY - PIECE)] = val[:, PIECE:]

    for x in range(BX):
        for c in range(COMP):
            for v in range(VEC):
                put(BX * c + x, 128 * v, BX * c + x, 512 + 32 * v, rows_of(f_ref, v * COMP + c, x))
        put(*at_coeff(COMP * BX, x), rows_of(f_ref, VEC * COMP, x))


def join_kernel(gy, placed_ref, l_ref, r_ref, own_ref, left_ref, right_ref):
    place = lax.axis_index("gy")
    from_left = (place > 0).astype(F32)
    from_right = (place < gy - 1).astype(F32)
    kept = BY - PIECE
    for i in range(COMP * BX + 2):
        own_ref[i] = placed_ref[i]

    def put(row, lane, piece_row, piece_lane, left, right):
        own_ref[row, :, pl.ds(lane, LEFT)] = left[:, RIM - LEFT :]
        own_ref[piece_row, :, pl.ds(piece_lane + kept, 32 - kept)] = right[:, : 32 - kept]

    for x in range(BX):
        for c in range(COMP):
            left = l_ref[c * 4 + x % 4] * from_left
            right = r_ref[c * 4 + x % 4] * from_right
            for v in range(VEC):
                at = (x // 4) * 64 + 16 * v
                put(BX * c + x, 128 * v, BX * c + x, 512 + 32 * v, left[:, at : at + RIM], right[:, at : at + RIM])
        left = l_ref[12, :, pl.ds(16 * x, 16)] * from_left
        right = r_ref[12, :, pl.ds(16 * x, 16)] * from_right
        put(*at_coeff(COMP * BX, x), left, right)
    for c in range(COMP):
        for x in range(FX):
            left_ref[c * FX + x] = own_ref[BX * c + x]
            right_ref[c * FX + x] = own_ref[BX * c + x + BX - FX]
    for i in range(2):
        left_ref[COMP * FX + i] = own_ref[COMP * BX + i]
        right_ref[COMP * FX + i] = own_ref[COMP * BX + i]


def down_kernel(
    gx, own_ref, l_ref, r_ref,
    pay_ref, send_l, send_r, x1_ref, x2_ref, c0_ref, y1, y2_ref, k1,
    x1, x2, k0, y2, cx, dr0, t0, p0, rest, stack, cstack, c1, dr1, f1, t1, p1, r1, stack1, pay, many, sems,
):
    place = lax.axis_index("gx")
    from_left = (place > 0).astype(F32)
    from_right = (place < gx - 1).astype(F32)
    a = Level(0, 1, 128, (0, 0, 0, 0, 1))

    def spread(plane, ref, base, x, factor):
        row, lane, piece_row, piece_lane = at_coeff(base, x)
        val = ref[row, :, pl.ds(lane, 128)]
        end = ref[piece_row, :, pl.ds(piece_lane, 32)]
        if factor is not None:
            val, end = val * factor, end * factor
        cx[plane + CX, :, pl.ds(0, 128)] = val
        for v in range(VEC):
            cx[plane + CX, :, pl.ds(128 + 32 * v, 32)] = end

    for x in range(BX):
        spread(x, own_ref, COMP * BX, x, None)
    for x in range(CX):
        spread(x - CX, l_ref, COMP * FX, x + BX - CX, from_left)
        spread(x + BX, r_ref, COMP * FX, x, from_right)

    def start(low, high, load):
        def body(p):
            gain, back = a.weights(cx, p + CX, k0, p + FX)
            for kind in range(2):
                dr0[p + FX, :, a.lanes(kind)] = back[kind]
            for c in range(COMP):
                plane = load(c, p)
                for tile, kind in enumerate(a.kinds):
                    x1[c, p + FX, :, a.lanes(tile)] = gain[kind] * plane[:, 128 * tile : 128 * tile + 128]

        each(low, high, 4, body)

    start(-FX, 0, lambda c, p: l_ref[c * FX + p + FX])
    start(0, BX, lambda c, p: own_ref[BX * c + p])
    start(BX, BX + FX, lambda c, p: r_ref[c * FX + p - BX])

    def to_x2(c, p, tile, lanes, d):
        x2[c, p + FX, :, lanes] = x1[c, p + FX, :, lanes] + d

    a.apply(x1, FX, t0, p0, k0, FX, x1, FX, 1 - FX, BX + FX - 1, UNROLL0, to_x2)

    def to_rest(c, p, tile, lanes, d):
        rest[c, p + 4, :, lanes] = d * dr0[p + FX, :, a.lanes(a.kinds[tile])]

    a.apply(x2, FX, t0, p0, k0, FX, x1, FX, -4, BX + 4, UNROLL0, to_rest)

    for c in range(COMP):
        for i in range(8):
            plane = rest[c, 2 * i] + rest[c, 2 * i + 1]
            stack[pl.ds(64 * c + 8 * i, 8), :] = plane + a.zp(plane)
    for i in range(10):
        plane = cx[2 * i + 1] + cx[2 * i + 2]
        cstack[pl.ds(8 * i, 8), :] = plane + a.zp(plane)
    selectors = []
    row, col = iota((K0, 128), 0), iota((K0, 128), 1)
    y, y_piece, vec = tile_y(row)
    for v in range(VEC):
        own_tile = (row < 128) & (y >= -10) & (y < SPLIT) & ((y >> 1) + 32 == col)
        piece = (row >= 128) & (vec == v) & (y_piece >= SPLIT) & (y_piece < BY + 10) & ((y_piece >> 1) + 32 == col)
        selectors.append(bf16(own_tile | piece, 0.125))
    parts = parts_of(stack[...])
    coarse = [
        exact_dot([jnp.concatenate([p[:, 128 * v : 128 * v + 128], p[:, 512:]], axis=1) for p in parts], selectors[v])
        for v in range(VEC)
    ]
    coarse_c = exact_dot(parts_of(cstack[...]), selectors[0])
    even = (iota((8, 128), 0) & 1) == 0
    for c in range(COMP):
        for i in range(8):
            at = 64 * c + 8 * i
            for low in range(2):
                odd = pltpu.roll(coarse[2 + low][at : at + 8], 1, 0)
                f1[c, i, :, pl.ds(128 * low, 128)] = jnp.where(even, coarse[low][at : at + 8], odd)
    for i in range(10):
        block = coarse_c[8 * i : 8 * i + 8]
        c1[i] = jnp.where(even, block, pltpu.roll(block, 1, 0))

    b = Level(1, 2, 128, (0, 0))
    for p in range(-2, 6):
        gain, back = b.weights(c1, p + 3, k1, p + 2)
        dr1[p + 2] = back[0]
        for c in range(COMP):
            for tile in range(2):
                y1[c, p + 2, :, b.lanes(tile)] = gain[0] * f1[c, p + 2, :, b.lanes(tile)]

    def to_y2(c, p, tile, lanes, d):
        y2[c, p + 1, :, lanes] = y1[c, p + 2, :, lanes] + d

    b.apply(y1, 2, t1, p1, k1, 2, y1, 2, -1, 5, UNROLL1, to_y2)
    for c in range(COMP):
        for i in range(3):
            send_l[3 * c + i] = y2[c, 1 + i]
            send_r[3 * c + i] = y2[c, 2 + i]

    def to_r1(c, p, tile, lanes, d):
        r1[c, p, :, lanes] = d * dr1[p + 2]

    b.apply(y2, 1, t1, p1, k1, 2, y1, 2, 0, 4, UNROLL1, to_r1)

    for c in range(COMP):
        for i in range(2):
            plane = r1[c, 2 * i] + r1[c, 2 * i + 1]
            plane = plane + pltpu.roll(plane, 6, 0)
            stack1[pl.ds(8 * (2 * c + i), 8), :] = plane[:, :128]
            stack1[pl.ds(64 + 8 * (2 * c + i), 8), :] = plane[:, 128:]
    for i in range(2):
        plane = c1[2 * i + 3] + c1[2 * i + 4]
        plane = plane + b.zp(plane)
        stack1[pl.ds(8 * (6 + i), 8), :] = plane
        stack1[pl.ds(64 + 8 * (6 + i), 8), :] = plane
    lane = iota((128, 128), 0) - 32
    selector1 = bf16((lane >> 1 == iota((128, 128), 1)) & (lane >= 0) & (lane < 64), 0.125)
    coarse1 = exact_dot(parts_of(stack1[...]), selector1)
    first = (iota((8, 32), 0) & 2) == 0
    blocks = []
    for g in range(8):
        low = coarse1[8 * g : 8 * g + 8]
        high = pltpu.roll(coarse1[64 + 8 * g : 72 + 8 * g], 2, 0)
        blocks.append(jnp.where(first, low[:, :32], high[:, :32]))
    for g in range(4):
        pay[pl.ds(0, 8), pl.ds(32 * g, 32)] = blocks[g]
    for g in range(2):
        pay[pl.ds(8, 4), pl.ds(32 * g, 32)] = blocks[4 + g][:4]
        pay[pl.ds(8, 4), pl.ds(64 + 32 * g, 32)] = blocks[4 + g][4:]
        pay[pl.ds(12, 1), pl.ds(64 * g, 32)] = blocks[6 + g][:1]
        pay[pl.ds(12, 1), pl.ds(64 * g + 32, 32)] = blocks[6 + g][4:5]
    batch = many.shape[0]
    for r in range(PAY):
        row = pay[pl.ds(r, 1), :]
        for i in range(batch):
            many[i, :, pl.ds(128 * r, 128)] = row
    copies = []
    for i in range(pay_ref.shape[0] // batch):
        copies.append(pltpu.make_async_copy(many, pay_ref.at[pl.ds(batch * i, batch)], sems.at[i]))
        copies[-1].start()
    for c in range(COMP):
        for i in range(10):
            x1_ref[c, i] = x1[c, i + 5]
        for i in range(12):
            x2_ref[c, i] = x2[c, i + 4]
        for i in range(4):
            y2_ref[c, i] = y2[c, i + 1]
    for i in range(12):
        c0_ref[i] = cx[i + 5]
    for copy in copies:
        copy.wait()


def up_kernel(
    gx, gy, got_ref, l_ref, r_ref, x1, x2, c0_ref, y1, y2, k1, out_ref,
    c2, f2, k2, dr2, x1c, ua, ub, rc, t2, p2, s2, c3, k3, x1d, va, vb, t3, p3, s3, sw, w0, w1, t1, p1, sp, k0, u0, u1, t0, p0, gs,
):
    nx2, nx3 = 2 * gx, gx
    yy2, l3 = 32 * gy, c3.shape[-1]
    place_x = lax.axis_index("gx")
    place_y = lax.axis_index("gy")
    from_left = (place_x > 0).astype(F32)
    from_right = (place_x < gx - 1).astype(F32)

    zero2 = jnp.zeros((8, yy2), F32)
    for ref in (ua, ub):
        for c in range(COMP):
            for i in (0, 1, nx2 + 2, nx2 + 3):
                ref[c, i] = zero2
    c2[0] = zero2
    c2[nx2 + 1] = zero2

    def unpack(i):
        for j in range(gy):
            at, lanes = i * gy + j, pl.ds(32 * j, 32)
            for r in range(PAY - 1):
                gs[at, pl.ds(r, 1), :] = got_ref[at, :, pl.ds(128 * r, 128)]
            for g in range(4):
                f2[g // 2, 2 * i + g % 2, :, lanes] = gs[at, pl.ds(0, 8), pl.ds(32 * g, 32)]
            for g in range(2):
                for half in range(2):
                    f2[2, 2 * i + g, pl.ds(4 * half, 4), lanes] = gs[at, pl.ds(8, 4), pl.ds(64 * half + 32 * g, 32)]
                    row = got_ref[at, :, pl.ds(128 * (PAY - 1) + 64 * g + 32 * half, 32)]
                    c2[2 * i + g + 1, pl.ds(4 * half, 4), lanes] = jnp.broadcast_to(row, (4, 32))

    each(0, gx, 8, unpack)
    m = Level(2, 4, yy2, (0,), yy2)

    def start2(p):
        gain, back = m.weights(c2, p + 1, k2, p)
        dr2[p] = back[0]
        for c in range(COMP):
            val = gain[0] * f2[c, p]
            x1c[c, p] = val
            ua[c, p + 2] = val

    each(0, nx2, 8, start2)

    def sweep2(src, dst):
        def write(c, p, tile, lanes, d):
            dst[c, p + 2] = src[c, p + 2] + d

        m.apply(src, 2, t2, p2, k2, 0, x1c, 0, 0, nx2, UNROLL2, write)

    sweep2(ua, ub)

    def to_rc(c, p, tile, lanes, d):
        rc[c, p] = d * dr2[p]

    m.apply(ub, 2, t2, p2, k2, 0, x1c, 0, 0, nx2, UNROLL2, to_rc)

    for i in range(nx3):
        for c in range(COMP):
            plane = rc[c, 2 * i] + rc[c, 2 * i + 1]
            s2[pl.ds(8 * (c * nx3 + i), 8), :] = plane + pltpu.roll(plane, 4, 0)
        plane = c2[2 * i + 1] + c2[2 * i + 2]
        s2[pl.ds(8 * (COMP * nx3 + i), 8), :] = plane + pltpu.roll(plane, 4, 0)
    selector = bf16((iota((yy2, l3), 0) >> 1) == iota((yy2, l3), 1), 0.125)
    coarse = exact_dot(parts_of(s2[...]), selector)
    zero3 = jnp.zeros((8, l3), F32)
    for ref in (va, vb):
        for c in range(COMP):
            ref[c, 0] = zero3
            ref[c, nx3 + 1] = zero3
    c3[0] = zero3
    c3[nx3 + 1] = zero3
    for i in range(nx3):
        c3[i + 1] = coarse[8 * (COMP * nx3 + i) : 8 * (COMP * nx3 + i) + 8]
    n = Level(3, 8, l3, (0,), 16 * gy)
    a = Level(0, 1, 128, (0, 0, 0, 0, 1))
    for p in range(nx3):
        gain, _ = n.weights(c3, p + 1, k3, p)
        for c in range(COMP):
            val = gain[0] * coarse[8 * (c * nx3 + p) : 8 * (c * nx3 + p) + 8]
            x1d[c, p] = val
            va[c, p + 1] = val
    src, dst = va, vb
    for sweep in range(COARSE - 1):

        def write3(c, p, tile, lanes, d, src=src, dst=dst):
            dst[c, p + 1] = src[c, p + 1] + d

        n.apply(src, 1, t3, p3, k3, 0, x1d, 0, 0, nx3, UNROLL2, write3)
        for p in (2 * sweep - 1, 2 * sweep):
            a.weights(c0_ref, p + 2, k0, p + 1)
        src, dst = dst, src
    for c in range(COMP):
        for i in range(nx3):
            s3[pl.ds(8 * (c * nx3 + i), 8), :] = src[c, i + 1]
    selector = bf16((iota((l3, yy2), 1) >> 1) == iota((l3, yy2), 0), 1.0)
    fine = exact_dot(parts_of(s3[...]), selector)
    for c in range(COMP):
        for i in range(nx3):
            block = fine[8 * (c * nx3 + i) : 8 * (c * nx3 + i) + 8]
            for j in range(2):
                ub[c, 2 * i + j + 2] = ub[c, 2 * i + j + 2] + block
    sweep2(ub, ua)
    sweep2(ua, ub)

    row = iota((8, yy2), 0)
    for c in range(COMP):
        for i in range(6):
            e = ub[c, 2 * place_x + i]
            at = 16 * (6 * c + i)
            sw[pl.ds(at, 8), :] = jnp.where((row & 2) == 0, e, pltpu.roll(e, 2, 0))
            sw[pl.ds(at + 8, 8), :] = jnp.where((row & 2) != 0, e, pltpu.roll(e, 6, 0))
    y1g = place_y * 64 + iota((yy2, 128), 1) - 32
    fine = exact_dot(parts_of(sw[...]), bf16((y1g >> 1) == iota((yy2, 128), 0), 1.0))
    for c in range(COMP):
        for p in range(-3, 7):
            if p < 0:
                val = l_ref[3 * c + p + 3] * from_left
            elif p < 4:
                val = y2[c, p]
            else:
                val = r_ref[3 * c + p - 4] * from_right
            at = 16 * (6 * c + (p + 4) // 2)
            w0[c, p + 3] = val + jnp.concatenate([fine[at : at + 8], fine[at + 8 : at + 16]], axis=1)
    b = Level(1, 2, 128, (0, 0))

    def write1(c, p, tile, lanes, d):
        w1[c, p + 3, :, lanes] = w0[c, p + 3, :, lanes] + d

    b.apply(w0, 3, t1, p1, k1, 2, y1, 2, -2, 6, UNROLL1, write1)
    odd = (iota((8, 128), 0) & 1) != 0

    def write1b(c, p, tile, lanes, d):
        e = w1[c, p + 3, :, lanes] + d
        rows = pl.ds(8 * (6 * c + p + 1), 8)
        sp[tile, rows, :] = jnp.where(odd, pltpu.roll(e, 1, 0), e)
        sp[2 + tile, rows, :] = jnp.where(odd, e, pltpu.roll(e, 7, 0))

    b.apply(w1, 3, t1, p1, k1, 2, y1, 2, -1, 5, 6, write1b)

    col = iota((128, K0), 1)
    y, y_piece, vec = tile_y(col)
    piece = None
    for v in range(VEC):
        parent = jnp.where(col < 128, y >> 1, y_piece >> 1) + 32
        selector = bf16((parent == iota((128, K0), 0)) & ((col < 128) | (vec == v)), 1.0)
        fine = exact_dot(parts_of(sp[v]), selector)
        piece = fine[:, 128:] if v == 0 else piece + fine[:, 128:]
        for c in range(COMP):
            for i in range(6):
                at = 8 * (6 * c + i)
                for j in range(2):
                    u0[c, 2 * i + j, :, pl.ds(128 * v, 128)] = x2[c, 2 * i + j, :, pl.ds(128 * v, 128)] + fine[at : at + 8, :128]
    for c in range(COMP):
        for i in range(6):
            at = 8 * (6 * c + i)
            for j in range(2):
                u0[c, 2 * i + j, :, pl.ds(512, 128)] = x2[c, 2 * i + j, :, pl.ds(512, 128)] + piece[at : at + 8]

    def write0(c, p, tile, lanes, d):
        u1[c, p + 2, :, lanes] = u0[c, p + 2, :, lanes] + d

    a.apply(u0, 2, t0, p0, k0, 1, x1, 1, -1, 9, UNROLL0, write0)

    def write_last(c, p, tile, lanes, d):
        u0[c, p + 2, :, lanes] = u1[c, p + 2, :, lanes] + d

    a.apply(u1, 2, t0, p0, k0, 1, x1, 1, 0, BX, UNROLL0, write_last)
    near = iota((8, 128), 1) < SPLIT
    for x in range(BX):
        for c in range(COMP):
            last = u0[c, x + 2, :, pl.ds(512, 128)]
            for v in range(VEC):
                main = pltpu.roll(u0[c, x + 2, :, pl.ds(128 * v, 128)], 128 - LEFT, 1)
                ends = pltpu.roll(last, (PIECE - 32 * v) % 128, 1)
                out_ref[pl.ds((v * COMP + c) * 64 + x, 8, stride=8), :] = jnp.where(near, main, ends)


def call(kernel, outs, scratch, *args, far=False):
    vmem = pl.BlockSpec(memory_space=pltpu.VMEM)
    shapes = [jax.ShapeDtypeStruct(s, F32) for s in outs]
    return pl.pallas_call(
        kernel,
        out_shape=shapes,
        in_specs=[vmem] * len(args),
        out_specs=[pl.BlockSpec(memory_space=pltpu.HBM) if far and i == 0 else vmem for i in range(len(outs))],
        scratch_shapes=[pltpu.VMEM(s, F32) if isinstance(s, tuple) else s for s in scratch],
        compiler_params=pltpu.CompilerParams(vmem_limit_bytes=48 * 1024 * 1024),
    )(*args)


def per_device(gx, gy, right_side, material):
    def ring(value, axis, size, step):
        return lax.ppermute(value, axis, [(i, (i + step) % size) for i in range(size)])

    f = right_side.reshape(VEC * COMP * NZ * BX, BY)
    rows = f.shape[0]
    m = jnp.pad(material.reshape(NZ * BX, BY), ((rows, 0), (0, 0)))
    coeff = jnp.where(m == 1, 1.0, 0.05).astype(F32)
    f = jnp.where(iota((rows + NZ * BX, BY), 0) < rows, jnp.pad(f, ((0, NZ * BX), (0, 0))), coeff)
    edge = (13, 8, 128)
    to_left, to_right = call(edge_kernel, [edge, edge], [], f)
    right = ring(to_left, "gy", gy, -1)
    left = ring(to_right, "gy", gy, 1)
    side = (COMP * FX + 2, 8, L0)
    whole = (COMP * BX + 2, 8, L0)
    (own,) = call(place_kernel, [whole], [], f)
    own, to_left, to_right = call(functools.partial(join_kernel, gy), [whole, side, side], [], own, left, right)
    right = ring(to_left, "gx", gx, -1)
    left = ring(to_right, "gx", gx, 1)
    n = gx * gy
    plane = lambda *lead: (*lead, 8, L0)
    plane1 = lambda *lead: (*lead, 8, L1)
    nf, nc = BX + 2 * FX, BX + 2 * CX
    pay, to_left, to_right, *kept = call(
        functools.partial(down_kernel, gx),
        [
            (n, 1, 128 * PAY), plane1(9), plane1(9), plane(3, 10), plane(3, 12), (12, 8, K0), plane1(3, 8), plane1(3, 4), (13, 8, 8, 128),
        ],
        [
            plane(3, nf), plane(3, nf), (13, nf, 8, K0), plane1(3, 6),
            (nc, 8, K0), (nf, 8, K0), plane(nf), plane(nf), plane(3, 16), (192, L0), (80, K0), (10, 8, 128),
            (8, 8, 128), plane1(3, 8), plane1(10), plane1(10), plane1(3, 4), (128, 128), (16, 128), (8, 1, 128 * PAY), pltpu.SemaphoreType.DMA((n // 8,)),
        ],
        own, left, right, far=True,
    )
    right = ring(to_left, "gx", gx, -1)
    left = ring(to_right, "gx", gx, 1)
    got = lax.all_to_all(pay, ("gx", "gy"), 0, 0)
    nx2, nx3, y2, l3 = 2 * gx, gx, 32 * gy, max(128, 16 * gy)
    plane2 = lambda *lead: (*lead, 8, y2)
    plane3 = lambda *lead: (*lead, 8, l3)
    (out,) = call(
        functools.partial(up_kernel, gx, gy),
        [(VEC * COMP * NZ * BX, BY)],
        [
            plane2(nx2 + 2), plane2(3, nx2), plane2(13, nx2), plane2(nx2), plane2(3, nx2), plane2(3, nx2 + 4), plane2(3, nx2 + 4),
            plane2(3, nx2), plane2(nx2 + 2), plane2(nx2 + 2), (32 * nx3, y2),
            plane3(nx3 + 2), plane3(13, nx3), plane3(3, nx3), plane3(3, nx3 + 2), plane3(3, nx3 + 2), plane3(nx3 + 2), plane3(nx3 + 2),
            (24 * nx3, l3), (288, y2), plane1(3, 10), plane1(3, 10), plane1(10), plane1(10), (4, 144, 128), (13, 10, 8, K0),
            plane(3, 12), plane(3, 12), plane(12), plane(12), (n, 16, 128),
        ],
        got, left, right, *kept,
    )
    return out.reshape(right_side.shape)


def solution(mesh):
    gx, gy = mesh.shape["gx"], mesh.shape["gy"]
    spec = P(None, None, None, "gx", "gy")
    return jax.shard_map(
        functools.partial(per_device, gx, gy), mesh=mesh, in_specs=(spec, P(None, "gx", "gy")), out_specs=spec, check_vma=False
    )
```

```python
import functools

import jax
import jax.numpy as jnp
from jax import lax
from jax.experimental import pallas as pl
from jax.experimental.pallas import tpu as pltpu
from jax.sharding import PartitionSpec as P

RELAX = 0.6
MASS = 0.01
GRAD_DIV = 2.5
VEC, COMP, NZ, BX, BY = 4, 3, 8, 8, 128
COARSE = 6
UNROLL0, UNROLL1, UNROLL2 = 20, 8, 16
RIM = 16
LEFT = 11
PIECE = 108
SPLIT = 112
L0 = 5 * 128
K0 = 2 * 128
PAY = 13
L1 = 2 * 128
FX = 6
CX = 7
F32 = jnp.float32


def iota(shape, dim):
    return lax.broadcasted_iota(jnp.int32, shape, dim)


def parts_of(value):
    high = value.astype(jnp.bfloat16)
    rest = value - high.astype(F32)
    mid = rest.astype(jnp.bfloat16)
    return high, mid, (rest - mid.astype(F32)).astype(jnp.bfloat16)


def exact_dot(parts, selector):
    out = [jnp.dot(p, selector, preferred_element_type=F32) for p in parts]
    return out[0] + out[1] + out[2]


class Level:
    def __init__(self, index, rows, width, kinds, length=None):
        self.scale = 0.25**index
        self.rows = rows
        self.width = width
        self.kinds = kinds
        row = iota((8, width), 0)
        self.has_zp, self.has_zm = row < 8 - rows, row >= rows
        self.has_yp = self.has_ym = None
        if length is not None:
            lane = iota((8, width), 1)
            self.has_yp, self.has_ym = lane < length - 1, lane > 0

    def lanes(self, tile):
        return pl.ds(tile * self.width, self.width)

    def yp(self, a):
        return pltpu.roll(a, self.width - 1, 1)

    def ym(self, a):
        return pltpu.roll(a, 1, 1)

    def zp(self, a):
        return pltpu.roll(a, 8 - self.rows, 0)

    def zm(self, a):
        return pltpu.roll(a, self.rows, 0)

    @staticmethod
    def keep(mask, a):
        return a if mask is None else jnp.where(mask, a, 0.0)

    def dy_of(self, up, down):
        return self.keep(self.has_yp, up) - self.keep(self.has_ym, down)

    def dz_of(self, up, down):
        return self.keep(self.has_zp, up) - self.keep(self.has_zm, down)

    @property
    def layered(self):
        return self.rows < 8

    def weights(self, coeff, at, k_ref, kat):
        gains, backs = [], []
        for kind in range(max(self.kinds) + 1):
            lanes = self.lanes(kind)
            c = coeff[at, :, lanes]
            near = [coeff[at + 1, :, lanes], coeff[at - 1, :, lanes]]
            near += [self.keep(self.has_yp, self.yp(c)), self.keep(self.has_ym, self.ym(c))]
            if self.layered:
                near += [self.keep(self.has_zp, self.zp(c)), self.keep(self.has_zm, self.zm(c))]
            total = near[0]
            for n in near[1:]:
                total = total + n
            diag = MASS + self.scale * (8.0 * c + 0.5 * total)
            gain = jnp.where(c > 0.0, RELAX / diag, 0.0)
            half = (0.5 * self.scale) * gain
            own = (GRAD_DIV * self.scale) * gain * c
            masks = [None, None, self.has_yp, self.has_ym, self.has_zp, self.has_zm]
            for i, n in enumerate(near):
                face = half * (c + n)
                k_ref[i, kat, :, lanes] = self.keep(masks[i], face)
                k_ref[6 + i, kat, :, lanes] = self.keep(masks[i], face + own)
            k_ref[12, kat, :, lanes] = 0.25 * own
            gains.append(gain)
            backs.append(diag * (1.0 / RELAX))
        return gains, backs

    def cross(self, u, at, t_ref, tat):
        for tile in range(len(self.kinds)):
            lanes = self.lanes(tile)
            uy = u[1, at, :, lanes]
            t = self.dy_of(self.yp(uy), self.ym(uy))
            if self.layered:
                uz = u[2, at, :, lanes]
                t = t + self.dz_of(self.zp(uz), self.zm(uz))
            t_ref[tat, :, lanes] = t

    def change(self, u, at, t_ref, px_ref, tat, k_ref, kat, x1, xat, write):
        for tile, kind in enumerate(self.kinds):
            lanes = self.lanes(tile)
            k = lambda i: k_ref[i, kat, :, self.lanes(kind)]
            mine = [u[c, at, :, lanes] for c in range(3)]
            fore = [u[c, at + 1, :, lanes] for c in range(3)]
            back = [u[c, at - 1, :, lanes] for c in range(3)]
            y_up = [self.yp(a) for a in mine]
            y_dn = [self.ym(a) for a in mine]
            dxx = fore[0] - back[0]
            dyy = self.dy_of(y_up[1], y_dn[1])
            side = dxx
            cross = dyy
            if self.layered:
                z_up = [self.zp(a) for a in mine]
                z_dn = [self.zm(a) for a in mine]
                dzz = self.dz_of(z_up[2], z_dn[2])
                side = dxx + dzz
                cross = dyy + dzz
            t_ref[tat, :, lanes] = cross
            mixed = [None, self.dy_of(self.yp(side), self.ym(side)), None]
            if self.layered:
                below = dxx + dyy
                mixed[2] = self.dz_of(self.zp(below), self.zm(below))
            for c in range(3):
                total = x1[c, xat, :, lanes] - RELAX * mine[c]
                total = total + (k(6 if c == 0 else 0) * fore[c] + k(7 if c == 0 else 1) * back[c])
                sides = k(8 if c == 1 else 2) * y_up[c] + k(9 if c == 1 else 3) * y_dn[c]
                if self.layered:
                    sides = sides + (k(10 if c == 2 else 4) * z_up[c] + k(11 if c == 2 else 5) * z_dn[c])
                if mixed[c] is not None:
                    sides = sides + k(12) * mixed[c]
                if c == 0:
                    px_ref[tat, :, lanes] = total + sides
                else:
                    write(c, tile, lanes, total + sides)

    def apply(self, u, uo, t_ref, px_ref, k_ref, ko, x1, xo, low, high, unroll, write):
        self.cross(u, low - 1 + uo, t_ref, 0)
        self.cross(u, high + uo, t_ref, high - low + 1)

        def one(p):
            def put(c, tile, lanes, d):
                write(c, p, tile, lanes, d)

            self.change(u, p + uo, t_ref, px_ref, p - low + 1, k_ref, p + ko, x1, p + xo, put)

        def mixed(p):
            at = p - low + 1
            for tile, kind in enumerate(self.kinds):
                lanes = self.lanes(tile)
                t = t_ref[at + 1, :, lanes] - t_ref[at - 1, :, lanes]
                write(0, p, tile, lanes, px_ref[at, :, lanes] + k_ref[12, p + ko, :, self.lanes(kind)] * t)

        each(low, high, unroll, one)
        each(low, high, 2 * unroll, mixed)


def each(low, high, unroll, body):
    count = high - low
    while count % unroll:
        unroll -= 1
    if count == unroll:
        for p in range(low, high):
            body(p)
        return

    def step(i, carry):
        for b in range(unroll):
            body(low + i * unroll + b)
        return carry

    lax.fori_loop(0, count // unroll, step, 0)


def tile_y(lane):
    return (lane & 127) - LEFT, PIECE + (lane & 31), (lane & 127) >> 5


def bf16(mask, value):
    return jnp.where(mask, value, 0.0).astype(jnp.bfloat16)


def rows_of(ref, group, x):
    return ref[pl.ds(group * 64 + x, 8, stride=8), :]


def edge_kernel(f_ref, left_ref, right_ref):
    for x in range(BX):
        for v in range(VEC):
            for c in range(COMP):
                val = rows_of(f_ref, v * COMP + c, x)
                lanes = pl.ds((x // 4) * 64 + 16 * v, 16)
                left_ref[c * 4 + x % 4, :, lanes] = val[:, :RIM]
                right_ref[c * 4 + x % 4, :, lanes] = val[:, BY - RIM :]
        val = rows_of(f_ref, VEC * COMP, x)
        left_ref[12, :, pl.ds(16 * x, 16)] = val[:, :RIM]
        right_ref[12, :, pl.ds(16 * x, 16)] = val[:, BY - RIM :]


def at_coeff(base, x):
    piece = 8 + x // 4
    return base + x // 5, 128 * (x % 5), base + piece // 5, 128 * (piece % 5) + 32 * (x % 4)


def place_kernel(f_ref, own_ref):
    def put(row, lane, piece_row, piece_lane, val):
        own_ref[row, :, pl.ds(lane + LEFT, 128 - LEFT)] = val[:, : 128 - LEFT]
        own_ref[piece_row, :, pl.ds(piece_lane, BY - PIECE)] = val[:, PIECE:]

    for x in range(BX):
        for c in range(COMP):
            for v in range(VEC):
                put(BX * c + x, 128 * v, BX * c + x, 512 + 32 * v, rows_of(f_ref, v * COMP + c, x))
        put(*at_coeff(COMP * BX, x), rows_of(f_ref, VEC * COMP, x))


def join_kernel(gy, placed_ref, l_ref, r_ref, own_ref, left_ref, right_ref):
    place = lax.axis_index("gy")
    from_left = (place > 0).astype(F32)
    from_right = (place < gy - 1).astype(F32)
    kept = BY - PIECE
    for i in range(COMP * BX + 2):
        own_ref[i] = placed_ref[i]

    def put(row, lane, piece_row, piece_lane, left, right):
        own_ref[row, :, pl.ds(lane, LEFT)] = left[:, RIM - LEFT :]
        own_ref[piece_row, :, pl.ds(piece_lane + kept, 32 - kept)] = right[:, : 32 - kept]

    for x in range(BX):
        for c in range(COMP):
            left = l_ref[c * 4 + x % 4] * from_left
            right = r_ref[c * 4 + x % 4] * from_right
            for v in range(VEC):
                at = (x // 4) * 64 + 16 * v
                put(BX * c + x, 128 * v, BX * c + x, 512 + 32 * v, left[:, at : at + RIM], right[:, at : at + RIM])
        left = l_ref[12, :, pl.ds(16 * x, 16)] * from_left
        right = r_ref[12, :, pl.ds(16 * x, 16)] * from_right
        put(*at_coeff(COMP * BX, x), left, right)
    for c in range(COMP):
        for x in range(FX):
            left_ref[c * FX + x] = own_ref[BX * c + x]
            right_ref[c * FX + x] = own_ref[BX * c + x + BX - FX]
    for i in range(2):
        left_ref[COMP * FX + i] = own_ref[COMP * BX + i]
        right_ref[COMP * FX + i] = own_ref[COMP * BX + i]


def down_kernel(
    gx, own_ref, l_ref, r_ref,
    pay_ref, send_l, send_r, x1_ref, x2_ref, c0_ref, y1, y2_ref, k1,
    x1, x2, k0, y2, cx, dr0, t0, p0, rest, stack, cstack, c1, dr1, f1, t1, p1, r1, stack1, pay, many, sems,
):
    place = lax.axis_index("gx")
    from_left = (place > 0).astype(F32)
    from_right = (place < gx - 1).astype(F32)
    a = Level(0, 1, 128, (0, 0, 0, 0, 1))

    def spread(plane, ref, base, x, factor):
        row, lane, piece_row, piece_lane = at_coeff(base, x)
        val = ref[row, :, pl.ds(lane, 128)]
        end = ref[piece_row, :, pl.ds(piece_lane, 32)]
        if factor is not None:
            val, end = val * factor, end * factor
        cx[plane + CX, :, pl.ds(0, 128)] = val
        for v in range(VEC):
            cx[plane + CX, :, pl.ds(128 + 32 * v, 32)] = end

    for x in range(BX):
        spread(x, own_ref, COMP * BX, x, None)
    for x in range(CX):
        spread(x - CX, l_ref, COMP * FX, x + BX - CX, from_left)
        spread(x + BX, r_ref, COMP * FX, x, from_right)

    def start(low, high, load):
        def body(p):
            gain, back = a.weights(cx, p + CX, k0, p + FX)
            for kind in range(2):
                dr0[p + FX, :, a.lanes(kind)] = back[kind]
            for c in range(COMP):
                plane = load(c, p)
                for tile, kind in enumerate(a.kinds):
                    x1[c, p + FX, :, a.lanes(tile)] = gain[kind] * plane[:, 128 * tile : 128 * tile + 128]

        each(low, high, 8, body)

    start(-FX, 0, lambda c, p: l_ref[c * FX + p + FX])
    start(0, BX, lambda c, p: own_ref[BX * c + p])
    start(BX, BX + FX, lambda c, p: r_ref[c * FX + p - BX])

    def to_x2(c, p, tile, lanes, d):
        x2[c, p + FX, :, lanes] = x1[c, p + FX, :, lanes] + d

    a.apply(x1, FX, t0, p0, k0, FX, x1, FX, 1 - FX, BX + FX - 1, UNROLL0, to_x2)

    def to_rest(c, p, tile, lanes, d):
        rest[c, p + 4, :, lanes] = d * dr0[p + FX, :, a.lanes(a.kinds[tile])]

    a.apply(x2, FX, t0, p0, k0, FX, x1, FX, -4, BX + 4, UNROLL0, to_rest)

    for c in range(COMP):
        for i in range(8):
            plane = rest[c, 2 * i] + rest[c, 2 * i + 1]
            stack[pl.ds(64 * c + 8 * i, 8), :] = plane + a.zp(plane)
    for i in range(10):
        plane = cx[2 * i + 1] + cx[2 * i + 2]
        cstack[pl.ds(8 * i, 8), :] = plane + a.zp(plane)
    selectors = []
    row, col = iota((K0, 128), 0), iota((K0, 128), 1)
    y, y_piece, vec = tile_y(row)
    for v in range(VEC):
        own_tile = (row < 128) & (y >= -10) & (y < SPLIT) & ((y >> 1) + 32 == col)
        piece = (row >= 128) & (vec == v) & (y_piece >= SPLIT) & (y_piece < BY + 10) & ((y_piece >> 1) + 32 == col)
        selectors.append(bf16(own_tile | piece, 0.125))
    parts = parts_of(stack[...])
    coarse = [
        exact_dot([jnp.concatenate([p[:, 128 * v : 128 * v + 128], p[:, 512:]], axis=1) for p in parts], selectors[v])
        for v in range(VEC)
    ]
    coarse_c = exact_dot(parts_of(cstack[...]), selectors[0])
    even = (iota((8, 128), 0) & 1) == 0
    for c in range(COMP):
        for i in range(8):
            at = 64 * c + 8 * i
            for low in range(2):
                odd = pltpu.roll(coarse[2 + low][at : at + 8], 1, 0)
                f1[c, i, :, pl.ds(128 * low, 128)] = jnp.where(even, coarse[low][at : at + 8], odd)
    for i in range(10):
        block = coarse_c[8 * i : 8 * i + 8]
        c1[i] = jnp.where(even, block, pltpu.roll(block, 1, 0))

    b = Level(1, 2, 128, (0, 0))
    for p in range(-2, 6):
        gain, back = b.weights(c1, p + 3, k1, p + 2)
        dr1[p + 2] = back[0]
        for c in range(COMP):
            for tile in range(2):
                y1[c, p + 2, :, b.lanes(tile)] = gain[0] * f1[c, p + 2, :, b.lanes(tile)]

    def to_y2(c, p, tile, lanes, d):
        y2[c, p + 1, :, lanes] = y1[c, p + 2, :, lanes] + d

    b.apply(y1, 2, t1, p1, k1, 2, y1, 2, -1, 5, UNROLL1, to_y2)
    for c in range(COMP):
        for i in range(3):
            send_l[3 * c + i] = y2[c, 1 + i]
            send_r[3 * c + i] = y2[c, 2 + i]

    def to_r1(c, p, tile, lanes, d):
        r1[c, p, :, lanes] = d * dr1[p + 2]

    b.apply(y2, 1, t1, p1, k1, 2, y1, 2, 0, 4, UNROLL1, to_r1)

    for c in range(COMP):
        for i in range(2):
            plane = r1[c, 2 * i] + r1[c, 2 * i + 1]
            plane = plane + pltpu.roll(plane, 6, 0)
            stack1[pl.ds(8 * (2 * c + i), 8), :] = plane[:, :128]
            stack1[pl.ds(64 + 8 * (2 * c + i), 8), :] = plane[:, 128:]
    for i in range(2):
        plane = c1[2 * i + 3] + c1[2 * i + 4]
        plane = plane + b.zp(plane)
        stack1[pl.ds(8 * (6 + i), 8), :] = plane
        stack1[pl.ds(64 + 8 * (6 + i), 8), :] = plane
    lane = iota((128, 128), 0) - 32
    selector1 = bf16((lane >> 1 == iota((128, 128), 1)) & (lane >= 0) & (lane < 64), 0.125)
    coarse1 = exact_dot(parts_of(stack1[...]), selector1)
    first = (iota((8, 32), 0) & 2) == 0
    blocks = []
    for g in range(8):
        low = coarse1[8 * g : 8 * g + 8]
        high = pltpu.roll(coarse1[64 + 8 * g : 72 + 8 * g], 2, 0)
        blocks.append(jnp.where(first, low[:, :32], high[:, :32]))
    for g in range(4):
        pay[pl.ds(0, 8), pl.ds(32 * g, 32)] = blocks[g]
    for g in range(2):
        pay[pl.ds(8, 4), pl.ds(32 * g, 32)] = blocks[4 + g][:4]
        pay[pl.ds(8, 4), pl.ds(64 + 32 * g, 32)] = blocks[4 + g][4:]
        pay[pl.ds(12, 1), pl.ds(64 * g, 32)] = blocks[6 + g][:1]
        pay[pl.ds(12, 1), pl.ds(64 * g + 32, 32)] = blocks[6 + g][4:5]
    batch = many.shape[0]
    for r in range(PAY):
        row = pay[pl.ds(r, 1), :]
        for i in range(batch):
            many[i, :, pl.ds(128 * r, 128)] = row
    copies = []
    for i in range(pay_ref.shape[0] // batch):
        copies.append(pltpu.make_async_copy(many, pay_ref.at[pl.ds(batch * i, batch)], sems.at[i]))
        copies[-1].start()
    for c in range(COMP):
        for i in range(10):
            x1_ref[c, i] = x1[c, i + 5]
        for i in range(12):
            x2_ref[c, i] = x2[c, i + 4]
        for i in range(4):
            y2_ref[c, i] = y2[c, i + 1]
    for i in range(12):
        c0_ref[i] = cx[i + 5]
    for copy in copies:
        copy.wait()


def up_kernel(
    gx, gy, got_ref, l_ref, r_ref, x1, x2, c0_ref, y1, y2, k1, out_ref,
    c2, f2, k2, dr2, x1c, ua, ub, rc, t2, p2, s2, c3, k3, x1d, va, vb, t3, p3, s3, sw, w0, w1, t1, p1, sp, k0, u0, u1, t0, p0, gs,
):
    nx2, nx3 = 2 * gx, gx
    yy2, l3 = 32 * gy, c3.shape[-1]
    place_x = lax.axis_index("gx")
    place_y = lax.axis_index("gy")
    from_left = (place_x > 0).astype(F32)
    from_right = (place_x < gx - 1).astype(F32)

    zero2 = jnp.zeros((8, yy2), F32)
    for ref in (ua, ub):
        for c in range(COMP):
            for i in (0, 1, nx2 + 2, nx2 + 3):
                ref[c, i] = zero2
    c2[0] = zero2
    c2[nx2 + 1] = zero2

    def unpack(i):
        for j in range(gy):
            at, lanes = i * gy + j, pl.ds(32 * j, 32)
            for r in range(PAY - 1):
                gs[at, pl.ds(r, 1), :] = got_ref[at, :, pl.ds(128 * r, 128)]
            for g in range(4):
                f2[g // 2, 2 * i + g % 2, :, lanes] = gs[at, pl.ds(0, 8), pl.ds(32 * g, 32)]
            for g in range(2):
                for half in range(2):
                    f2[2, 2 * i + g, pl.ds(4 * half, 4), lanes] = gs[at, pl.ds(8, 4), pl.ds(64 * half + 32 * g, 32)]
                    row = got_ref[at, :, pl.ds(128 * (PAY - 1) + 64 * g + 32 * half, 32)]
                    c2[2 * i + g + 1, pl.ds(4 * half, 4), lanes] = jnp.broadcast_to(row, (4, 32))

    each(0, gx, 8, unpack)
    m = Level(2, 4, yy2, (0,), yy2)

    def start2(p):
        gain, back = m.weights(c2, p + 1, k2, p)
        dr2[p] = back[0]
        for c in range(COMP):
            val = gain[0] * f2[c, p]
            x1c[c, p] = val
            ua[c, p + 2] = val

    each(0, nx2, 16, start2)

    def sweep2(src, dst):
        def write(c, p, tile, lanes, d):
            dst[c, p + 2] = src[c, p + 2] + d

        m.apply(src, 2, t2, p2, k2, 0, x1c, 0, 0, nx2, UNROLL2, write)

    sweep2(ua, ub)

    def to_rc(c, p, tile, lanes, d):
        rc[c, p] = d * dr2[p]

    m.apply(ub, 2, t2, p2, k2, 0, x1c, 0, 0, nx2, UNROLL2, to_rc)

    for i in range(nx3):
        for c in range(COMP):
            plane = rc[c, 2 * i] + rc[c, 2 * i + 1]
            s2[pl.ds(8 * (c * nx3 + i), 8), :] = plane + pltpu.roll(plane, 4, 0)
        plane = c2[2 * i + 1] + c2[2 * i + 2]
        s2[pl.ds(8 * (COMP * nx3 + i), 8), :] = plane + pltpu.roll(plane, 4, 0)
    selector = bf16((iota((yy2, l3), 0) >> 1) == iota((yy2, l3), 1), 0.125)
    coarse = exact_dot(parts_of(s2[...]), selector)
    zero3 = jnp.zeros((8, l3), F32)
    for ref in (va, vb):
        for c in range(COMP):
            ref[c, 0] = zero3
            ref[c, nx3 + 1] = zero3
    c3[0] = zero3
    c3[nx3 + 1] = zero3
    for i in range(nx3):
        c3[i + 1] = coarse[8 * (COMP * nx3 + i) : 8 * (COMP * nx3 + i) + 8]
    n = Level(3, 8, l3, (0,), 16 * gy)
    a = Level(0, 1, 128, (0, 0, 0, 0, 1))
    for p in range(nx3):
        gain, _ = n.weights(c3, p + 1, k3, p)
        for c in range(COMP):
            val = gain[0] * coarse[8 * (c * nx3 + p) : 8 * (c * nx3 + p) + 8]
            x1d[c, p] = val
            va[c, p + 1] = val
    src, dst = va, vb
    for sweep in range(COARSE - 1):

        def write3(c, p, tile, lanes, d, src=src, dst=dst):
            dst[c, p + 1] = src[c, p + 1] + d

        n.apply(src, 1, t3, p3, k3, 0, x1d, 0, 0, nx3, UNROLL2, write3)
        for p in (2 * sweep - 1, 2 * sweep):
            a.weights(c0_ref, p + 2, k0, p + 1)
        src, dst = dst, src
    for c in range(COMP):
        for i in range(nx3):
            s3[pl.ds(8 * (c * nx3 + i), 8), :] = src[c, i + 1]
    selector = bf16((iota((l3, yy2), 1) >> 1) == iota((l3, yy2), 0), 1.0)
    fine = exact_dot(parts_of(s3[...]), selector)
    for c in range(COMP):
        for i in range(nx3):
            block = fine[8 * (c * nx3 + i) : 8 * (c * nx3 + i) + 8]
            for j in range(2):
                ub[c, 2 * i + j + 2] = ub[c, 2 * i + j + 2] + block
    sweep2(ub, ua)
    sweep2(ua, ub)

    row = iota((8, yy2), 0)
    for c in range(COMP):
        for i in range(6):
            e = ub[c, 2 * place_x + i]
            at = 16 * (6 * c + i)
            sw[pl.ds(at, 8), :] = jnp.where((row & 2) == 0, e, pltpu.roll(e, 2, 0))
            sw[pl.ds(at + 8, 8), :] = jnp.where((row & 2) != 0, e, pltpu.roll(e, 6, 0))
    y1g = place_y * 64 + iota((yy2, 128), 1) - 32
    fine = exact_dot(parts_of(sw[...]), bf16((y1g >> 1) == iota((yy2, 128), 0), 1.0))
    for c in range(COMP):
        for p in range(-3, 7):
            if p < 0:
                val = l_ref[3 * c + p + 3] * from_left
            elif p < 4:
                val = y2[c, p]
            else:
                val = r_ref[3 * c + p - 4] * from_right
            at = 16 * (6 * c + (p + 4) // 2)
            w0[c, p + 3] = val + jnp.concatenate([fine[at : at + 8], fine[at + 8 : at + 16]], axis=1)
    b = Level(1, 2, 128, (0, 0))

    def write1(c, p, tile, lanes, d):
        w1[c, p + 3, :, lanes] = w0[c, p + 3, :, lanes] + d

    b.apply(w0, 3, t1, p1, k1, 2, y1, 2, -2, 6, UNROLL1, write1)
    odd = (iota((8, 128), 0) & 1) != 0

    def write1b(c, p, tile, lanes, d):
        e = w1[c, p + 3, :, lanes] + d
        rows = pl.ds(8 * (6 * c + p + 1), 8)
        sp[tile, rows, :] = jnp.where(odd, pltpu.roll(e, 1, 0), e)
        sp[2 + tile, rows, :] = jnp.where(odd, e, pltpu.roll(e, 7, 0))

    b.apply(w1, 3, t1, p1, k1, 2, y1, 2, -1, 5, 6, write1b)

    col = iota((128, K0), 1)
    y, y_piece, vec = tile_y(col)
    piece = None
    for v in range(VEC):
        parent = jnp.where(col < 128, y >> 1, y_piece >> 1) + 32
        selector = bf16((parent == iota((128, K0), 0)) & ((col < 128) | (vec == v)), 1.0)
        fine = exact_dot(parts_of(sp[v]), selector)
        piece = fine[:, 128:] if v == 0 else piece + fine[:, 128:]
        for c in range(COMP):
            for i in range(6):
                at = 8 * (6 * c + i)
                for j in range(2):
                    u0[c, 2 * i + j, :, pl.ds(128 * v, 128)] = x2[c, 2 * i + j, :, pl.ds(128 * v, 128)] + fine[at : at + 8, :128]
    for c in range(COMP):
        for i in range(6):
            at = 8 * (6 * c + i)
            for j in range(2):
                u0[c, 2 * i + j, :, pl.ds(512, 128)] = x2[c, 2 * i + j, :, pl.ds(512, 128)] + piece[at : at + 8]

    def write0(c, p, tile, lanes, d):
        u1[c, p + 2, :, lanes] = u0[c, p + 2, :, lanes] + d

    a.apply(u0, 2, t0, p0, k0, 1, x1, 1, -1, 9, UNROLL0, write0)

    def write_last(c, p, tile, lanes, d):
        u0[c, p + 2, :, lanes] = u1[c, p + 2, :, lanes] + d

    a.apply(u1, 2, t0, p0, k0, 1, x1, 1, 0, BX, UNROLL0, write_last)
    near = iota((8, 128), 1) < SPLIT
    for x in range(BX):
        for c in range(COMP):
            last = u0[c, x + 2, :, pl.ds(512, 128)]
            for v in range(VEC):
                main = pltpu.roll(u0[c, x + 2, :, pl.ds(128 * v, 128)], 128 - LEFT, 1)
                ends = pltpu.roll(last, (PIECE - 32 * v) % 128, 1)
                out_ref[pl.ds((v * COMP + c) * 64 + x, 8, stride=8), :] = jnp.where(near, main, ends)


def call(kernel, outs, scratch, *args, far=False):
    vmem = pl.BlockSpec(memory_space=pltpu.VMEM)
    shapes = [jax.ShapeDtypeStruct(s, F32) for s in outs]
    return pl.pallas_call(
        kernel,
        out_shape=shapes,
        in_specs=[vmem] * len(args),
        out_specs=[pl.BlockSpec(memory_space=pltpu.HBM) if far and i == 0 else vmem for i in range(len(outs))],
        scratch_shapes=[pltpu.VMEM(s, F32) if isinstance(s, tuple) else s for s in scratch],
        compiler_params=pltpu.CompilerParams(vmem_limit_bytes=48 * 1024 * 1024),
    )(*args)


def per_device(gx, gy, right_side, material):
    def ring(value, axis, size, step):
        return lax.ppermute(value, axis, [(i, (i + step) % size) for i in range(size)])

    f = right_side.reshape(VEC * COMP * NZ * BX, BY)
    rows = f.shape[0]
    m = jnp.pad(material.reshape(NZ * BX, BY), ((rows, 0), (0, 0)))
    coeff = jnp.where(m == 1, 1.0, 0.05).astype(F32)
    f = jnp.where(iota((rows + NZ * BX, BY), 0) < rows, jnp.pad(f, ((0, NZ * BX), (0, 0))), coeff)
    edge = (13, 8, 128)
    to_left, to_right = call(edge_kernel, [edge, edge], [], f)
    right = ring(to_left, "gy", gy, -1)
    left = ring(to_right, "gy", gy, 1)
    side = (COMP * FX + 2, 8, L0)
    whole = (COMP * BX + 2, 8, L0)
    (own,) = call(place_kernel, [whole], [], f)
    own, to_left, to_right = call(functools.partial(join_kernel, gy), [whole, side, side], [], own, left, right)
    right = ring(to_left, "gx", gx, -1)
    left = ring(to_right, "gx", gx, 1)
    n = gx * gy
    plane = lambda *lead: (*lead, 8, L0)
    plane1 = lambda *lead: (*lead, 8, L1)
    nf, nc = BX + 2 * FX, BX + 2 * CX
    pay, to_left, to_right, *kept = call(
        functools.partial(down_kernel, gx),
        [
            (n, 1, 128 * PAY), plane1(9), plane1(9), plane(3, 10), plane(3, 12), (12, 8, K0), plane1(3, 8), plane1(3, 4), (13, 8, 8, 128),
        ],
        [
            plane(3, nf), plane(3, nf), (13, nf, 8, K0), plane1(3, 6),
            (nc, 8, K0), (nf, 8, K0), plane(nf), plane(nf), plane(3, 16), (192, L0), (80, K0), (10, 8, 128),
            (8, 8, 128), plane1(3, 8), plane1(10), plane1(10), plane1(3, 4), (128, 128), (16, 128), (8, 1, 128 * PAY), pltpu.SemaphoreType.DMA((n // 8,)),
        ],
        own, left, right, far=True,
    )
    right = ring(to_left, "gx", gx, -1)
    left = ring(to_right, "gx", gx, 1)
    got = lax.all_to_all(pay, ("gx", "gy"), 0, 0)
    nx2, nx3, y2, l3 = 2 * gx, gx, 32 * gy, max(128, 16 * gy)
    plane2 = lambda *lead: (*lead, 8, y2)
    plane3 = lambda *lead: (*lead, 8, l3)
    (out,) = call(
        functools.partial(up_kernel, gx, gy),
        [(VEC * COMP * NZ * BX, BY)],
        [
            plane2(nx2 + 2), plane2(3, nx2), plane2(13, nx2), plane2(nx2), plane2(3, nx2), plane2(3, nx2 + 4), plane2(3, nx2 + 4),
            plane2(3, nx2), plane2(nx2 + 2), plane2(nx2 + 2), (32 * nx3, y2),
            plane3(nx3 + 2), plane3(13, nx3), plane3(3, nx3), plane3(3, nx3 + 2), plane3(3, nx3 + 2), plane3(nx3 + 2), plane3(nx3 + 2),
            (24 * nx3, l3), (288, y2), plane1(3, 10), plane1(3, 10), plane1(10), plane1(10), (4, 144, 128), (13, 10, 8, K0),
            plane(3, 12), plane(3, 12), plane(12), plane(12), (n, 16, 128),
        ],
        got, left, right, *kept,
    )
    return out.reshape(right_side.shape)


def solution(mesh):
    gx, gy = mesh.shape["gx"], mesh.shape["gy"]
    spec = P(None, None, None, "gx", "gy")
    return jax.shard_map(
        functools.partial(per_device, gx, gy), mesh=mesh, in_specs=(spec, P(None, "gx", "gy")), out_specs=spec, check_vma=False
    )
```
